128 devices in a mesh: lap: 4 (over x), space: 32 (over y, z, core).
Axes of the slice: x: 4, y: 4, z: 4, core: 2. Of those that a mesh axis runs over, the one named last changes fastest.
Arguments:
- slowness: float32 [64, 512, 128], P('space'), may hold values from 0.25 to 1
- damping: float32 [16], P('lap'), may hold values from 0.2 to 1.5
- src_index: int32 [32768], P('space'), may hold values from 0 to 4194303, as said below
- src_amp: float32 [16, 32768], P('lap', 'space'), may hold values from -12 to 12
- rec_index: int32 [32768], P('space'), may hold values from 0 to 4194303, as said below
- observed: float32 [16, 32768], P('lap', 'space'), may hold values from -0.6 to 0.6
- dual: float32 [3, 64, 512, 128], P(None, 'space', 'lap'), may hold values from -2 to 2
Outputs:
- model: float32 [64, 512, 128], P('space', 'lap')
- dual_next: float32 [3, 64, 512, 128], P(None, 'space', 'lap')
The draws below stay inside these ranges and needn't reach their ends.
Inputs may be any that keep to these rules, and one draw needn't show every extreme that they name: `src_index`: entry k lies in the slab of grid cells whose first index is from (k // 1024) * 2 to (k // 1024) * 2 + 1; cells may repeat. `rec_index`: entry k lies in the slab of grid cells whose first index is from (k // 1024) * 2 to (k // 1024) * 2 + 1; cells may repeat.
All inputs are finite; a program needn't handle non-finite values.
Results may differ from the reference program's by a relative error of at most 0.0001.
Values sent between devices are 32-bit elements; how exact they have to be, the bound alone decides.
No kernel may reach another device: no remote copies, remote signals or barrier semaphores. Data moves between devices by JAX's collectives and lax.ppermute only.
A program may use at most 192 MiB of HBM per device.

```python
import math
import jax
import jax.numpy as jnp
from jax import lax

CX = 2
NY = 512
NZ = 128
ITERS = 3
SRC_DEV = 1024
REC_DEV = 1024
NX = 64
CONSTS = 16
NSRC = 32768
NREC = 32768


source_run = 8


receiver_run = 4


def run_indices(key, total, per_device, run):
    slab_cells = CX * NY * NZ
    count = total // run
    runs_each = per_device // run
    key_x, key_y, key_z = jax.random.split(key, 3)
    first_x = jax.random.randint(key_x, (count,), 0, CX, dtype=jnp.int32)
    first_y = jax.random.randint(key_y, (count,), 0, NY, dtype=jnp.int32)
    first_z = jax.random.randint(key_z, (count,), 0, NZ - run + 1, dtype=jnp.int32)
    first_x = first_x.at[0].set(0).at[count - 1].set(CX - 1)
    first_y = first_y.at[0].set(0).at[count - 1].set(NY - 1)
    first_z = first_z.at[0].set(0).at[count - 1].set(NZ - run)
    blocks = jnp.arange(count, dtype=jnp.int32) // runs_each
    starts = blocks * slab_cells + (first_x * NY + first_y) * NZ + first_z
    spots = starts[:, None] + jnp.arange(run, dtype=jnp.int32)[None, :]
    return spots.reshape(-1).astype(jnp.int32)


def draw_src_index(key, part):
    key = jax.random.fold_in(key, 11)
    return run_indices(key, NSRC, SRC_DEV, source_run)


def draw_rec_index(key, part):
    key = jax.random.fold_in(key, 12)
    return run_indices(key, NREC, REC_DEV, receiver_run)


def draw_src_amp(key, part):
    key = jax.random.fold_in(key, 13)
    count = NSRC // source_run
    blocks = (jnp.arange(count, dtype=jnp.int32) // (SRC_DEV // source_run)).astype(jnp.float32)
    number = NSRC // SRC_DEV
    rising = jnp.exp(jnp.log(3.0) * blocks / max(number - 1, 1))
    values = jnp.clip(jax.random.normal(key, (CONSTS, count), jnp.float32), -4.0, 4.0)
    values = values * rising[None, :]
    return jnp.repeat(values, source_run, axis=1).astype(jnp.float32)


def draw_observed(key, part):
    key = jax.random.fold_in(key, 14)
    key_common, key_own = jax.random.split(key)
    count = NREC // receiver_run
    common = jax.random.normal(key_common, (CONSTS, count), jnp.float32)
    own = jax.random.normal(key_own, (CONSTS, NREC), jnp.float32)
    values = 0.1 * (0.8 * jnp.repeat(common, receiver_run, axis=1) + 0.6 * own)
    return jnp.clip(values, -0.6, 0.6).astype(jnp.float32)


def levels(own_key, dims, cuts, smallest, largest):
    def one(axis_at, blocks):
        heights = jax.random.uniform(jax.random.fold_in(jax.random.fold_in(own_key, 6), axis_at), (blocks,), jnp.float32, smallest / len(cuts), largest / len(cuts))
        return jnp.repeat(jnp.exp(heights), dims[axis_at] // blocks).reshape((-1,) + (1,) * (len(dims) - axis_at - 1))

    level = one(*cuts[0])
    for cut in cuts[1:]:
        level = level * one(*cut)
    return level


def centred(stream_key, extent, width, most, pieces=(), held_as=jnp.bfloat16):
    gain = levels(stream_key, extent, pieces, -0.22, 0.18) if pieces else 1.0
    array = jax.random.normal(stream_key, extent, jnp.float32) * width * gain
    return jnp.minimum(jnp.maximum(array, -most), most).astype(held_as)


def setup_inputs(seed: int = 0) -> dict:
    splits = jax.random.split(jax.random.key(seed), 8)
    slowness = jnp.clip(0.25 + 0.75 * jax.random.uniform(splits[0], (NX, NY, NZ), jnp.float32) ** levels(splits[0], (NX, NY, NZ), ((0, 32),), -0.2, 0.2), 0.25, 1.0)
    damping = jnp.clip(jnp.exp(math.log(1.5) - 2.014903 * jax.random.uniform(splits[1], (CONSTS,), jnp.float32) ** levels(splits[1], (CONSTS,), ((0, 4),), -0.2, 0.2)), 0.2, 1.5)
    src_index = draw_src_index(jax.random.fold_in(splits[7], 71), 0)
    src_amp = draw_src_amp(jax.random.fold_in(splits[7], 71), 0)
    rec_index = draw_rec_index(jax.random.fold_in(splits[7], 71), 0)
    observed = draw_observed(jax.random.fold_in(splits[7], 71), 0)
    dual = centred(splits[6], (3, NX, NY, NZ), 0.3, 2.0, ((1, 32), (2, 4)), jnp.float32)
    return dict(slowness=slowness, damping=damping, src_index=src_index, src_amp=src_amp, rec_index=rec_index, observed=observed, dual=dual)


dual_step = 0.5
primal_step = 0.2
tv_weight = 0.5

def operate(field, diagonal):
    padded = jnp.pad(field, 1)
    beside = padded[2:, 1:-1, 1:-1] + padded[:-2, 1:-1, 1:-1]
    beside = beside + padded[1:-1, 2:, 1:-1] + padded[1:-1, :-2, 1:-1]
    beside = beside + padded[1:-1, 1:-1, 2:] + padded[1:-1, 1:-1, :-2]
    return diagonal * field - beside

def precond_solve(right_side, diagonal):
    iterate = jnp.zeros_like(right_side)
    residual = right_side
    precon = residual / diagonal
    direction = precon
    energy = jnp.sum(residual * precon)
    for iteration in range(ITERS):
        applied = operate(direction, diagonal)
        stride = energy / jnp.sum(direction * applied)
        iterate = iterate + stride * direction
        if iteration + 1 < ITERS:
            residual = residual - stride * applied
            precon = residual / diagonal
            energy_new = jnp.sum(residual * precon)
            direction = precon + energy_new / energy * direction
            energy = energy_new
    return iterate

def reference(slowness, damping, src_index, src_amp, rec_index, observed, dual):
    cells = NX * NY * NZ

    def accumulate(total, inputs):
        damping_value, amplitude, measured = inputs
        squared = damping_value * damping_value
        diagonal = 6.0 + squared * slowness
        source = jnp.zeros((cells,), slowness.dtype).at[src_index].add(amplitude).reshape(slowness.shape)
        wavefield = precond_solve(source, diagonal)
        misfit = wavefield.reshape(-1)[rec_index] - measured
        adjoint_source = jnp.zeros((cells,), slowness.dtype).at[rec_index].add(misfit).reshape(slowness.shape)
        adjoint = precond_solve(adjoint_source, diagonal)
        return (total - squared * wavefield * adjoint, None)
    gradient, leftover = lax.scan(accumulate, jnp.zeros_like(slowness), (damping, src_amp, observed))
    scaled = gradient / jnp.sqrt(jnp.mean(gradient * gradient) + 1e-06)
    step_x = jnp.concatenate([slowness[1:] - slowness[:-1], jnp.zeros_like(slowness[:1])], 0)
    step_y = jnp.concatenate([slowness[:, 1:] - slowness[:, :-1], jnp.zeros_like(slowness[:, :1])], 1)
    step_z = jnp.concatenate([slowness[:, :, 1:] - slowness[:, :, :-1], jnp.zeros_like(slowness[:, :, :1])], 2)
    dual_trial = dual + dual_step * jnp.stack([step_x, step_y, step_z])
    magnitude = jnp.sqrt(lax.optimization_barrier(jnp.sum(dual_trial * dual_trial, axis=0)))
    dual_next = dual_trial / jnp.maximum(1.0, magnitude / tv_weight)
    comp_x = dual_next[0].at[-1].set(0.0)
    comp_y = dual_next[1].at[:, -1].set(0.0)
    comp_z = dual_next[2].at[:, :, -1].set(0.0)
    back_x = jnp.concatenate([jnp.zeros_like(comp_x[:1]), comp_x[:-1]], 0) - comp_x
    back_y = jnp.concatenate([jnp.zeros_like(comp_y[:, :1]), comp_y[:, :-1]], 1) - comp_y
    back_z = jnp.concatenate([jnp.zeros_like(comp_z[:, :, :1]), comp_z[:, :, :-1]], 2) - comp_z
    model = slowness - primal_step * (scaled + back_x + back_y + back_z)
    return (model, dual_next)
```

```python
import functools

import jax
import jax.numpy as jnp
from jax import lax
from jax.experimental import pallas as pl
from jax.experimental.pallas import tpu as pltpu
from jax.sharding import Mesh
from jax.sharding import PartitionSpec as P


HALF = 2
PLANES = 13
KEPT = 9
PAD = 8
CHUNK = 256

dual_step = 0.5
primal_step = 0.2
tv_weight = 0.5

VMEM = pl.BlockSpec(memory_space=pltpu.VMEM)
SMEM = pl.BlockSpec(memory_space=pltpu.SMEM)


def params(mib):
    return pltpu.CompilerParams(vmem_limit_bytes=mib * 2**20)


def spread_points(index, values, pieces, first, store, planes):
    points = index.shape[1]
    column = (index >> 16) * 128 + (index & 127)
    row = (index >> 7) & 511
    lanes = lax.broadcasted_iota(jnp.int32, (planes * 128, points), 0)
    right = jnp.where(lanes == column, 1.0, 0.0).astype(jnp.bfloat16)
    sub = lax.broadcasted_iota(jnp.int32, (8, points), 0)
    row = row - sub // HALF
    parts = []
    for value, count in zip(values, pieces):
        high = value.astype(jnp.bfloat16).astype(jnp.float32)
        parts.append([high, value - high][:count])
    rows = 512 * HALF
    step = 8 // HALF

    def body(k, _):
        tile = lax.broadcasted_iota(jnp.int32, (CHUNK // 8, 8, points), 0)
        mask = row[None] - step * tile == k * (CHUNK // HALF)
        for which, part in enumerate(parts):
            total = None
            for piece in part:
                left = jnp.where(mask, piece[None], 0.0).reshape(CHUNK, points).astype(jnp.bfloat16)
                got = lax.dot_general(
                    left, right, (((1,), (1,)), ((), ())), preferred_element_type=jnp.float32
                )
                total = got if total is None else total + got
            at = pl.ds(pl.multiple_of(k * CHUNK, CHUNK), CHUNK)
            for p in range(planes):
                store[which][first[which] + p, at, :] = total[:, p * 128 : (p + 1) * 128]
        return 0

    lax.fori_loop(0, rows // CHUNK, body, 0)


def scatter_kernel(core_ref, mine_ref, theirs_ref, b_ref, ob_ref, cn_ref):
    core = core_ref[0]
    points = mine_ref.shape[2]
    parity = lax.broadcasted_iota(jnp.int32, (8, points), 0) % HALF
    for slab in range(7):
        q, h = slab // 2, slab % 2
        rows = jnp.where(core == h, mine_ref[q], theirs_ref[q])
        src = rows[0:1].astype(jnp.int32)
        rec = rows[1:2].astype(jnp.int32)
        amp = jnp.where(parity == 0, rows[2:3], rows[3:4])
        obs = jnp.where(parity == 0, rows[4:5], rows[5:6])
        planes = 1 if slab == 6 else 2
        spread_points(src, [amp], [1 if slab in (0, 5, 6) else 2], [2 * slab], [b_ref], planes)
        if 1 <= slab <= 5:
            near = 1 if slab == 5 else 2
            at = 2 * slab - 2
            spread_points(
                rec, [obs, jnp.ones_like(obs)], [near, 1], [at, at], [ob_ref, cn_ref], near
            )


def neighbours(ref, t, r0):
    x = ref[t, pl.ds(PAD + r0, CHUNK), :]
    prev = ref[t, pl.ds(r0, 8), :]
    after = ref[t, pl.ds(PAD + r0 + CHUNK, 8), :]
    ext = jnp.concatenate([prev, x, after], 0)
    rows = CHUNK + 16
    down = pltpu.roll(ext, HALF, 0)[8 : 8 + CHUNK]
    up = pltpu.roll(ext, rows - HALF, 0)[8 : 8 + CHUNK]
    lane = lax.broadcasted_iota(jnp.int32, (CHUNK, 128), 1)
    low = jnp.where(lane == 0, 0.0, pltpu.roll(x, 1, 1))
    high = jnp.where(lane == 127, 0.0, pltpu.roll(x, 127, 1))
    return x, (down + up) + (low + high)


def fold(x):
    return jnp.sum(x.reshape(CHUNK // 8, 8, 128), 0)


def walk(first, last, body, carry):
    steps = 512 * HALF // CHUNK

    def step(i, c):
        t = first + i // steps
        return body(t, pl.multiple_of((i % steps) * CHUNK, CHUNK), c)

    return lax.fori_loop(0, (last - first) * steps, step, carry)


def advance(src, s_off, inv, i_off, dst, d_off, first, last, dots):
    def body(t, r0, carry):
        at = pl.ds(PAD + r0, CHUNK)
        x, q = neighbours(src, t - s_off, r0)
        q = q + (src[t - s_off - 1, at, :] + src[t - s_off + 1, at, :])
        new = inv[t - i_off, pl.ds(r0, CHUNK), :] * q
        dst[t - d_off, at, :] = new
        if not dots:
            return carry
        return carry[0] + fold(x * q), carry[1] + fold(new * q)

    zero = jnp.zeros((8, 128), jnp.float32)
    return walk(first, last, body, (zero, zero) if dots else 0)


def last_moment(src, off):
    def body(t, r0, carry):
        x, q = neighbours(src, t - off, r0)
        q = q + 2.0 * src[t - off + 1, pl.ds(PAD + r0, CHUNK), :]
        return carry + fold(x * q)

    return walk(4, 8, body, jnp.zeros((8, 128), jnp.float32))


def clear_pads(*refs):
    for ref in refs:
        zero = jnp.zeros((8, 128), jnp.float32)
        for t in range(ref.shape[0]):
            ref[t, 0:PAD, :] = zero
            ref[t, ref.shape[1] - PAD :, :] = zero


def message(moments):
    sub = lax.broadcasted_iota(jnp.int32, (8, 128), 0)
    lane = lax.broadcasted_iota(jnp.int32, (8, 128), 1)
    out = jnp.zeros((8, 128), jnp.float32)
    for k, moment in enumerate(moments):
        for c in range(HALF):
            total = jnp.sum(jnp.where(sub % HALF == c, moment, 0.0))
            out = out + jnp.where((sub == k) & (lane == c), total, 0.0)
    return out


def coefficients(moments):
    m = [moments[k : k + 1, :] for k in range(6)]

    def product(p, shift):
        total = 0.0
        for i, a in enumerate(p):
            for j, b in enumerate(p):
                total = total + a * b * (m[i + j] - m[i + j + 1] if shift else m[i + j])
        return total

    one = jnp.ones_like(m[0])
    z, p, energy = [one], [one], m[0]
    x = [0.0 * one] * 3
    for it in range(3):
        stride = energy / product(p, True)
        x = [x[i] + (stride * p[i] if i < len(p) else 0.0) for i in range(3)]
        if it < 2:
            applied = [a - b for a, b in zip(p + [0.0 * one], [0.0 * one] + p)]
            z = [a - stride * b for a, b in zip(z + [0.0 * one], applied)]
            new = product(z, False)
            p = [a + new / energy * b for a, b in zip(z, p + [0.0 * one])]
            energy = new
    lane = lax.broadcasted_iota(jnp.int32, (1, 128), 1)
    sub = lax.broadcasted_iota(jnp.int32, (8, 128), 0)
    out = []
    for v in x:
        value = [jnp.sum(jnp.where(lane == c, v, 0.0)) for c in range(HALF)]
        out.append(jnp.where(sub % HALF == 0, value[0], value[1]))
    return out


def times(pattern, x):
    return (pattern[None] * x.reshape(CHUNK // 8, 8, 128)).reshape(CHUNK, 128)


def forward_kernel(par, own_m, own_t, near_m, near_t, b, inv, v0, v1, v2, msg):
    core = par[5]
    slabs = (
        (near_m, near_t, 0, 0, 2), (near_m, near_t, 0, 1, 2),
        (own_m, own_t, 0, 0, None), (own_m, own_t, 0, 1, None),
        (near_m, near_t, 2, 0, 3), (near_m, near_t, 2, 1, 3), (near_m, near_t, 4, 0, 4),
    )
    clear_pads(v0, v1, v2)
    for slab, (mine, theirs, base, h, flag) in enumerate(slabs):
        valid = 1.0 if flag is None else par[flag]
        planes = 1 if slab == 6 else 2

        def fill(p, _, mine=mine, theirs=theirs, base=base, h=h, valid=valid, slab=slab):
            sigma = jnp.where(core == float(h), mine[base + p], theirs[base + p])
            for c in range(HALF):
                inv[2 * slab + p, pl.ds(c, 512, stride=HALF), :] = valid / (6.0 + par[c] * sigma)
            return 0

        lax.fori_loop(0, planes, fill, 0)

    def start(dots):
        def body(t, r0, carry):
            right = b[t, pl.ds(r0, CHUNK), :]
            new = inv[t, pl.ds(r0, CHUNK), :] * right
            v0[t, pl.ds(PAD + r0, CHUNK), :] = new
            return carry + fold(new * right) if dots else carry

        return body

    zero = jnp.zeros((8, 128), jnp.float32)
    walk(0, 4, start(False), 0)
    m0 = walk(4, 8, start(True), zero)
    walk(8, 13, start(False), 0)
    advance(v0, 0, inv, 0, v1, 1, 1, 4, False)
    m1, m2 = advance(v0, 0, inv, 0, v1, 1, 4, 8, True)
    advance(v0, 0, inv, 0, v1, 1, 8, 12, False)
    advance(v1, 1, inv, 0, v2, 2, 2, 4, False)
    m3, m4 = advance(v1, 1, inv, 0, v2, 2, 4, 8, True)
    advance(v1, 1, inv, 0, v2, 2, 8, 11, False)
    m5 = last_moment(v2, 2)
    msg[...] = message([m0, m1, m2, m3, m4, m5])


def adjoint_kernel(total, inv, v0, v1, v2, ob, cn, wave, u0, u1, u2, msg):
    a = coefficients(total[...])
    clear_pads(u0, u1, u2)

    def start(own):
        def body(t, r0, carry):
            at = pl.ds(PAD + r0, CHUNK)
            here = pl.ds(r0, CHUNK)
            w = times(a[0], v0[t, at, :]) + times(a[1], v1[t - 1, at, :])
            w = w + times(a[2], v2[t - 2, at, :])
            right = cn[t - 2, here, :] * w - ob[t - 2, here, :]
            new = inv[t, here, :] * right
            u0[t - 2, at, :] = new
            if not own:
                return carry
            wave[t - 4, here, :] = w
            return carry + fold(new * right)

        return body

    zero = jnp.zeros((8, 128), jnp.float32)
    walk(2, 4, start(False), 0)
    m0 = walk(4, 8, start(True), zero)
    walk(8, 11, start(False), 0)
    advance(u0, 2, inv, 0, u1, 3, 3, 4, False)
    m1, m2 = advance(u0, 2, inv, 0, u1, 3, 4, 8, True)
    advance(u0, 2, inv, 0, u1, 3, 8, 10, False)
    m3, m4 = advance(u1, 3, inv, 0, u2, 4, 4, 8, True)
    advance(u1, 3, inv, 0, u2, 4, 8, 9, False)
    m5 = last_moment(u2, 4)
    msg[...] = message([m0, m1, m2, m3, m4, m5])


def gradient_kernel(par, total, wave, u0, u1, u2, out, held):
    a = coefficients(total[...])
    sub = lax.broadcasted_iota(jnp.int32, (8, 128), 0)
    square = jnp.where(sub % HALF == 0, par[0], par[1])
    a = [-square * v for v in a]

    def body(t, r0, carry):
        at = pl.ds(PAD + r0, CHUNK)
        x = times(a[0], u0[t - 2, at, :]) + times(a[1], u1[t - 3, at, :])
        x = x + times(a[2], u2[t - 4, at, :])
        held[pl.ds((t - 4) * 1024 + r0, CHUNK), :] = x * wave[t - 4, pl.ds(r0, CHUNK), :]
        return carry

    walk(4, 8, body, 0)
    for t in range(4):
        for band in range(4):
            at = t * 1024 + band * 256
            both = held[pl.ds(at, 128, stride=HALF), :] + held[pl.ds(at + 1, 128, stride=HALF), :]
            out[band * 2 + t // 2, t % 2] = both


def power_kernel(parts, own, msg):
    g = parts[0]
    for k in range(1, 8):
        g = g + parts[k]
    own[...] = g
    msg[...] = jnp.full((128, 128), jnp.sum(g * g), jnp.float32)


def struct(*shape):
    return jax.ShapeDtypeStruct(shape, jnp.float32)


def moved(x, axis, by):
    peers = lax.axis_size(axis)
    return lax.ppermute(x, axis, [(i, i + by) for i in range(peers) if 0 <= i + by < peers])


def swapped(x):
    return lax.ppermute(x, "core", [(0, 1), (1, 0)])


def pair_sum(x):
    for masks in ((1, 2, 3), (4, 8, 12)):
        x = x + sum(lax.ppermute(x, "pair", [(i, i ^ d) for i in range(16)]) for d in masks)
    return x


def on_device(slowness, damping, src_index, src_amp, rec_index, observed, dual):
    width_x, rows_y, depth_z = slowness.shape
    slab_cells = width_x * rows_y * depth_z
    lap, pair, core = (lax.axis_index(name) for name in ("lap", "pair", "core"))
    pairs = lax.axis_size("pair")
    offset = (pair * 2 + core) * slab_cells

    squared = damping * damping
    own_sq = lax.dynamic_slice_in_dim(squared, core * HALF, HALF)
    flags = jnp.stack([pair >= 1, pair + 1 < pairs, pair + 2 < pairs, core == 1])
    par = jnp.concatenate([own_sq, flags.astype(jnp.float32), jnp.zeros(2, jnp.float32)])
    core_in = core.astype(jnp.int32).reshape(1)

    index = jnp.stack([src_index - offset, rec_index - offset]).astype(jnp.float32)
    blank = jnp.zeros_like(index)
    lists = jnp.stack(
        [jnp.concatenate([index, src_amp[2 * k : 2 * k + 2], observed[2 * k : 2 * k + 2], blank])
         for k in range(2)]
    )
    around = [moved(lists, "pair", 1), lists, moved(lists, "pair", -1), moved(lists, "pair", -2)]
    stack = jnp.stack(around)
    mine = lax.dynamic_index_in_dim(stack, core, 1, False)
    theirs = swapped(lax.dynamic_index_in_dim(stack, 1 - core, 1, False))

    own_t = swapped(slowness)
    near_m = jnp.concatenate(
        [moved(slowness, "pair", 1), moved(slowness, "pair", -1), moved(slowness[:1], "pair", -2)]
    )
    near_t = swapped(near_m)

    b, ob, cn = pl.pallas_call(
        scatter_kernel,
        out_shape=(struct(PLANES, 1024, 128), struct(KEPT, 1024, 128), struct(KEPT, 1024, 128)),
        in_specs=[SMEM, VMEM, VMEM],
        out_specs=(VMEM,) * 3,
        compiler_params=params(24),
        name="scatter",
    )(core_in, mine, theirs)

    padded = 1024 + 2 * PAD
    inv, v0, v1, v2, msg = pl.pallas_call(
        forward_kernel,
        out_shape=(
            struct(PLANES, 1024, 128), struct(13, padded, 128), struct(11, padded, 128),
            struct(9, padded, 128), struct(8, 128),
        ),
        in_specs=[SMEM] + [VMEM] * 5,
        out_specs=(VMEM,) * 5,
        compiler_params=params(40),
        name="forward",
    )(par, slowness, own_t, near_m, near_t, b)

    wave, u0, u1, u2, msg = pl.pallas_call(
        adjoint_kernel,
        out_shape=(
            struct(4, 1024, 128), struct(9, padded, 128), struct(7, padded, 128),
            struct(5, padded, 128), struct(8, 128),
        ),
        in_specs=[VMEM] * 7,
        out_specs=(VMEM,) * 5,
        compiler_params=params(50),
        name="adjoint",
    )(pair_sum(msg), inv, v0, v1, v2, ob, cn)

    parts = pl.pallas_call(
        gradient_kernel,
        out_shape=struct(8, 2, 128, 128),
        in_specs=[SMEM] + [VMEM] * 5,
        out_specs=VMEM,
        scratch_shapes=[pltpu.VMEM((4096, 128), jnp.float32)],
        compiler_params=params(24),
        name="gradient",
    )(par, pair_sum(msg), wave, u0, u1, u2)

    parts = lax.all_to_all(parts, ("lap", "core"), 0, 0, tiled=True)
    own_grad, power = pl.pallas_call(
        power_kernel,
        out_shape=(struct(2, 128, 128), struct(128, 128)),
        in_specs=[VMEM],
        out_specs=(VMEM, VMEM),
        name="power",
    )(parts)
    power = lax.all_to_all(power, ("lap", "pair", "core"), 0, 0, tiled=True)
    power_sum = jnp.sum(power[:, 0])

    band_rows = rows_y // lax.axis_size("lap")
    start_y = lap * band_rows
    space_pos = pair * 2 + core
    slabs = pairs * 2
    total_cells = slab_cells * slabs
    scaled = own_grad / jnp.sqrt(power_sum / total_cells + 1e-06)
    padded_model = jnp.pad(slowness, ((0, 0), (0, 1), (0, 0)))
    window = lax.dynamic_slice_in_dim(padded_model, start_y, band_rows + 1, 1)
    own_model = window[:, :band_rows]
    x_glob = space_pos * width_x + jnp.arange(width_x, dtype=jnp.int32)
    last_x = (x_glob == width_x * slabs - 1)[:, None, None]
    y_glob = start_y + jnp.arange(band_rows, dtype=jnp.int32)
    last_y = (y_glob == rows_y - 1)[None, :, None]
    following = lax.dynamic_slice_in_dim(
        jnp.where(core == 0, own_t[:1], near_t[2:3]), start_y, band_rows, 1
    )
    step_x = jnp.where(last_x, 0.0, jnp.concatenate([own_model[1:], following], 0) - own_model)
    step_y = jnp.where(last_y, 0.0, window[:, 1:] - own_model)
    step_z = jnp.concatenate(
        [own_model[:, :, 1:] - own_model[:, :, :-1], jnp.zeros_like(own_model[:, :, :1])], 2
    )
    dual_trial = dual + dual_step * jnp.stack([step_x, step_y, step_z])
    magnitude = jnp.sqrt(jnp.sum(dual_trial * dual_trial, axis=0))
    dual_next = dual_trial / jnp.maximum(1.0, magnitude / tv_weight)
    comp_x = jnp.where(last_x, 0.0, dual_next[0])
    comp_y = jnp.where(last_y, 0.0, dual_next[1])
    comp_z = jnp.concatenate([dual_next[2][:, :, :-1], jnp.zeros_like(dual_next[2][:, :, :1])], 2)
    prior_x = moved(comp_x[-1:], ("pair", "core"), 1)
    back_x = jnp.concatenate([prior_x, comp_x[:-1]], 0) - comp_x
    prior_y = moved(comp_y[:, -1:], "lap", 1)
    back_y = jnp.concatenate([prior_y, comp_y[:, :-1]], 1) - comp_y
    back_z = jnp.concatenate([jnp.zeros_like(comp_z[:, :, :1]), comp_z[:, :, :-1]], 2) - comp_z
    model = own_model - primal_step * (scaled + back_x + back_y + back_z)
    return (model, dual_next)


def solution(mesh):
    space = mesh.devices.shape[1]
    mesh = Mesh(mesh.devices.reshape(-1, space // 2, 2), ("lap", "pair", "core"))
    both = ("pair", "core")
    in_specs = (
        P(both, None, None),
        P("lap"),
        P(both),
        P("lap", both),
        P(both),
        P("lap", both),
        P(None, both, "lap", None),
    )
    out_specs = (P(both, "lap", None), P(None, both, "lap", None))
    return jax.shard_map(
        on_device, mesh=mesh, in_specs=in_specs, out_specs=out_specs, check_vma=False
    )
```

```python
import functools

import jax
import jax.numpy as jnp
from jax import lax
from jax.experimental import pallas as pl
from jax.experimental.pallas import tpu as pltpu
from jax.sharding import Mesh
from jax.sharding import PartitionSpec as P


HALF = 2
PLANES = 13
KEPT = 9
PAD = 8
ROWS = 1024

dual_step = 0.5
primal_step = 0.2
tv_weight = 0.5

VMEM = pl.BlockSpec(memory_space=pltpu.VMEM)
SMEM = pl.BlockSpec(memory_space=pltpu.SMEM)


def params(mib):
    return pltpu.CompilerParams(vmem_limit_bytes=mib * 2**20)


def spread_points(index, parts, right_planes, write):
    points = index.shape[1]
    column = (index >> 16) * 128 + (index & 127)
    row = ((index >> 7) & 511) - lax.broadcasted_iota(jnp.int32, (8, points), 0) // HALF
    lanes = lax.broadcasted_iota(jnp.int32, (right_planes * 128, points), 0)
    right = jnp.where(lanes == column, 1.0, 0.0).astype(jnp.bfloat16)
    tile = lax.broadcasted_iota(jnp.int32, (ROWS // 8, 8, points), 0)
    mask = row[None] == (8 // HALF) * tile
    for which, part in enumerate(parts):
        total = None
        for piece in part:
            left = jnp.where(mask, piece[None], 0.0).reshape(ROWS, points).astype(jnp.bfloat16)
            got = lax.dot_general(
                left, right, (((1,), (1,)), ((), ())), preferred_element_type=jnp.float32
            )
            total = got if total is None else total + got
        for p in range(right_planes):
            write(which, p, total[:, p * 128 : (p + 1) * 128])


def pieces_of(value, count):
    high = value.astype(jnp.bfloat16).astype(jnp.float32)
    return [high, value - high][:count]


def points_of(core, lists, first):
    points = lists.shape[1]
    parity = lax.broadcasted_iota(jnp.int32, (8, points), 0) % HALF
    even = jnp.where(core == 0, lists[first : first + 1], lists[first + 2 : first + 3])
    odd = jnp.where(core == 0, lists[first + 1 : first + 2], lists[first + 3 : first + 4])
    return jnp.where(parity == 0, even, odd)


def writer(stores):
    def write(which, p, value):
        ref, first = stores[which]
        ref[first + p] = value

    return write


def scatter_src(core, lists, count, store, first):
    amp = points_of(core, lists, 2)
    index = lists[0:1].astype(jnp.int32)
    spread_points(index, [pieces_of(amp, count)], 2, writer([(store, first)]))


def scatter_rec(core, lists, count, planes, ob, cn, first):
    obs = points_of(core, lists, 6)
    index = lists[1:2].astype(jnp.int32)
    parts = [pieces_of(obs, count), [jnp.ones_like(obs)]]
    spread_points(index, parts, planes, writer([(ob, first), (cn, first)]))


def scatter_own_kernel(core_ref, lists, b, ob, cn):
    core = core_ref[0]

    def body(h, _):
        scatter_src(core, lists[h], 2, b, 2 * h)
        scatter_rec(core, lists[h], 2, 2, ob, cn, 2 * h)
        return 0

    lax.fori_loop(0, 2, body, 0)


def scatter_src_kernel(core_ref, low, high, far, b, held):
    core = core_ref[0]
    for k, rows in enumerate((low[1], high[0], low[0], high[1], far[0])):
        held[k, 0:10] = rows

    def two(k, _):
        scatter_src(core, held[k, 0:10], 2, b, 2 + 2 * k)
        return 0

    def one(k, _):
        scatter_src(core, held[2 + k, 0:10], 1, b, jnp.where(k == 0, 0, 4 + 2 * k))
        return 0

    lax.fori_loop(0, 2, two, 0)
    lax.fori_loop(0, 3, one, 0)


def scatter_rec_kernel(core_ref, low, high, ob, cn, held):
    core = core_ref[0]
    for k, rows in enumerate((low[1], high[0])):
        held[k, 0:10] = rows

    def two(k, _):
        scatter_rec(core, held[k, 0:10], 2, 2, ob, cn, 2 * k)
        return 0

    lax.fori_loop(0, 2, two, 0)
    scatter_rec(core, high[1], 1, 1, ob, cn, 4)


def shift_matrix():
    i = lax.broadcasted_iota(jnp.int32, (128, 128), 0)
    j = lax.broadcasted_iota(jnp.int32, (128, 128), 1)
    return jnp.where(jnp.abs(i - j) == 1, 1.0, 0.0).astype(jnp.bfloat16)


def neighbours(ref, t):
    ext = ref[t]
    x = ext[PAD : PAD + ROWS]
    total = ROWS + 2 * PAD
    down = pltpu.roll(ext, HALF, 0)[PAD : PAD + ROWS]
    up = pltpu.roll(ext, total - HALF, 0)[PAD : PAD + ROWS]
    high = x.astype(jnp.bfloat16)
    low = (x - high.astype(jnp.float32)).astype(jnp.bfloat16)
    matrix = shift_matrix()
    along = jnp.dot(high, matrix, preferred_element_type=jnp.float32)
    along = along + jnp.dot(low, matrix, preferred_element_type=jnp.float32)
    return x, (down + up) + along


def fold(x):
    return jnp.sum(x.reshape(ROWS // 8, 8, 128), 0)


def walk(first, last, body, carry):
    return lax.fori_loop(first, last, body, carry)


INNER = pl.ds(PAD, 1024)


def advance(src, s_off, inv, i_off, dst, d_off, first, last, dots):
    def body(t, carry):
        x, q = neighbours(src, t - s_off)
        q = q + (src[t - s_off - 1, INNER, :] + src[t - s_off + 1, INNER, :])
        new = inv[t - i_off] * q
        dst[t - d_off, INNER, :] = new
        if not dots:
            return carry
        return carry[0] + fold(x * q), carry[1] + fold(new * q)

    zero = jnp.zeros((8, 128), jnp.float32)
    return walk(first, last, body, (zero, zero) if dots else 0)


def last_moment(src, off):
    def body(t, carry):
        x, q = neighbours(src, t - off)
        q = q + 2.0 * src[t - off + 1, INNER, :]
        return carry + fold(x * q)

    return walk(4, 8, body, jnp.zeros((8, 128), jnp.float32))


def clear_pads(*refs):
    for ref in refs:
        zero = jnp.zeros((8, 128), jnp.float32)
        for t in range(ref.shape[0]):
            ref[t, 0:PAD, :] = zero
            ref[t, ref.shape[1] - PAD :, :] = zero


def message(moments):
    sub = lax.broadcasted_iota(jnp.int32, (8, 128), 0)
    lane = lax.broadcasted_iota(jnp.int32, (8, 128), 1)
    out = jnp.zeros((8, 128), jnp.float32)
    for k, moment in enumerate(moments):
        for c in range(HALF):
            total = jnp.sum(jnp.where(sub % HALF == c, moment, 0.0))
            out = out + jnp.where((sub == k) & (lane == c), total, 0.0)
    return out


def coefficients(moments):
    m = [moments[k : k + 1, :] for k in range(6)]

    def product(p, shift):
        total = 0.0
        for i, a in enumerate(p):
            for j, b in enumerate(p):
                total = total + a * b * (m[i + j] - m[i + j + 1] if shift else m[i + j])
        return total

    one = jnp.ones_like(m[0])
    z, p, energy = [one], [one], m[0]
    x = [0.0 * one] * 3
    for it in range(3):
        stride = energy / product(p, True)
        x = [x[i] + (stride * p[i] if i < len(p) else 0.0) for i in range(3)]
        if it < 2:
            applied = [a - b for a, b in zip(p + [0.0 * one], [0.0 * one] + p)]
            z = [a - stride * b for a, b in zip(z + [0.0 * one], applied)]
            new = product(z, False)
            p = [a + new / energy * b for a, b in zip(z, p + [0.0 * one])]
            energy = new
    lane = lax.broadcasted_iota(jnp.int32, (1, 128), 1)
    sub = lax.broadcasted_iota(jnp.int32, (8, 128), 0)
    out = []
    for v in x:
        value = [jnp.sum(jnp.where(lane == c, v, 0.0)) for c in range(HALF)]
        out.append(jnp.where(sub % HALF == 0, value[0], value[1]))
    return out


def times(pattern, x):
    return (pattern[None] * x.reshape(ROWS // 8, 8, 128)).reshape(ROWS, 128)


def forward_kernel(par, own_m, own_t, near_m, near_t, b_own, b_near, inv, v0, v1, v2, msg):
    core = par[5]
    slabs = (
        (near_m, near_t, 0, 0, 2), (near_m, near_t, 0, 1, 2),
        (own_m, own_t, 0, 0, None), (own_m, own_t, 0, 1, None),
        (near_m, near_t, 2, 0, 3), (near_m, near_t, 2, 1, 3), (near_m, near_t, 4, 0, 4),
    )
    clear_pads(v0, v1, v2)
    for slab, (mine, theirs, base, h, flag) in enumerate(slabs):
        valid = 1.0 if flag is None else par[flag]
        planes = 1 if slab == 6 else 2

        def fill(p, _, mine=mine, theirs=theirs, base=base, h=h, valid=valid, slab=slab):
            sigma = jnp.where(core == float(h), mine[base + p], theirs[base + p])
            for c in range(HALF):
                inv[2 * slab + p, pl.ds(c, 512, stride=HALF), :] = valid / (6.0 + par[c] * sigma)
            return 0

        lax.fori_loop(0, planes, fill, 0)

    def start(b, off, dots):
        def body(t, carry):
            right = b[t - off]
            new = inv[t] * right
            v0[t, INNER, :] = new
            return carry + fold(new * right) if dots else carry

        return body

    zero = jnp.zeros((8, 128), jnp.float32)
    walk(0, 4, start(b_near, 0, False), 0)
    m0 = walk(4, 8, start(b_own, 4, True), zero)
    walk(8, 13, start(b_near, 4, False), 0)
    advance(v0, 0, inv, 0, v1, 1, 1, 4, False)
    m1, m2 = advance(v0, 0, inv, 0, v1, 1, 4, 8, True)
    advance(v0, 0, inv, 0, v1, 1, 8, 12, False)
    advance(v1, 1, inv, 0, v2, 2, 2, 4, False)
    m3, m4 = advance(v1, 1, inv, 0, v2, 2, 4, 8, True)
    advance(v1, 1, inv, 0, v2, 2, 8, 11, False)
    m5 = last_moment(v2, 2)
    msg[...] = message([m0, m1, m2, m3, m4, m5])


def adjoint_kernel(
    total, inv, v0, v1, v2, ob_own, cn_own, ob_near, cn_near, wave, u0, u1, u2, msg
):
    a = coefficients(total[...])

    def start(ob, cn, off, own):
        def body(t, carry):
            w = times(a[0], v0[t, INNER, :]) + times(a[1], v1[t - 1, INNER, :])
            w = w + times(a[2], v2[t - 2, INNER, :])
            right = cn[t - off] * w - ob[t - off]
            new = inv[t] * right
            u0[t, INNER, :] = new
            if not own:
                return carry
            wave[t - 4] = w
            return carry + fold(new * right)

        return body

    zero = jnp.zeros((8, 128), jnp.float32)
    walk(2, 4, start(ob_near, cn_near, 2, False), 0)
    m0 = walk(4, 8, start(ob_own, cn_own, 4, True), zero)
    walk(8, 11, start(ob_near, cn_near, 6, False), 0)
    advance(u0, 0, inv, 0, u1, 1, 3, 4, False)
    m1, m2 = advance(u0, 0, inv, 0, u1, 1, 4, 8, True)
    advance(u0, 0, inv, 0, u1, 1, 8, 10, False)
    m3, m4 = advance(u1, 1, inv, 0, u2, 2, 4, 8, True)
    advance(u1, 1, inv, 0, u2, 2, 8, 9, False)
    m5 = last_moment(u2, 2)
    msg[...] = message([m0, m1, m2, m3, m4, m5])


def gradient_kernel(other, spot, par, total, wave, u0, u1, u2, *rest):
    out, held = rest[-2:]
    a = coefficients(total[...])
    sub = lax.broadcasted_iota(jnp.int32, (8, 128), 0)
    square = jnp.where(sub % HALF == 0, par[0], par[1])
    a = [-square * v for v in a]
    core = 1 - spot[2] if other else spot[2]
    for p in range(2):
        t = 4 + 2 * core + p
        x = times(a[0], u0[t, INNER, :]) + times(a[1], u1[t - 1, INNER, :])
        x = x + times(a[2], u2[t - 2, INNER, :])
        held[...] = x * wave[t - 4]
        for band in range(4):
            at = band * 256
            both = held[pl.ds(at, 128, stride=HALF), :] + held[pl.ds(at + 1, 128, stride=HALF), :]
            out[band, p] = both if other else both + rest[0][band, p]


def power_kernel(parts, own, msg):
    g = (parts[0] + parts[1]) + (parts[2] + parts[3])
    own[...] = g
    msg[...] = jnp.full((128, 128), jnp.sum(g * g), jnp.float32)


def variation_kernel(spot, slow, own_t, near_t, dual, dual_next, base, send_x, send_y):
    lap, pair, core = spot[0], spot[1], spot[2]
    start = pl.multiple_of(lap * 128, 128)
    band = pl.ds(start, 128)
    after = pl.ds(pl.multiple_of(jnp.minimum(start + 128, 504), 8), 8)
    row = lax.broadcasted_iota(jnp.int32, (128, 128), 0)
    lane = lax.broadcasted_iota(jnp.int32, (128, 128), 1)
    last_y = (row == 127) & (lap == 3)
    last_z = lane == 127
    comps = []
    for p in range(2):
        here = slow[p, band, :]
        if p == 0:
            step_x = slow[1, band, :] - here
        else:
            step_x = jnp.where(core == 0, own_t[0, band, :], near_t[2, band, :]) - here
            step_x = jnp.where((core == 1) & (pair == 15), 0.0, step_x)
        rolled = pltpu.roll(here, 127, 0)
        step_y = jnp.where(row == 127, slow[p, after, :][0:1], rolled) - here
        step_y = jnp.where(last_y, 0.0, step_y)
        step_z = jnp.where(last_z, 0.0, pltpu.roll(here, 127, 1) - here)
        trial = [dual[k, p] + dual_step * step for k, step in enumerate((step_x, step_y, step_z))]
        magnitude = jnp.sqrt(trial[0] * trial[0] + trial[1] * trial[1] + trial[2] * trial[2])
        scale = jnp.maximum(1.0, magnitude / tv_weight)
        new = [x / scale for x in trial]
        for k in range(3):
            dual_next[k, p] = new[k]
        if p == 1:
            new[0] = jnp.where((core == 1) & (pair == 15), 0.0, new[0])
        new[1] = jnp.where(last_y, 0.0, new[1])
        new[2] = jnp.where(last_z, 0.0, new[2])
        comps.append(new)
    for p in range(2):
        x, y, z = comps[p]
        back = jnp.where(row == 0, 0.0, pltpu.roll(y, 1, 0)) - y
        back = back + (jnp.where(lane == 0, 0.0, pltpu.roll(z, 1, 1)) - z)
        back = back + (comps[0][0] - x if p == 1 else -x)
        base[p] = slow[p, band, :] - primal_step * back
        send_y[p] = y[120:128]
    send_x[0] = comps[1][0]


def model_kernel(cells, base, grad, power, prior_x, prior_y, model):
    total = power[0]
    for k in range(1, 16):
        total = total + power[k]
    total = jnp.sum(total, axis=0, keepdims=True)
    scale = 1.0 / jnp.sqrt(total / cells + 1e-06)
    row = lax.broadcasted_iota(jnp.int32, (128, 128), 0)
    for p in range(2):
        back = jnp.where(row == 0, prior_y[p][7:8], 0.0)
        if p == 0:
            back = back + prior_x[0]
        model[p] = base[p] - primal_step * (grad[p] * scale + back)


def cost(work):
    return pl.CostEstimate(flops=work * 10**9, bytes_accessed=10**6, transcendentals=0)


def struct(*shape):
    return jax.ShapeDtypeStruct(shape, jnp.float32)


def moved(x, axis, by):
    peers = lax.axis_size(axis)
    return lax.ppermute(x, axis, [(i, i + by) for i in range(peers) if 0 <= i + by < peers])


def swapped(x):
    return lax.ppermute(x, "core", [(0, 1), (1, 0)])


def pair_sum(x):
    for masks in ((1, 2, 3), (4, 8, 12)):
        x = x + sum(lax.ppermute(x, "pair", [(i, i ^ d) for i in range(16)]) for d in masks)
    return x


def on_device(slowness, damping, src_index, src_amp, rec_index, observed, dual):
    width_x, rows_y, depth_z = slowness.shape
    slab_cells = width_x * rows_y * depth_z
    lap, pair, core = (lax.axis_index(name) for name in ("lap", "pair", "core"))
    pairs = lax.axis_size("pair")
    offset = (pair * 2 + core) * slab_cells

    squared = damping * damping
    own_sq = lax.dynamic_slice_in_dim(squared, core * HALF, HALF)
    flags = jnp.stack([pair >= 1, pair + 1 < pairs, pair + 2 < pairs, core == 1])
    par = jnp.concatenate([own_sq, flags.astype(jnp.float32), jnp.zeros(2, jnp.float32)])
    core_in = core.astype(jnp.int32).reshape(1)

    index = jnp.stack([src_index - offset, rec_index - offset]).astype(jnp.float32)
    lists = jnp.concatenate([index, src_amp, observed])
    spot = jnp.stack([lap, pair, core, core]).astype(jnp.int32)
    lists, par, core_in, spot = lax.optimization_barrier((lists, par, core_in, spot))
    other = swapped(lists)
    both = jnp.where(core_in[0] == 0, jnp.stack([lists, other]), jnp.stack([other, lists]))
    low, high, far = (moved(both, "pair", by) for by in (1, -1, -2))
    first = slowness[:1]
    sigma, first, both = lax.optimization_barrier((slowness, first, both))
    around = [
        moved(sigma, "pair", 1),
        moved(sigma, "pair", -1),
        lax.ppermute(first, ("pair", "core"), [(2 * i, 2 * i - 4) for i in range(2, pairs)]),
    ]
    own_t = swapped(sigma)

    points = lists.shape[1]
    b_own, ob_own, cn_own = pl.pallas_call(
        scatter_own_kernel,
        out_shape=(struct(4, ROWS, 128),) * 3,
        in_specs=[SMEM, VMEM],
        out_specs=(VMEM,) * 3,
        compiler_params=params(24),
        cost_estimate=cost(10),
        name="scatter_own",
    )(core_in, both)
    low, high, far, b_own = lax.optimization_barrier((low, high, far, b_own))
    held = pltpu.VMEM((5, 16, points), jnp.float32)
    b_near = pl.pallas_call(
        scatter_src_kernel,
        out_shape=struct(10, ROWS, 128),
        in_specs=[SMEM] + [VMEM] * 3,
        out_specs=VMEM,
        scratch_shapes=[held],
        compiler_params=params(24),
        cost_estimate=cost(7),
        name="scatter_src",
    )(core_in, low, high, far)
    around, b_near = lax.optimization_barrier((around, b_near))
    near_m = jnp.concatenate(around)
    near_t = swapped(near_m)
    near_m, low = lax.optimization_barrier((near_m, low))
    ob_near, cn_near = pl.pallas_call(
        scatter_rec_kernel,
        out_shape=(struct(5, ROWS, 128),) * 2,
        in_specs=[SMEM] + [VMEM] * 2,
        out_specs=(VMEM,) * 2,
        scratch_shapes=[held],
        compiler_params=params(24),
        cost_estimate=cost(8),
        name="scatter_rec",
    )(core_in, low, high)
    near_t, ob_near = lax.optimization_barrier((near_t, ob_near))

    padded = ROWS + 2 * PAD
    inv, v0, v1, v2, msg = pl.pallas_call(
        forward_kernel,
        out_shape=(
            struct(PLANES, ROWS, 128), struct(13, padded, 128), struct(11, padded, 128),
            struct(9, padded, 128), struct(8, 128),
        ),
        in_specs=[SMEM] + [VMEM] * 6,
        out_specs=(VMEM,) * 5,
        compiler_params=params(8),
        cost_estimate=cost(20),
        name="forward",
    )(par, slowness, own_t, near_m, near_t, b_own, b_near)

    wave, u0, u1, u2, msg = pl.pallas_call(
        adjoint_kernel,
        out_shape=(
            struct(4, ROWS, 128), struct(13, padded, 128), struct(11, padded, 128),
            struct(9, padded, 128), struct(8, 128),
        ),
        in_specs=[VMEM] * 9,
        out_specs=(VMEM,) * 5,
        input_output_aliases={2: 1, 3: 2, 4: 3},
        compiler_params=params(8),
        cost_estimate=cost(14),
        name="adjoint",
    )(pair_sum(msg), inv, v0, v1, v2, ob_own, cn_own, ob_near, cn_near)

    total = pair_sum(msg)

    def gradient(other, *more):
        return pl.pallas_call(
            functools.partial(gradient_kernel, other),
            out_shape=struct(4, 2, 128, 128),
            in_specs=[SMEM, SMEM] + [VMEM] * (5 + len(more)),
            out_specs=VMEM,
            scratch_shapes=[pltpu.VMEM((ROWS, 128), jnp.float32)],
            compiler_params=params(8),
            name="gradient",
        )(spot, par, total, wave, u0, u1, u2, *more)

    parts = gradient(False, swapped(gradient(True)))
    slowness, dual, own_t, near_t, parts = lax.optimization_barrier(
        (slowness, dual, own_t, near_t, parts)
    )
    arrived = lax.all_to_all(parts, "lap", 0, 0, tiled=True)
    dual_next, base, send_x, send_y = pl.pallas_call(
        variation_kernel,
        out_shape=(
            struct(3, 2, 128, 128), struct(2, 128, 128), struct(1, 128, 128), struct(2, 8, 128),
        ),
        in_specs=[SMEM] + [VMEM] * 4,
        out_specs=(VMEM,) * 4,
        compiler_params=params(8),
        cost_estimate=cost(1),
        name="variation",
    )(spot, slowness, own_t, near_t, dual)
    own_grad, power = pl.pallas_call(
        power_kernel,
        out_shape=(struct(2, 128, 128), struct(128, 128)),
        in_specs=[VMEM],
        out_specs=(VMEM, VMEM),
        compiler_params=params(8),
        name="power",
    )(arrived)
    power = lax.all_to_all(power, ("lap", "pair", "core"), 0, 0, tiled=True)
    prior_x = moved(send_x, ("pair", "core"), 1)
    prior_y = moved(send_y, "lap", 1)
    model = pl.pallas_call(
        functools.partial(model_kernel, float(slab_cells * 2 * pairs)),
        out_shape=struct(2, 128, 128),
        in_specs=[VMEM] * 5,
        out_specs=VMEM,
        compiler_params=params(8),
        name="model",
    )(base, own_grad, power.reshape(16, 8, 128), prior_x, prior_y)
    return (model, dual_next)


def solution(mesh):
    space = mesh.devices.shape[1]
    mesh = Mesh(mesh.devices.reshape(-1, space // 2, 2), ("lap", "pair", "core"))
    both = ("pair", "core")
    in_specs = (
        P(both, None, None),
        P("lap"),
        P(both),
        P("lap", both),
        P(both),
        P("lap", both),
        P(None, both, "lap", None),
    )
    out_specs = (P(both, "lap", None), P(None, both, "lap", None))
    return jax.shard_map(
        on_device, mesh=mesh, in_specs=in_specs, out_specs=out_specs, check_vma=False
    )
```

```python
import functools

import jax
import jax.numpy as jnp
from jax import lax
from jax.experimental import pallas as pl
from jax.experimental.pallas import tpu as pltpu
from jax.sharding import Mesh
from jax.sharding import PartitionSpec as P


HALF = 2
PLANES = 13
KEPT = 9
PAD = 8
ROWS = 1024
LIST = 88
SLAB = ROWS + LIST

dual_step = 0.5
primal_step = 0.2
tv_weight = 0.5

VMEM = pl.BlockSpec(memory_space=pltpu.VMEM)
SMEM = pl.BlockSpec(memory_space=pltpu.SMEM)


def params(mib):
    return pltpu.CompilerParams(vmem_limit_bytes=mib * 2**20)


def spread_points(index, parts, right_planes, write):
    points = index.shape[1]
    column = (index >> 16) * 128 + (index & 127)
    row = ((index >> 7) & 511) - lax.broadcasted_iota(jnp.int32, (8, points), 0) // HALF
    lanes = lax.broadcasted_iota(jnp.int32, (right_planes * 128, points), 0)
    right = jnp.where(lanes == column, 1.0, 0.0).astype(jnp.bfloat16)
    tile = lax.broadcasted_iota(jnp.int32, (ROWS // 8, 8, points), 0)
    mask = row[None] == (8 // HALF) * tile
    for which, part in enumerate(parts):
        total = None
        for piece in part:
            left = jnp.where(mask, piece[None], 0.0).reshape(ROWS, points).astype(jnp.bfloat16)
            got = lax.dot_general(
                left, right, (((1,), (1,)), ((), ())), preferred_element_type=jnp.float32
            )
            total = got if total is None else total + got
        for p in range(right_planes):
            write(which, p, total[:, p * 128 : (p + 1) * 128])


def pieces_of(value, count):
    high = value.astype(jnp.bfloat16).astype(jnp.float32)
    return [high, value - high][:count]


def list_row(ref, base, i):
    block = ref[base + 8 * i : base + 8 * i + 8, :]
    return jnp.concatenate([block[j : j + 1] for j in range(8)], 1)


def either(core, zero, one):
    return lambda i: jnp.where(core == 0, list_row(*zero, i), list_row(*one, i))


def by_parity(even, odd, points):
    parity = lax.broadcasted_iota(jnp.int32, (8, points), 0) % HALF
    return jnp.where(parity == 0, even, odd)


def points_of(core, row, first):
    even = jnp.where(core == 0, row(first), row(first + 2))
    odd = jnp.where(core == 0, row(first + 1), row(first + 3))
    return by_parity(even, odd, even.shape[1])


def writer(stores):
    def write(which, p, value):
        ref, first = stores[which]
        ref[first + p] = value

    return write


def scatter_src(core, row, count, store, first, divisor=None, planes=2):
    amp = points_of(core, row, 2)
    if divisor is not None:
        amp = amp / divisor
    index = row(0).astype(jnp.int32)
    spread_points(index, [pieces_of(amp, count)], planes, writer([(store, first)]))


def scatter_rec(core, row, count, planes, ob, cn, first):
    obs = points_of(core, row, 6)
    parts = [pieces_of(obs, count), [jnp.ones_like(obs)]]
    index = row(1).astype(jnp.int32)
    spread_points(index, parts, planes, writer([(ob, first), (cn, first)]))


def squares(damp):
    core = lax.axis_index("core")
    first, second = damp[HALF * core], damp[HALF * core + 1]
    return first * first, second * second


def diagonal_at(damp, row):
    sigma = row(10)
    first, second = squares(damp)
    return by_parity(6.0 + first * sigma, 6.0 + second * sigma, sigma.shape[1])


def pack_kernel(slow_in, src_in, rec_in, amp_in, obs_in, out, far, src, rec, amp, obs, sem):
    slab = lax.axis_index("pair") * 2 + lax.axis_index("core")
    offset = slab * (2 * 512 * 128)
    pairs = ((src_in, src), (rec_in, rec), (amp_in, amp), (obs_in, obs), (slow_in, out.at[0:ROWS]))
    copies = [pltpu.make_async_copy(x, y, sem.at[k]) for k, (x, y) in enumerate(pairs)]
    for copy in copies:
        copy.start()
    for copy in copies:
        copy.wait()
    points = amp.shape[1]
    far[0:8, :] = (src[...] - offset).astype(jnp.float32)
    far[8:16, :] = (rec[...] - offset).astype(jnp.float32)
    for k, values in ((2, amp), (6, obs)):
        for i in range(4):
            for j in range(8):
                at = 8 * (k + i) + j
                far[at : at + 1, :] = values[i : i + 1, 128 * j : 128 * j + 128]
    index = list_row(far, 0, 0).astype(jnp.int32)
    rows = lax.broadcasted_iota(jnp.int32, (ROWS, points), 0)
    pick = jnp.where(rows == index >> 7, 1.0, 0.0).astype(jnp.bfloat16)
    sigma = out[0:ROWS, :]
    high = sigma.astype(jnp.bfloat16)
    low = (sigma - high.astype(jnp.float32)).astype(jnp.bfloat16)
    dims = (((0,), (0,)), ((), ()))
    got = lax.dot_general(high, pick, dims, preferred_element_type=jnp.float32)
    got = got + lax.dot_general(low, pick, dims, preferred_element_type=jnp.float32)
    lane = lax.broadcasted_iota(jnp.int32, (128, points), 0)
    found = jnp.sum(jnp.where(lane == index & 127, got, 0.0), axis=0, keepdims=True)
    for j in range(8):
        far[80 + j : 81 + j, :] = found[:, 128 * j : 128 * j + 128]
    out[ROWS : ROWS + LIST, :] = far[...]


def scatter_slab(h, row, b, ob, cn):
    core = lax.axis_index("core")
    scatter_src(core, row, 2, b, 2 * h)
    scatter_rec(core, row, 2, 2, ob, cn, 2 * h)


def scatter_own_kernel(lists, b, ob, cn):
    scatter_slab(lax.axis_index("core"), functools.partial(list_row, lists, 0), b, ob, cn)


def scatter_other_kernel(lists, other, b_in, ob_in, cn_in, b, ob, cn, first):
    core = lax.axis_index("core")
    first[...] = jnp.where(core == 0, lists[...], other[ROWS:SLAB, :])
    row = functools.partial(list_row, other, ROWS)
    scatter_slab(1 - lax.axis_index("core"), row, b, ob, cn)


def scatter_near(core, damp, heavy, heavy_low, light, light_low, b):
    scatter_src(core, heavy, 2, b, jnp.where(heavy_low, 2, 4))
    divisor = jnp.where(light_low, diagonal_at(damp, light), 1.0)
    scatter_src(core, light, 1, b, jnp.where(light_low, 0, 6), divisor)


def scatter_mine_kernel(damp, low, high, b, ob, cn):
    core = lax.axis_index("core")
    heavy = either(core, (high, ROWS), (low, ROWS))
    light = either(core, (low, ROWS), (high, ROWS))
    scatter_near(core, damp, heavy, core == 1, light, core == 0, b)
    scatter_rec(core, heavy, 2, 2, ob, cn, jnp.where(core == 1, 0, 2))


def scatter_theirs_kernel(damp, far, near, b_in, b):
    core = lax.axis_index("core")
    low_at, high_at = ROWS, SLAB + ROWS
    heavy = either(core, (near, low_at), (near, high_at))
    light = either(core, (near, high_at), (near, low_at))
    scatter_near(core, damp, heavy, core == 0, light, core == 1, b)
    last = functools.partial(list_row, far, 0)
    scatter_src(core, last, 1, b, 8, diagonal_at(damp, last), 1)


def scatter_late_kernel(high, near, ob_in, cn_in, ob, cn):
    core = lax.axis_index("core")
    low_at, high_at = ROWS, SLAB + ROWS
    heavy = either(core, (near, low_at), (near, high_at))
    scatter_rec(core, heavy, 2, 2, ob, cn, jnp.where(core == 0, 0, 2))
    scatter_rec(core, either(core, (near, high_at), (high, ROWS)), 1, 1, ob, cn, 4)


def shift_matrix():
    i = lax.broadcasted_iota(jnp.int32, (128, 128), 0)
    j = lax.broadcasted_iota(jnp.int32, (128, 128), 1)
    return jnp.where(jnp.abs(i - j) == 1, 1.0, 0.0).astype(jnp.bfloat16)


def neighbours(ref, t):
    ext = ref[t]
    x = ext[PAD : PAD + ROWS]
    total = ROWS + 2 * PAD
    down = pltpu.roll(ext, HALF, 0)[PAD : PAD + ROWS]
    up = pltpu.roll(ext, total - HALF, 0)[PAD : PAD + ROWS]
    high = x.astype(jnp.bfloat16)
    low = (x - high.astype(jnp.float32)).astype(jnp.bfloat16)
    matrix = shift_matrix()
    along = jnp.dot(high, matrix, preferred_element_type=jnp.float32)
    along = along + jnp.dot(low, matrix, preferred_element_type=jnp.float32)
    return x, (down + up) + along


def fold(x):
    return jnp.sum(x.reshape(ROWS // 8, 8, 128), 0)


def walk(first, last, body, carry):
    return lax.fori_loop(first, last, body, carry, unroll=True)


INNER = pl.ds(PAD, 1024)


def advance(src, s_off, inv, i_off, dst, d_off, first, last, dots):
    def body(t, carry):
        x, q = neighbours(src, t - s_off)
        q = q + (src[t - s_off - 1, INNER, :] + src[t - s_off + 1, INNER, :])
        new = inv[t - i_off] * q
        dst[t - d_off, INNER, :] = new
        if not dots:
            return carry
        return carry[0] + fold(x * q), carry[1] + fold(new * q)

    zero = jnp.zeros((8, 128), jnp.float32)
    return walk(first, last, body, (zero, zero) if dots else 0)


def last_moment(src, off):
    def body(t, carry):
        x, q = neighbours(src, t - off)
        q = q + 2.0 * src[t - off + 1, INNER, :]
        return carry + fold(x * q)

    return walk(4, 8, body, jnp.zeros((8, 128), jnp.float32))


def clear_pads(*refs):
    for ref in refs:
        zero = jnp.zeros((8, 128), jnp.float32)
        for t in range(ref.shape[0]):
            ref[t, 0:PAD, :] = zero
            ref[t, ref.shape[1] - PAD :, :] = zero


def message(moments):
    sub = lax.broadcasted_iota(jnp.int32, (8, 128), 0)
    lane = lax.broadcasted_iota(jnp.int32, (8, 128), 1)
    out = jnp.zeros((8, 128), jnp.float32)
    for k, moment in enumerate(moments):
        for c in range(HALF):
            total = jnp.sum(jnp.where(sub % HALF == c, moment, 0.0))
            out = out + jnp.where((sub == k) & (lane == c), total, 0.0)
    return out


def coefficients(moments):
    m = [moments[k : k + 1, :] for k in range(6)]

    def product(p, shift):
        total = 0.0
        for i, a in enumerate(p):
            for j, b in enumerate(p):
                total = total + a * b * (m[i + j] - m[i + j + 1] if shift else m[i + j])
        return total

    one = jnp.ones_like(m[0])
    z, p, energy = [one], [one], m[0]
    x = [0.0 * one] * 3
    for it in range(3):
        stride = energy / product(p, True)
        x = [x[i] + (stride * p[i] if i < len(p) else 0.0) for i in range(3)]
        if it < 2:
            applied = [a - b for a, b in zip(p + [0.0 * one], [0.0 * one] + p)]
            z = [a - stride * b for a, b in zip(z + [0.0 * one], applied)]
            new = product(z, False)
            p = [a + new / energy * b for a, b in zip(z, p + [0.0 * one])]
            energy = new
    lane = lax.broadcasted_iota(jnp.int32, (1, 128), 1)
    sub = lax.broadcasted_iota(jnp.int32, (8, 128), 0)
    out = []
    for v in x:
        value = [jnp.sum(jnp.where(lane == c, v, 0.0)) for c in range(HALF)]
        out.append(jnp.where(sub % HALF == 0, value[0], value[1]))
    return out


def times(pattern, x):
    return (pattern[None] * x.reshape(ROWS // 8, 8, 128)).reshape(ROWS, 128)


def forward_kernel(
    damp, own_m, own_t, low_m, high_m, near_t, b_own, b_near, inv, v0, v1, v2, msg
):
    pair, core = lax.axis_index("pair"), lax.axis_index("core")
    low = jnp.where(pair >= 1, 1.0, 0.0)
    high = jnp.where(pair + 1 < lax.axis_size("pair"), 1.0, 0.0)
    slabs = (
        (low_m, near_t, 0, low), (low_m, near_t, 0, low), (own_m, own_t, 0, 1.0),
        (own_m, own_t, 0, 1.0), (high_m, near_t, SLAB, high), (high_m, near_t, SLAB, high),
    )
    clear_pads(v0, v1, v2)
    square = squares(damp)
    for slab, (mine, theirs, base, valid) in enumerate(slabs):

        def fill(p, _, mine=mine, theirs=theirs, base=base, valid=valid, slab=slab):
            at = pl.multiple_of(p * 512, 512)
            here = mine[pl.ds(at, 512), :]
            there = theirs[pl.ds(pl.multiple_of(base + at, 8), 512), :]
            sigma = jnp.where(core == slab % 2, here, there)
            for c in range(HALF):
                inv[2 * slab + p, pl.ds(c, 512, stride=HALF), :] = valid / (6.0 + square[c] * sigma)
            return 0

        lax.fori_loop(1 if slab == 0 else 0, 2, fill, 0)

    def start(b, off, dots):
        def body(t, carry):
            right = b[t - off]
            new = inv[t] * right
            v0[t, INNER, :] = new
            return carry + fold(new * right) if dots else carry

        return body

    zero = jnp.zeros((8, 128), jnp.float32)
    for t, k in ((0, 0), (1, 1), (12, 8)):
        v0[t, INNER, :] = b_near[k]
    walk(2, 4, start(b_near, 0, False), 0)
    m0 = walk(4, 8, start(b_own, 4, True), zero)
    walk(8, 12, start(b_near, 4, False), 0)
    advance(v0, 0, inv, 0, v1, 1, 1, 4, False)
    m1, m2 = advance(v0, 0, inv, 0, v1, 1, 4, 8, True)
    advance(v0, 0, inv, 0, v1, 1, 8, 12, False)
    advance(v1, 1, inv, 0, v2, 2, 2, 4, False)
    m3, m4 = advance(v1, 1, inv, 0, v2, 2, 4, 8, True)
    advance(v1, 1, inv, 0, v2, 2, 8, 11, False)
    m5 = last_moment(v2, 2)
    msg[...] = message([m0, m1, m2, m3, m4, m5])


def adjoint_kernel(
    total, inv, v0, v1, v2, ob_own, cn_own, ob_near, cn_near, wave, u0, u1, u2, msg
):
    a = coefficients(total[...])

    def start(ob, cn, off, own):
        def body(t, carry):
            w = times(a[0], v0[t, INNER, :]) + times(a[1], v1[t - 1, INNER, :])
            w = w + times(a[2], v2[t - 2, INNER, :])
            right = cn[t - off] * w - ob[t - off]
            new = inv[t] * right
            u0[t, INNER, :] = new
            if not own:
                return carry
            wave[t - 4] = w
            return carry + fold(new * right)

        return body

    zero = jnp.zeros((8, 128), jnp.float32)
    walk(2, 4, start(ob_near, cn_near, 2, False), 0)
    m0 = walk(4, 8, start(ob_own, cn_own, 4, True), zero)
    walk(8, 11, start(ob_near, cn_near, 6, False), 0)
    advance(u0, 0, inv, 0, u1, 1, 3, 4, False)
    m1, m2 = advance(u0, 0, inv, 0, u1, 1, 4, 8, True)
    advance(u0, 0, inv, 0, u1, 1, 8, 10, False)
    m3, m4 = advance(u1, 1, inv, 0, u2, 2, 4, 8, True)
    advance(u1, 1, inv, 0, u2, 2, 8, 9, False)
    m5 = last_moment(u2, 2)
    msg[...] = message([m0, m1, m2, m3, m4, m5])


def gradient_kernel(other, damp, total, wave, u0, u1, u2, *rest):
    out, held = rest[-2:]
    a = coefficients(total[...])
    sub = lax.broadcasted_iota(jnp.int32, (8, 128), 0)
    square = jnp.where(sub % HALF == 0, *squares(damp))
    a = [-square * v for v in a]
    core = lax.axis_index("core")
    core = 1 - core if other else core
    for p in range(2):
        t = 4 + 2 * core + p
        x = times(a[0], u0[t, INNER, :]) + times(a[1], u1[t - 1, INNER, :])
        x = x + times(a[2], u2[t - 2, INNER, :])
        held[...] = x * wave[t - 4]
        for band in range(4):
            at = band * 256
            both = held[pl.ds(at, 128, stride=HALF), :] + held[pl.ds(at + 1, 128, stride=HALF), :]
            out[band, p] = both if other else both + rest[0][band, p]


def power_kernel(parts, own, msg):
    g = (parts[0] + parts[1]) + (parts[2] + parts[3])
    own[...] = g
    msg[...] = jnp.full((128, 128), jnp.sum(g * g), jnp.float32)


def variation_kernel(slow, own_t, near_t, dual, dual_next, base, send_x, send_y):
    lap, pair, core = (lax.axis_index(name) for name in ("lap", "pair", "core"))
    start = pl.multiple_of(lap * 128, 128)
    band = pl.ds(start, 128)
    after = pl.ds(pl.multiple_of(jnp.minimum(start + 128, 504), 8), 8)
    row = lax.broadcasted_iota(jnp.int32, (128, 128), 0)
    lane = lax.broadcasted_iota(jnp.int32, (128, 128), 1)
    last_y = (row == 127) & (lap == 3)
    last_z = lane == 127
    comps = []
    for p in range(2):
        here = slow[p, band, :]
        if p == 0:
            step_x = slow[1, band, :] - here
        else:
            beyond = near_t[pl.ds(pl.multiple_of(SLAB + start, 8), 128), :]
            step_x = jnp.where(core == 0, own_t[band, :], beyond) - here
            step_x = jnp.where((core == 1) & (pair == 15), 0.0, step_x)
        rolled = pltpu.roll(here, 127, 0)
        step_y = jnp.where(row == 127, slow[p, after, :][0:1], rolled) - here
        step_y = jnp.where(last_y, 0.0, step_y)
        step_z = jnp.where(last_z, 0.0, pltpu.roll(here, 127, 1) - here)
        trial = [dual[k, p] + dual_step * step for k, step in enumerate((step_x, step_y, step_z))]
        magnitude = jnp.sqrt(trial[0] * trial[0] + trial[1] * trial[1] + trial[2] * trial[2])
        scale = jnp.maximum(1.0, magnitude / tv_weight)
        new = [x / scale for x in trial]
        for k in range(3):
            dual_next[k, p] = new[k]
        if p == 1:
            new[0] = jnp.where((core == 1) & (pair == 15), 0.0, new[0])
        new[1] = jnp.where(last_y, 0.0, new[1])
        new[2] = jnp.where(last_z, 0.0, new[2])
        comps.append(new)
    for p in range(2):
        x, y, z = comps[p]
        back = jnp.where(row == 0, 0.0, pltpu.roll(y, 1, 0)) - y
        back = back + (jnp.where(lane == 0, 0.0, pltpu.roll(z, 1, 1)) - z)
        back = back + (comps[0][0] - x if p == 1 else -x)
        base[p] = slow[p, band, :] - primal_step * back
        send_y[p] = y[120:128]
    send_x[0] = comps[1][0]


def model_kernel(cells, base, grad, power, prior_x, prior_y, model):
    total = power[0]
    for k in range(1, 16):
        total = total + power[k]
    total = jnp.sum(total, axis=0, keepdims=True)
    scale = 1.0 / jnp.sqrt(total / cells + 1e-06)
    row = lax.broadcasted_iota(jnp.int32, (128, 128), 0)
    for p in range(2):
        back = jnp.where(row == 0, prior_y[p][7:8], 0.0)
        if p == 0:
            back = back + prior_x[0]
        model[p] = base[p] - primal_step * (grad[p] * scale + back)


def cost(work):
    return pl.CostEstimate(flops=work * 10**9, bytes_accessed=10**6, transcendentals=0)


def struct(*shape):
    return jax.ShapeDtypeStruct(shape, jnp.float32)


def moved(x, axis, by):
    peers = lax.axis_size(axis)
    return lax.ppermute(x, axis, [(i, i + by) for i in range(peers) if 0 <= i + by < peers])


def swapped(x):
    return lax.ppermute(x, "core", [(0, 1), (1, 0)])


def pair_sum(x):
    for masks in ((1, 2, 3), (4, 8, 12)):
        x = x + sum(lax.ppermute(x, "pair", [(i, i ^ d) for i in range(16)]) for d in masks)
    return x


def scatter(kernel, name, work, inputs, shapes, into=()):
    scalars = 1 if inputs[0].ndim == 1 else 0
    first = len(inputs)
    return pl.pallas_call(
        kernel,
        out_shape=tuple(struct(*shape) for shape in shapes),
        in_specs=[SMEM] * scalars + [VMEM] * (len(inputs) - scalars + len(into)),
        out_specs=(VMEM,) * len(shapes),
        input_output_aliases={first + k: k for k in range(len(into))},
        compiler_params=params(12),
        cost_estimate=cost(work),
        name=name,
    )(*inputs, *into)


def on_device(slowness, damping, src_index, src_amp, rec_index, observed, dual):
    width_x, rows_y, depth_z = slowness.shape
    slab_cells = width_x * rows_y * depth_z
    pairs = lax.axis_size("pair")

    packed, lists = pl.pallas_call(
        pack_kernel,
        out_shape=(struct(SLAB, 128), struct(LIST, 128)),
        in_specs=[pl.BlockSpec(memory_space=pltpu.HBM)] * 5,
        out_specs=(VMEM,) * 2,
        scratch_shapes=[
            pltpu.VMEM((8, 128), jnp.int32), pltpu.VMEM((8, 128), jnp.int32),
            pltpu.VMEM(src_amp.shape, jnp.float32), pltpu.VMEM(observed.shape, jnp.float32),
            pltpu.SemaphoreType.DMA((5,)),
        ],
        compiler_params=params(8),
        name="pack",
    )(
        *(
            pltpu.with_memory_space_constraint(x, pltpu.HBM)
            for x in (
                slowness.reshape(ROWS, 128), src_index.reshape(8, 128), rec_index.reshape(8, 128),
                src_amp, observed,
            )
        )
    )
    low_m, high_m = moved(packed, "pair", 1), moved(packed, "pair", -1)
    own_t = swapped(packed)

    block, near_block = (4, ROWS, 128), (5, ROWS, 128)
    own = scatter(scatter_own_kernel, "scatter_own", 5, (lists,), [block] * 3)
    b_own, ob_own, cn_own, first = scatter(
        scatter_other_kernel, "scatter_other", 5, (lists, own_t), [block] * 3 + [(LIST, 128)], own
    )
    far_m = moved(first, "pair", -2)
    low_m, high_m, far_m, b_own = lax.optimization_barrier((low_m, high_m, far_m, b_own))
    near_t = swapped(jnp.concatenate([low_m, high_m]))
    b_near, ob_near, cn_near = scatter(
        scatter_mine_kernel, "scatter_mine", 6, (damping, low_m, high_m),
        [(9, ROWS, 128), near_block, near_block],
    )
    near_t, b_near = lax.optimization_barrier((near_t, b_near))
    b_near, = scatter(
        scatter_theirs_kernel, "scatter_theirs", 5, (damping, far_m, near_t), [(9, ROWS, 128)],
        (b_near,),
    )

    padded = ROWS + 2 * PAD
    inv, v0, v1, v2, msg = pl.pallas_call(
        forward_kernel,
        out_shape=(
            struct(PLANES, ROWS, 128), struct(13, padded, 128), struct(11, padded, 128),
            struct(9, padded, 128), struct(8, 128),
        ),
        in_specs=[SMEM] + [VMEM] * 7,
        out_specs=(VMEM,) * 5,
        compiler_params=params(8),
        cost_estimate=cost(20),
        name="forward",
    )(damping, slowness.reshape(ROWS, 128), own_t, low_m, high_m, near_t, b_own, b_near)

    near_t, msg = lax.optimization_barrier((near_t, msg))
    ob_near, cn_near = scatter(
        scatter_late_kernel, "scatter_late", 5, (high_m, near_t), [near_block] * 2,
        (ob_near, cn_near),
    )
    wave, u0, u1, u2, msg = pl.pallas_call(
        adjoint_kernel,
        out_shape=(
            struct(4, ROWS, 128), struct(13, padded, 128), struct(11, padded, 128),
            struct(9, padded, 128), struct(8, 128),
        ),
        in_specs=[VMEM] * 9,
        out_specs=(VMEM,) * 5,
        input_output_aliases={2: 1, 3: 2, 4: 3},
        compiler_params=params(8),
        cost_estimate=cost(14),
        name="adjoint",
    )(pair_sum(msg), inv, v0, v1, v2, ob_own, cn_own, ob_near, cn_near)

    total = pair_sum(msg)

    def gradient(other, *more):
        return pl.pallas_call(
            functools.partial(gradient_kernel, other),
            out_shape=struct(4, 2, 128, 128),
            in_specs=[SMEM] + [VMEM] * (5 + len(more)),
            out_specs=VMEM,
            scratch_shapes=[pltpu.VMEM((ROWS, 128), jnp.float32)],
            compiler_params=params(8),
            name="gradient",
        )(damping, total, wave, u0, u1, u2, *more)

    parts = gradient(False, swapped(gradient(True)))
    slowness, dual, own_t, near_t, parts = lax.optimization_barrier(
        (slowness, dual, own_t, near_t, parts)
    )
    arrived = lax.all_to_all(parts, "lap", 0, 0, tiled=True)
    dual_next, base, send_x, send_y = pl.pallas_call(
        variation_kernel,
        out_shape=(
            struct(3, 2, 128, 128), struct(2, 128, 128), struct(1, 128, 128), struct(2, 8, 128),
        ),
        in_specs=[VMEM] * 4,
        out_specs=(VMEM,) * 4,
        compiler_params=params(8),
        cost_estimate=cost(1),
        name="variation",
    )(slowness, own_t, near_t, dual)
    prior_x = moved(send_x, ("pair", "core"), 1)
    prior_y = moved(send_y, "lap", 1)
    arrived, prior_x, prior_y = lax.optimization_barrier((arrived, prior_x, prior_y))
    own_grad, power = pl.pallas_call(
        power_kernel,
        out_shape=(struct(2, 128, 128), struct(128, 128)),
        in_specs=[VMEM],
        out_specs=(VMEM, VMEM),
        compiler_params=params(8),
        name="power",
    )(arrived)
    power = lax.all_to_all(power, ("lap", "pair", "core"), 0, 0, tiled=True)
    model = pl.pallas_call(
        functools.partial(model_kernel, float(slab_cells * 2 * pairs)),
        out_shape=struct(2, 128, 128),
        in_specs=[VMEM] * 5,
        out_specs=VMEM,
        compiler_params=params(8),
        name="model",
    )(base, own_grad, power.reshape(16, 8, 128), prior_x, prior_y)
    return (model, dual_next)


def solution(mesh):
    space = mesh.devices.shape[1]
    mesh = Mesh(mesh.devices.reshape(-1, space // 2, 2), ("lap", "pair", "core"))
    both = ("pair", "core")
    in_specs = (
        P(both, None, None),
        P("lap"),
        P(both),
        P("lap", both),
        P(both),
        P("lap", both),
        P(None, both, "lap", None),
    )
    out_specs = (P(both, "lap", None), P(None, both, "lap", None))
    return jax.shard_map(
        on_device, mesh=mesh, in_specs=in_specs, out_specs=out_specs, check_vma=False
    )
```

```python
import functools

import jax
import jax.numpy as jnp
from jax import lax
from jax.experimental import pallas as pl
from jax.experimental.pallas import tpu as pltpu
from jax.sharding import Mesh
from jax.sharding import PartitionSpec as P


HALF = 2
PLANES = 13
KEPT = 9
PAD = 8
ROWS = 1024
LIST = 88
SLAB = ROWS + LIST

dual_step = 0.5
primal_step = 0.2
tv_weight = 0.5

VMEM = pl.BlockSpec(memory_space=pltpu.VMEM)
SMEM = pl.BlockSpec(memory_space=pltpu.SMEM)


def params(mib):
    return pltpu.CompilerParams(vmem_limit_bytes=mib * 2**20)


def spread_points(index, parts, right_planes, write):
    points = index.shape[1]
    column = (index >> 16) * 128 + (index & 127)
    row = ((index >> 7) & 511) - lax.broadcasted_iota(jnp.int32, (8, points), 0) // HALF
    lanes = lax.broadcasted_iota(jnp.int32, (right_planes * 128, points), 0)
    right = jnp.where(lanes == column, 1.0, 0.0).astype(jnp.bfloat16)
    tile = lax.broadcasted_iota(jnp.int32, (ROWS // 8, 8, points), 0)
    mask = row[None] == (8 // HALF) * tile
    for which, part in enumerate(parts):
        total = None
        for piece in part:
            left = jnp.where(mask, piece[None], 0.0).reshape(ROWS, points).astype(jnp.bfloat16)
            got = lax.dot_general(
                left, right, (((1,), (1,)), ((), ())), preferred_element_type=jnp.float32
            )
            total = got if total is None else total + got
        for p in range(right_planes):
            write(which, p, total[:, p * 128 : (p + 1) * 128])


def pieces_of(value, count):
    high = value.astype(jnp.bfloat16).astype(jnp.float32)
    return [high, value - high][:count]


def list_row(ref, base, i):
    block = ref[base + 8 * i : base + 8 * i + 8, :]
    return jnp.concatenate([block[j : j + 1] for j in range(8)], 1)


def either(core, zero, one):
    return lambda i: jnp.where(core == 0, list_row(*zero, i), list_row(*one, i))


def by_parity(even, odd, points):
    parity = lax.broadcasted_iota(jnp.int32, (8, points), 0) % HALF
    return jnp.where(parity == 0, even, odd)


def points_of(core, row, first):
    even = jnp.where(core == 0, row(first), row(first + 2))
    odd = jnp.where(core == 0, row(first + 1), row(first + 3))
    return by_parity(even, odd, even.shape[1])


def writer(stores):
    def write(which, p, value):
        ref, first = stores[which]
        ref[first + p] = value

    return write


def scatter_src(core, row, count, store, first, divisor=None, planes=2):
    amp = points_of(core, row, 2)
    if divisor is not None:
        amp = amp / divisor
    index = row(0).astype(jnp.int32)
    spread_points(index, [pieces_of(amp, count)], planes, writer([(store, first)]))


def scatter_rec(core, row, count, planes, ob, cn, first):
    obs = points_of(core, row, 6)
    parts = [pieces_of(obs, count), [jnp.ones_like(obs)]]
    index = row(1).astype(jnp.int32)
    spread_points(index, parts, planes, writer([(ob, first), (cn, first)]))


def squares(damp):
    core = lax.axis_index("core")
    first, second = damp[HALF * core], damp[HALF * core + 1]
    return first * first, second * second


def diagonal_at(damp, row):
    sigma = row(10)
    first, second = squares(damp)
    return by_parity(6.0 + first * sigma, 6.0 + second * sigma, sigma.shape[1])


def pack_kernel(slow_in, src_in, rec_in, amp_in, obs_in, out, far, src, rec, amp, obs, sem):
    slab = lax.axis_index("pair") * 2 + lax.axis_index("core")
    offset = slab * (2 * 512 * 128)
    pairs = ((src_in, src), (rec_in, rec), (amp_in, amp), (obs_in, obs), (slow_in, out.at[0:ROWS]))
    copies = [pltpu.make_async_copy(x, y, sem.at[k]) for k, (x, y) in enumerate(pairs)]
    for copy in copies:
        copy.start()
    for copy in copies:
        copy.wait()
    points = amp.shape[1]
    far[0:8, :] = (src[...] - offset).astype(jnp.float32)
    far[8:16, :] = (rec[...] - offset).astype(jnp.float32)
    for k, values in ((2, amp), (6, obs)):
        for i in range(4):
            for j in range(8):
                at = 8 * (k + i) + j
                far[at : at + 1, :] = values[i : i + 1, 128 * j : 128 * j + 128]
    index = list_row(far, 0, 0).astype(jnp.int32)
    rows = lax.broadcasted_iota(jnp.int32, (ROWS, points), 0)
    pick = jnp.where(rows == index >> 7, 1.0, 0.0).astype(jnp.bfloat16)
    sigma = out[0:ROWS, :]
    high = sigma.astype(jnp.bfloat16)
    low = (sigma - high.astype(jnp.float32)).astype(jnp.bfloat16)
    dims = (((0,), (0,)), ((), ()))
    got = lax.dot_general(high, pick, dims, preferred_element_type=jnp.float32)
    got = got + lax.dot_general(low, pick, dims, preferred_element_type=jnp.float32)
    lane = lax.broadcasted_iota(jnp.int32, (128, points), 0)
    found = jnp.sum(jnp.where(lane == index & 127, got, 0.0), axis=0, keepdims=True)
    for j in range(8):
        far[80 + j : 81 + j, :] = found[:, 128 * j : 128 * j + 128]
    out[ROWS : ROWS + LIST, :] = far[...]


def scatter_slab(h, row, b, ob, cn):
    core = lax.axis_index("core")
    scatter_src(core, row, 2, b, 2 * h)
    scatter_rec(core, row, 2, 2, ob, cn, 2 * h)


def scatter_own_kernel(lists, b, ob, cn):
    scatter_slab(lax.axis_index("core"), functools.partial(list_row, lists, 0), b, ob, cn)


def scatter_other_kernel(lists, other, b_in, ob_in, cn_in, b, ob, cn, first):
    core = lax.axis_index("core")
    first[...] = jnp.where(core == 0, lists[...], other[ROWS:SLAB, :])
    row = functools.partial(list_row, other, ROWS)
    scatter_slab(1 - lax.axis_index("core"), row, b, ob, cn)


def scatter_near(core, damp, heavy, heavy_low, light, light_low, b):
    scatter_src(core, heavy, 2, b, jnp.where(heavy_low, 2, 4))
    divisor = jnp.where(light_low, diagonal_at(damp, light), 1.0)
    scatter_src(core, light, 1, b, jnp.where(light_low, 0, 6), divisor)


def scatter_mine_kernel(damp, low, high, b, ob, cn):
    core = lax.axis_index("core")
    heavy = either(core, (high, ROWS), (low, ROWS))
    light = either(core, (low, ROWS), (high, ROWS))
    scatter_near(core, damp, heavy, core == 1, light, core == 0, b)
    scatter_rec(core, heavy, 2, 2, ob, cn, jnp.where(core == 1, 0, 2))


def scatter_theirs_kernel(damp, far, near, b_in, b):
    core = lax.axis_index("core")
    low_at, high_at = ROWS, SLAB + ROWS
    heavy = either(core, (near, low_at), (near, high_at))
    light = either(core, (near, high_at), (near, low_at))
    scatter_near(core, damp, heavy, core == 0, light, core == 1, b)
    last = functools.partial(list_row, far, 0)
    scatter_src(core, last, 1, b, 8, diagonal_at(damp, last), 1)


def scatter_late_kernel(high, near, ob_in, cn_in, ob, cn):
    core = lax.axis_index("core")
    low_at, high_at = ROWS, SLAB + ROWS
    heavy = either(core, (near, low_at), (near, high_at))
    scatter_rec(core, heavy, 2, 2, ob, cn, jnp.where(core == 0, 0, 2))
    scatter_rec(core, either(core, (near, high_at), (high, ROWS)), 1, 1, ob, cn, 4)


def shift_matrix():
    i = lax.broadcasted_iota(jnp.int32, (128, 128), 0)
    j = lax.broadcasted_iota(jnp.int32, (128, 128), 1)
    return jnp.where(jnp.abs(i - j) == 1, 1.0, 0.0).astype(jnp.bfloat16)


def neighbours(ref, t):
    ext = ref[t]
    x = ext[PAD : PAD + ROWS]
    total = ROWS + 2 * PAD
    down = pltpu.roll(ext, HALF, 0)[PAD : PAD + ROWS]
    up = pltpu.roll(ext, total - HALF, 0)[PAD : PAD + ROWS]
    high = x.astype(jnp.bfloat16)
    low = (x - high.astype(jnp.float32)).astype(jnp.bfloat16)
    matrix = shift_matrix()
    along = jnp.dot(high, matrix, preferred_element_type=jnp.float32)
    along = along + jnp.dot(low, matrix, preferred_element_type=jnp.float32)
    return x, (down + up) + along


def fold(x):
    return jnp.sum(x.reshape(ROWS // 8, 8, 128), 0)


def walk(first, last, body, carry):
    return lax.fori_loop(first, last, body, carry)


INNER = pl.ds(PAD, 1024)


def advance(src, s_off, inv, i_off, dst, d_off, first, last, dots):
    def body(t, carry):
        x, q = neighbours(src, t - s_off)
        q = q + (src[t - s_off - 1, INNER, :] + src[t - s_off + 1, INNER, :])
        new = inv[t - i_off] * q
        dst[t - d_off, INNER, :] = new
        if not dots:
            return carry
        return carry[0] + fold(x * q), carry[1] + fold(new * q)

    zero = jnp.zeros((8, 128), jnp.float32)
    return walk(first, last, body, (zero, zero) if dots else 0)


def last_moment(src, off):
    def body(t, carry):
        x, q = neighbours(src, t - off)
        q = q + 2.0 * src[t - off + 1, INNER, :]
        return carry + fold(x * q)

    return walk(4, 8, body, jnp.zeros((8, 128), jnp.float32))


def clear_pads(*refs):
    for ref in refs:
        zero = jnp.zeros((8, 128), jnp.float32)
        for t in range(ref.shape[0]):
            ref[t, 0:PAD, :] = zero
            ref[t, ref.shape[1] - PAD :, :] = zero


def message(moments):
    sub = lax.broadcasted_iota(jnp.int32, (8, 128), 0)
    lane = lax.broadcasted_iota(jnp.int32, (8, 128), 1)
    out = jnp.zeros((8, 128), jnp.float32)
    for k, moment in enumerate(moments):
        for c in range(HALF):
            total = jnp.sum(jnp.where(sub % HALF == c, moment, 0.0))
            out = out + jnp.where((sub == k) & (lane == c), total, 0.0)
    return out


def coefficients(moments):
    m = [moments[k : k + 1, :] for k in range(6)]

    def product(p, shift):
        total = 0.0
        for i, a in enumerate(p):
            for j, b in enumerate(p):
                total = total + a * b * (m[i + j] - m[i + j + 1] if shift else m[i + j])
        return total

    one = jnp.ones_like(m[0])
    z, p, energy = [one], [one], m[0]
    x = [0.0 * one] * 3
    for it in range(3):
        stride = energy / product(p, True)
        x = [x[i] + (stride * p[i] if i < len(p) else 0.0) for i in range(3)]
        if it < 2:
            applied = [a - b for a, b in zip(p + [0.0 * one], [0.0 * one] + p)]
            z = [a - stride * b for a, b in zip(z + [0.0 * one], applied)]
            new = product(z, False)
            p = [a + new / energy * b for a, b in zip(z, p + [0.0 * one])]
            energy = new
    lane = lax.broadcasted_iota(jnp.int32, (1, 128), 1)
    sub = lax.broadcasted_iota(jnp.int32, (8, 128), 0)
    out = []
    for v in x:
        value = [jnp.sum(jnp.where(lane == c, v, 0.0)) for c in range(HALF)]
        out.append(jnp.where(sub % HALF == 0, value[0], value[1]))
    return out


def times(pattern, x):
    return (pattern[None] * x.reshape(ROWS // 8, 8, 128)).reshape(ROWS, 128)


def fill_inverse(core, square, inv, slab, mine, theirs, base, valid, first=0):
    def fill(p, _):
        at = pl.multiple_of(p * 512, 512)
        here = mine[pl.ds(at, 512), :]
        there = theirs[pl.ds(pl.multiple_of(base + at, 8), 512), :]
        sigma = jnp.where(core == slab % 2, here, there)
        for c in range(HALF):
            inv[2 * slab + p, pl.ds(c, 512, stride=HALF), :] = valid / (6.0 + square[c] * sigma)
        return 0

    lax.fori_loop(first, 2, fill, 0)


def forward_own_kernel(damp, own_m, own_t, b_own, inv, v0, v1, held):
    core = lax.axis_index("core")
    square = squares(damp)
    clear_pads(v0, v1)
    for slab in (2, 3):
        fill_inverse(core, square, inv, slab, own_m, own_t, 0, 1.0)

    def start(t, carry):
        right = b_own[t - 4]
        new = inv[t] * right
        v0[t, INNER, :] = new
        return carry + fold(new * right)

    held[0:8, :] = walk(4, 8, start, jnp.zeros((8, 128), jnp.float32))
    held[8:16, :], held[16:24, :] = advance(v0, 0, inv, 0, v1, 1, 5, 7, True)


def forward_kernel(
    damp, low_m, high_m, near_t, b_near, held, inv_in, v0_in, v1_in, inv, v0, v1, v2, msg
):
    pair, core = lax.axis_index("pair"), lax.axis_index("core")
    low = jnp.where(pair >= 1, 1.0, 0.0)
    high = jnp.where(pair + 1 < lax.axis_size("pair"), 1.0, 0.0)
    square = squares(damp)
    clear_pads(v2)
    fill_inverse(core, square, inv, 0, low_m, near_t, 0, low, 1)
    fill_inverse(core, square, inv, 1, low_m, near_t, 0, low)
    fill_inverse(core, square, inv, 4, high_m, near_t, SLAB, high)
    fill_inverse(core, square, inv, 5, high_m, near_t, SLAB, high)

    def start(off):
        def body(t, carry):
            v0[t, INNER, :] = inv[t] * b_near[t - off]
            return carry

        return body

    for t, k in ((0, 0), (1, 1), (12, 8)):
        v0[t, INNER, :] = b_near[k]
    walk(2, 4, start(0), 0)
    walk(8, 12, start(4), 0)
    advance(v0, 0, inv, 0, v1, 1, 1, 4, False)
    m1, m2 = advance(v0, 0, inv, 0, v1, 1, 4, 5, True)
    more1, more2 = advance(v0, 0, inv, 0, v1, 1, 7, 8, True)
    advance(v0, 0, inv, 0, v1, 1, 8, 12, False)
    m1 = m1 + more1 + held[8:16, :]
    m2 = m2 + more2 + held[16:24, :]
    advance(v1, 1, inv, 0, v2, 2, 2, 4, False)
    m3, m4 = advance(v1, 1, inv, 0, v2, 2, 4, 8, True)
    advance(v1, 1, inv, 0, v2, 2, 8, 11, False)
    m5 = last_moment(v2, 2)
    msg[...] = message([held[0:8, :], m1, m2, m3, m4, m5])


def adjoint_kernel(
    total, inv, v0, v1, v2, ob_own, cn_own, ob_near, cn_near, wave, u0, u1, u2, msg
):
    a = coefficients(total[...])

    def start(ob, cn, off, own):
        def body(t, carry):
            w = times(a[0], v0[t, INNER, :]) + times(a[1], v1[t - 1, INNER, :])
            w = w + times(a[2], v2[t - 2, INNER, :])
            right = cn[t - off] * w - ob[t - off]
            new = inv[t] * right
            u0[t, INNER, :] = new
            if not own:
                return carry
            wave[t - 4] = w
            return carry + fold(new * right)

        return body

    zero = jnp.zeros((8, 128), jnp.float32)
    walk(2, 4, start(ob_near, cn_near, 2, False), 0)
    m0 = walk(4, 8, start(ob_own, cn_own, 4, True), zero)
    walk(8, 11, start(ob_near, cn_near, 6, False), 0)
    advance(u0, 0, inv, 0, u1, 1, 3, 4, False)
    m1, m2 = advance(u0, 0, inv, 0, u1, 1, 4, 8, True)
    advance(u0, 0, inv, 0, u1, 1, 8, 10, False)
    m3, m4 = advance(u1, 1, inv, 0, u2, 2, 4, 8, True)
    advance(u1, 1, inv, 0, u2, 2, 8, 9, False)
    m5 = last_moment(u2, 2)
    msg[...] = message([m0, m1, m2, m3, m4, m5])


def gradient_kernel(other, damp, total, wave, u0, u1, u2, *rest):
    out, held = rest[-2:]
    a = coefficients(total[...])
    sub = lax.broadcasted_iota(jnp.int32, (8, 128), 0)
    square = jnp.where(sub % HALF == 0, *squares(damp))
    a = [-square * v for v in a]
    core = lax.axis_index("core")
    core = 1 - core if other else core
    for p in range(2):
        t = 4 + 2 * core + p
        x = times(a[0], u0[t, INNER, :]) + times(a[1], u1[t - 1, INNER, :])
        x = x + times(a[2], u2[t - 2, INNER, :])
        held[...] = x * wave[t - 4]
        for band in range(4):
            at = band * 256
            both = held[pl.ds(at, 128, stride=HALF), :] + held[pl.ds(at + 1, 128, stride=HALF), :]
            out[band, p] = both if other else both + rest[0][band, p]


def power_kernel(parts, own, msg):
    g = (parts[0] + parts[1]) + (parts[2] + parts[3])
    own[...] = g
    msg[...] = jnp.full((128, 128), jnp.sum(g * g), jnp.float32)


def variation_kernel(slow, own_t, near_t, dual, dual_next, base, send_x, send_y):
    lap, pair, core = (lax.axis_index(name) for name in ("lap", "pair", "core"))
    start = pl.multiple_of(lap * 128, 128)
    band = pl.ds(start, 128)
    after = pl.ds(pl.multiple_of(jnp.minimum(start + 128, 504), 8), 8)
    row = lax.broadcasted_iota(jnp.int32, (128, 128), 0)
    lane = lax.broadcasted_iota(jnp.int32, (128, 128), 1)
    last_y = (row == 127) & (lap == 3)
    last_z = lane == 127
    comps = []
    for p in range(2):
        here = slow[p, band, :]
        if p == 0:
            step_x = slow[1, band, :] - here
        else:
            beyond = near_t[pl.ds(pl.multiple_of(SLAB + start, 8), 128), :]
            step_x = jnp.where(core == 0, own_t[band, :], beyond) - here
            step_x = jnp.where((core == 1) & (pair == 15), 0.0, step_x)
        rolled = pltpu.roll(here, 127, 0)
        step_y = jnp.where(row == 127, slow[p, after, :][0:1], rolled) - here
        step_y = jnp.where(last_y, 0.0, step_y)
        step_z = jnp.where(last_z, 0.0, pltpu.roll(here, 127, 1) - here)
        trial = [dual[k, p] + dual_step * step for k, step in enumerate((step_x, step_y, step_z))]
        magnitude = jnp.sqrt(trial[0] * trial[0] + trial[1] * trial[1] + trial[2] * trial[2])
        scale = jnp.maximum(1.0, magnitude / tv_weight)
        new = [x / scale for x in trial]
        for k in range(3):
            dual_next[k, p] = new[k]
        if p == 1:
            new[0] = jnp.where((core == 1) & (pair == 15), 0.0, new[0])
        new[1] = jnp.where(last_y, 0.0, new[1])
        new[2] = jnp.where(last_z, 0.0, new[2])
        comps.append(new)
    for p in range(2):
        x, y, z = comps[p]
        back = jnp.where(row == 0, 0.0, pltpu.roll(y, 1, 0)) - y
        back = back + (jnp.where(lane == 0, 0.0, pltpu.roll(z, 1, 1)) - z)
        back = back + (comps[0][0] - x if p == 1 else -x)
        base[p] = slow[p, band, :] - primal_step * back
        send_y[p] = y[120:128]
    send_x[0] = comps[1][0]


def model_kernel(cells, base, grad, power, prior_x, prior_y, model):
    total = power[0]
    for k in range(1, 16):
        total = total + power[k]
    total = jnp.sum(total, axis=0, keepdims=True)
    scale = 1.0 / jnp.sqrt(total / cells + 1e-06)
    row = lax.broadcasted_iota(jnp.int32, (128, 128), 0)
    for p in range(2):
        back = jnp.where(row == 0, prior_y[p][7:8], 0.0)
        if p == 0:
            back = back + prior_x[0]
        model[p] = base[p] - primal_step * (grad[p] * scale + back)


def cost(work):
    return pl.CostEstimate(flops=work * 10**9, bytes_accessed=10**6, transcendentals=0)


def struct(*shape):
    return jax.ShapeDtypeStruct(shape, jnp.float32)


def moved(x, axis, by):
    peers = lax.axis_size(axis)
    return lax.ppermute(x, axis, [(i, i + by) for i in range(peers) if 0 <= i + by < peers])


def swapped(x):
    return lax.ppermute(x, "core", [(0, 1), (1, 0)])


def pair_sum(x):
    for masks in ((1, 2, 3), (4, 8, 12)):
        x = x + sum(lax.ppermute(x, "pair", [(i, i ^ d) for i in range(16)]) for d in masks)
    return x


def scatter(kernel, name, work, inputs, shapes, into=()):
    scalars = 1 if inputs[0].ndim == 1 else 0
    first = len(inputs)
    return pl.pallas_call(
        kernel,
        out_shape=tuple(struct(*shape) for shape in shapes),
        in_specs=[SMEM] * scalars + [VMEM] * (len(inputs) - scalars + len(into)),
        out_specs=(VMEM,) * len(shapes),
        input_output_aliases={first + k: k for k in range(len(into))},
        compiler_params=params(12),
        cost_estimate=cost(work),
        name=name,
    )(*inputs, *into)


def on_device(slowness, damping, src_index, src_amp, rec_index, observed, dual):
    width_x, rows_y, depth_z = slowness.shape
    slab_cells = width_x * rows_y * depth_z
    pairs = lax.axis_size("pair")

    packed, lists = pl.pallas_call(
        pack_kernel,
        out_shape=(struct(SLAB, 128), struct(LIST, 128)),
        in_specs=[pl.BlockSpec(memory_space=pltpu.HBM)] * 5,
        out_specs=(VMEM,) * 2,
        scratch_shapes=[
            pltpu.VMEM((8, 128), jnp.int32), pltpu.VMEM((8, 128), jnp.int32),
            pltpu.VMEM(src_amp.shape, jnp.float32), pltpu.VMEM(observed.shape, jnp.float32),
            pltpu.SemaphoreType.DMA((5,)),
        ],
        compiler_params=params(8),
        name="pack",
    )(
        *(
            pltpu.with_memory_space_constraint(x, pltpu.HBM)
            for x in (
                slowness.reshape(ROWS, 128), src_index.reshape(8, 128), rec_index.reshape(8, 128),
                src_amp, observed,
            )
        )
    )
    low_m, high_m = moved(packed, "pair", 1), moved(packed, "pair", -1)
    own_t = swapped(packed)

    block, near_block = (4, ROWS, 128), (5, ROWS, 128)
    own = scatter(scatter_own_kernel, "scatter_own", 5, (lists,), [block] * 3)
    b_own, ob_own, cn_own, first = scatter(
        scatter_other_kernel, "scatter_other", 5, (lists, own_t), [block] * 3 + [(LIST, 128)], own
    )
    far_m = moved(first, "pair", -2)
    padded = ROWS + 2 * PAD
    inv, v0, v1, held = pl.pallas_call(
        forward_own_kernel,
        out_shape=(
            struct(PLANES, ROWS, 128), struct(13, padded, 128), struct(11, padded, 128),
            struct(24, 128),
        ),
        in_specs=[SMEM] + [VMEM] * 3,
        out_specs=(VMEM,) * 4,
        compiler_params=params(8),
        cost_estimate=cost(4),
        name="forward_own",
    )(damping, slowness.reshape(ROWS, 128), own_t, b_own)
    low_m, high_m, far_m, held = lax.optimization_barrier((low_m, high_m, far_m, held))
    near_t = swapped(jnp.concatenate([low_m, high_m]))
    b_near, ob_near, cn_near = scatter(
        scatter_mine_kernel, "scatter_mine", 6, (damping, low_m, high_m),
        [(9, ROWS, 128), near_block, near_block],
    )
    near_t, b_near = lax.optimization_barrier((near_t, b_near))
    b_near, = scatter(
        scatter_theirs_kernel, "scatter_theirs", 5, (damping, far_m, near_t), [(9, ROWS, 128)],
        (b_near,),
    )

    inv, v0, v1, v2, msg = pl.pallas_call(
        forward_kernel,
        out_shape=(
            struct(PLANES, ROWS, 128), struct(13, padded, 128), struct(11, padded, 128),
            struct(9, padded, 128), struct(8, 128),
        ),
        in_specs=[SMEM] + [VMEM] * 8,
        out_specs=(VMEM,) * 5,
        input_output_aliases={6: 0, 7: 1, 8: 2},
        compiler_params=params(8),
        cost_estimate=cost(20),
        name="forward",
    )(damping, low_m, high_m, near_t, b_near, held, inv, v0, v1)

    near_t, msg = lax.optimization_barrier((near_t, msg))
    ob_near, cn_near = scatter(
        scatter_late_kernel, "scatter_late", 5, (high_m, near_t), [near_block] * 2,
        (ob_near, cn_near),
    )
    wave, u0, u1, u2, msg = pl.pallas_call(
        adjoint_kernel,
        out_shape=(
            struct(4, ROWS, 128), struct(13, padded, 128), struct(11, padded, 128),
            struct(9, padded, 128), struct(8, 128),
        ),
        in_specs=[VMEM] * 9,
        out_specs=(VMEM,) * 5,
        input_output_aliases={2: 1, 3: 2, 4: 3},
        compiler_params=params(8),
        cost_estimate=cost(14),
        name="adjoint",
    )(pair_sum(msg), inv, v0, v1, v2, ob_own, cn_own, ob_near, cn_near)

    total = pair_sum(msg)

    def gradient(other, *more):
        return pl.pallas_call(
            functools.partial(gradient_kernel, other),
            out_shape=struct(4, 2, 128, 128),
            in_specs=[SMEM] + [VMEM] * (5 + len(more)),
            out_specs=VMEM,
            scratch_shapes=[pltpu.VMEM((ROWS, 128), jnp.float32)],
            compiler_params=params(8),
            name="gradient",
        )(damping, total, wave, u0, u1, u2, *more)

    parts = gradient(False, swapped(gradient(True)))
    slowness, dual, own_t, near_t, parts = lax.optimization_barrier(
        (slowness, dual, own_t, near_t, parts)
    )
    arrived = lax.all_to_all(parts, "lap", 0, 0, tiled=True)
    dual_next, base, send_x, send_y = pl.pallas_call(
        variation_kernel,
        out_shape=(
            struct(3, 2, 128, 128), struct(2, 128, 128), struct(1, 128, 128), struct(2, 8, 128),
        ),
        in_specs=[VMEM] * 4,
        out_specs=(VMEM,) * 4,
        compiler_params=params(8),
        cost_estimate=cost(1),
        name="variation",
    )(slowness, own_t, near_t, dual)
    prior_x = moved(send_x, ("pair", "core"), 1)
    prior_y = moved(send_y, "lap", 1)
    arrived, prior_x, prior_y = lax.optimization_barrier((arrived, prior_x, prior_y))
    own_grad, power = pl.pallas_call(
        power_kernel,
        out_shape=(struct(2, 128, 128), struct(128, 128)),
        in_specs=[VMEM],
        out_specs=(VMEM, VMEM),
        compiler_params=params(8),
        name="power",
    )(arrived)
    power = lax.all_to_all(power, ("lap", "pair", "core"), 0, 0, tiled=True)
    model = pl.pallas_call(
        functools.partial(model_kernel, float(slab_cells * 2 * pairs)),
        out_shape=struct(2, 128, 128),
        in_specs=[VMEM] * 5,
        out_specs=VMEM,
        compiler_params=params(8),
        name="model",
    )(base, own_grad, power.reshape(16, 8, 128), prior_x, prior_y)
    return (model, dual_next)


def solution(mesh):
    space = mesh.devices.shape[1]
    mesh = Mesh(mesh.devices.reshape(-1, space // 2, 2), ("lap", "pair", "core"))
    both = ("pair", "core")
    in_specs = (
        P(both, None, None),
        P("lap"),
        P(both),
        P("lap", both),
        P(both),
        P("lap", both),
        P(None, both, "lap", None),
    )
    out_specs = (P(both, "lap", None), P(None, both, "lap", None))
    return jax.shard_map(
        on_device, mesh=mesh, in_specs=in_specs, out_specs=out_specs, check_vma=False
    )
```

```python
import functools

import jax
import jax.numpy as jnp
from jax import lax
from jax.experimental import pallas as pl
from jax.experimental.pallas import tpu as pltpu
from jax.sharding import Mesh
from jax.sharding import PartitionSpec as P


HALF = 2
PLANES = 13
KEPT = 9
PAD = 8
ROWS = 1024
LIST = 88
SLAB = ROWS + LIST

dual_step = 0.5
primal_step = 0.2
tv_weight = 0.5

VMEM = pl.BlockSpec(memory_space=pltpu.VMEM)
SMEM = pl.BlockSpec(memory_space=pltpu.SMEM)


def params(mib):
    return pltpu.CompilerParams(vmem_limit_bytes=mib * 2**20)


def spread_points(index, parts, right_planes, write):
    points = index.shape[1]
    column = (index >> 16) * 128 + (index & 127)
    row = (index >> 7) & 511
    rows = ROWS
    if right_planes == 1:
        rows = ROWS // 2
        column = jnp.where(index >> 16 == 0, (row >> 8) * 128 + (index & 127), -1)
        row = row & 255
    row = row - lax.broadcasted_iota(jnp.int32, (8, points), 0) // HALF
    lanes = lax.broadcasted_iota(jnp.int32, (256, points), 0)
    right = jnp.where(lanes == column, 1.0, 0.0).astype(jnp.bfloat16)
    tile = lax.broadcasted_iota(jnp.int32, (rows // 8, 8, points), 0)
    mask = row[None] == (8 // HALF) * tile
    for which, part in enumerate(parts):
        total = None
        for piece in part:
            left = jnp.where(mask, piece[None], 0.0).reshape(rows, points).astype(jnp.bfloat16)
            got = lax.dot_general(
                left, right, (((1,), (1,)), ((), ())), preferred_element_type=jnp.float32
            )
            total = got if total is None else total + got
        lower, upper = total[:, 0:128], total[:, 128:256]
        if right_planes == 1:
            write(which, 0, jnp.concatenate([lower, upper]))
        else:
            write(which, 0, lower)
            write(which, 1, upper)


def pieces_of(value, count):
    high = value.astype(jnp.bfloat16).astype(jnp.float32)
    return [high, value - high][:count]


def list_row(ref, base, i):
    block = ref[base + 8 * i : base + 8 * i + 8, :]
    return jnp.concatenate([block[j : j + 1] for j in range(8)], 1)


def either(core, zero, one):
    return lambda i: jnp.where(core == 0, list_row(*zero, i), list_row(*one, i))


def by_parity(even, odd, points):
    parity = lax.broadcasted_iota(jnp.int32, (8, points), 0) % HALF
    return jnp.where(parity == 0, even, odd)


def points_of(core, row, first):
    even = jnp.where(core == 0, row(first), row(first + 2))
    odd = jnp.where(core == 0, row(first + 1), row(first + 3))
    return by_parity(even, odd, even.shape[1])


def writer(stores):
    def write(which, p, value):
        ref, first = stores[which]
        ref[first + p] = value

    return write


def scatter_src(core, row, count, store, first, divisor=None, planes=2):
    amp = points_of(core, row, 2)
    if divisor is not None:
        amp = amp / divisor
    index = row(0).astype(jnp.int32)
    spread_points(index, [pieces_of(amp, count)], planes, writer([(store, first)]))


def scatter_rec(core, row, count, planes, ob, cn, first):
    obs = points_of(core, row, 6)
    parts = [pieces_of(obs, count), [jnp.ones_like(obs)]]
    index = row(1).astype(jnp.int32)
    spread_points(index, parts, planes, writer([(ob, first), (cn, first)]))


def squares(damp):
    core = lax.axis_index("core")
    first, second = damp[HALF * core], damp[HALF * core + 1]
    return first * first, second * second


def diagonal_at(damp, row):
    sigma = row(10)
    first, second = squares(damp)
    return by_parity(6.0 + first * sigma, 6.0 + second * sigma, sigma.shape[1])


def pack_kernel(slow_in, src_in, rec_in, amp_in, obs_in, out, far, src, rec, amp, obs, sem):
    slab = lax.axis_index("pair") * 2 + lax.axis_index("core")
    offset = slab * (2 * 512 * 128)
    pairs = ((src_in, src), (rec_in, rec), (amp_in, amp), (obs_in, obs), (slow_in, out.at[0:ROWS]))
    copies = [pltpu.make_async_copy(x, y, sem.at[k]) for k, (x, y) in enumerate(pairs)]
    for copy in copies[::-1]:
        copy.start()
    for copy in copies[:4]:
        copy.wait()
    far[80:88, :] = jnp.zeros((8, 128), jnp.float32)
    points = amp.shape[1]
    far[0:8, :] = (src[...] - offset).astype(jnp.float32)
    far[8:16, :] = (rec[...] - offset).astype(jnp.float32)
    for k, values in ((2, amp), (6, obs)):
        for i in range(4):
            for j in range(8):
                at = 8 * (k + i) + j
                far[at : at + 1, :] = values[i : i + 1, 128 * j : 128 * j + 128]
    out[ROWS : ROWS + LIST, :] = far[...]
    for copy in copies[4:]:
        copy.wait()


def gather_sigma(sigma, row, store):
    index = row(0).astype(jnp.int32)
    points = index.shape[1]
    rows = lax.broadcasted_iota(jnp.int32, (ROWS, points), 0)
    pick = jnp.where(rows == index >> 7, 1.0, 0.0).astype(jnp.bfloat16)
    high = sigma.astype(jnp.bfloat16)
    low = (sigma - high.astype(jnp.float32)).astype(jnp.bfloat16)
    dims = (((0,), (0,)), ((), ()))
    got = lax.dot_general(high, pick, dims, preferred_element_type=jnp.float32)
    got = got + lax.dot_general(low, pick, dims, preferred_element_type=jnp.float32)
    lane = lax.broadcasted_iota(jnp.int32, (128, points), 0)
    found = jnp.sum(jnp.where(lane == index & 127, got, 0.0), axis=0, keepdims=True)
    for j in range(8):
        store[80 + j : 81 + j, :] = found[:, 128 * j : 128 * j + 128]


def scatter_slab(h, row, b, ob, cn):
    core = lax.axis_index("core")
    scatter_src(core, row, 2, b, 2 * h)
    scatter_rec(core, row, 2, 2, ob, cn, 2 * h)


def scatter_own_kernel(lists, b, ob, cn):
    scatter_slab(lax.axis_index("core"), functools.partial(list_row, lists, 0), b, ob, cn)


def scatter_other_kernel(mine, other, b_in, ob_in, cn_in, b, ob, cn, first):
    core = lax.axis_index("core")
    whole = jnp.where(core == 0, mine[...], other[...])
    first[...] = whole[ROWS:SLAB]
    gather_sigma(whole[0:ROWS], functools.partial(list_row, first, 0), first)
    row = functools.partial(list_row, other, ROWS)
    scatter_slab(1 - lax.axis_index("core"), row, b, ob, cn)


def scatter_near(core, heavy, heavy_low, light, light_low, b):
    scatter_src(core, heavy, 2, b, jnp.where(heavy_low, 2, 4))
    scatter_src(core, light, 1, b, jnp.where(light_low, 0, 6))


def scatter_mine_kernel(low, high, b, ob, cn):
    core = lax.axis_index("core")
    heavy = either(core, (high, ROWS), (low, ROWS))
    light = either(core, (low, ROWS), (high, ROWS))
    scatter_near(core, heavy, core == 1, light, core == 0, b)
    scatter_rec(core, heavy, 2, 2, ob, cn, jnp.where(core == 1, 0, 2))


def scatter_theirs_kernel(damp, far, near, b_in, b):
    core = lax.axis_index("core")
    low_at, high_at = ROWS, SLAB + ROWS
    heavy = either(core, (near, low_at), (near, high_at))
    light = either(core, (near, high_at), (near, low_at))
    scatter_near(core, heavy, core == 0, light, core == 1, b)
    last = functools.partial(list_row, far, 0)
    scatter_src(core, last, 1, b, 8, diagonal_at(damp, last), 1)


def scatter_late_kernel(high, near, ob_in, cn_in, ob, cn):
    core = lax.axis_index("core")
    low_at, high_at = ROWS, SLAB + ROWS
    heavy = either(core, (near, low_at), (near, high_at))
    scatter_rec(core, heavy, 2, 2, ob, cn, jnp.where(core == 0, 0, 2))
    scatter_rec(core, either(core, (near, high_at), (high, ROWS)), 1, 1, ob, cn, 4)


def shift_matrix():
    i = lax.broadcasted_iota(jnp.int32, (128, 128), 0)
    j = lax.broadcasted_iota(jnp.int32, (128, 128), 1)
    return jnp.where(jnp.abs(i - j) == 1, 1.0, 0.0).astype(jnp.bfloat16)


def neighbours(ref, t):
    ext = ref[t]
    x = ext[PAD : PAD + ROWS]
    total = ROWS + 2 * PAD
    down = pltpu.roll(ext, HALF, 0)[PAD : PAD + ROWS]
    up = pltpu.roll(ext, total - HALF, 0)[PAD : PAD + ROWS]
    high = x.astype(jnp.bfloat16)
    low = (x - high.astype(jnp.float32)).astype(jnp.bfloat16)
    matrix = shift_matrix()
    along = jnp.dot(high, matrix, preferred_element_type=jnp.float32)
    along = along + jnp.dot(low, matrix, preferred_element_type=jnp.float32)
    return x, (down + up) + along


def fold(x):
    return jnp.sum(x.reshape(ROWS // 8, 8, 128), 0)


def walk(first, last, body, carry):
    return lax.fori_loop(first, last, body, carry)


INNER = pl.ds(PAD, 1024)


def advance(src, s_off, inv, i_off, dst, d_off, first, last, dots):
    def body(t, carry):
        x, q = neighbours(src, t - s_off)
        q = q + (src[t - s_off - 1, INNER, :] + src[t - s_off + 1, INNER, :])
        new = inv[t - i_off] * q
        dst[t - d_off, INNER, :] = new
        if not dots:
            return carry
        return carry[0] + fold(x * q), carry[1] + fold(new * q)

    zero = jnp.zeros((8, 128), jnp.float32)
    return walk(first, last, body, (zero, zero) if dots else 0)


def last_moment(src, off):
    def body(t, carry):
        x, q = neighbours(src, t - off)
        q = q + 2.0 * src[t - off + 1, INNER, :]
        return carry + fold(x * q)

    return walk(4, 8, body, jnp.zeros((8, 128), jnp.float32))


def clear_pads(*refs):
    for ref in refs:
        zero = jnp.zeros((8, 128), jnp.float32)
        for t in range(ref.shape[0]):
            ref[t, 0:PAD, :] = zero
            ref[t, ref.shape[1] - PAD :, :] = zero


def message(moments):
    sub = lax.broadcasted_iota(jnp.int32, (8, 128), 0)
    lane = lax.broadcasted_iota(jnp.int32, (8, 128), 1)
    out = jnp.zeros((8, 128), jnp.float32)
    for k, moment in enumerate(moments):
        for c in range(HALF):
            total = jnp.sum(jnp.where(sub % HALF == c, moment, 0.0))
            out = out + jnp.where((sub == k) & (lane == c), total, 0.0)
    return out


def coefficients(terms):
    moments = (terms[0][...] + terms[1][...]) + (terms[2][...] + terms[3][...])
    m = [moments[k : k + 1, :] for k in range(6)]

    def product(p, shift):
        total = 0.0
        for i, a in enumerate(p):
            for j, b in enumerate(p):
                total = total + a * b * (m[i + j] - m[i + j + 1] if shift else m[i + j])
        return total

    one = jnp.ones_like(m[0])
    z, p, energy = [one], [one], m[0]
    x = [0.0 * one] * 3
    for it in range(3):
        stride = energy / product(p, True)
        x = [x[i] + (stride * p[i] if i < len(p) else 0.0) for i in range(3)]
        if it < 2:
            applied = [a - b for a, b in zip(p + [0.0 * one], [0.0 * one] + p)]
            z = [a - stride * b for a, b in zip(z + [0.0 * one], applied)]
            new = product(z, False)
            p = [a + new / energy * b for a, b in zip(z, p + [0.0 * one])]
            energy = new
    lane = lax.broadcasted_iota(jnp.int32, (1, 128), 1)
    sub = lax.broadcasted_iota(jnp.int32, (8, 128), 0)
    out = []
    for v in x:
        value = [jnp.sum(jnp.where(lane == c, v, 0.0)) for c in range(HALF)]
        out.append(jnp.where(sub % HALF == 0, value[0], value[1]))
    return out


def times(pattern, x):
    return (pattern[None] * x.reshape(ROWS // 8, 8, 128)).reshape(ROWS, 128)


def fill_inverse(core, square, inv, slab, mine, theirs, base, valid):
    def fill(p, _):
        at = pl.multiple_of(p * 512, 512)
        here = mine[pl.ds(at, 512), :]
        there = theirs[pl.ds(pl.multiple_of(base + at, 8), 512), :]
        sigma = jnp.where(core == slab % 2, here, there)
        for c in range(HALF):
            inv[2 * slab + p, pl.ds(c, 512, stride=HALF), :] = valid / (6.0 + square[c] * sigma)
        return 0

    lax.fori_loop(0, 2, fill, 0)


def forward_own_kernel(damp, own_m, own_t, b_own, inv, v0, v1, held):
    core = lax.axis_index("core")
    square = squares(damp)
    clear_pads(v0, v1)
    for slab in (2, 3):
        fill_inverse(core, square, inv, slab, own_m, own_t, 0, 1.0)

    def start(t, carry):
        right = b_own[t - 4]
        new = inv[t] * right
        v0[t, INNER, :] = new
        return carry + fold(new * right)

    held[0:8, :] = walk(4, 8, start, jnp.zeros((8, 128), jnp.float32))
    held[8:16, :], held[16:24, :] = advance(v0, 0, inv, 0, v1, 1, 5, 7, True)


def forward_kernel(
    damp, low_m, high_m, near_t, b_near, held, inv_in, v0_in, v1_in, inv, v0, v1, v2, msg
):
    pair, core = lax.axis_index("pair"), lax.axis_index("core")
    low = jnp.where(pair >= 1, 1.0, 0.0)
    high = jnp.where(pair + 1 < lax.axis_size("pair"), 1.0, 0.0)
    square = squares(damp)
    clear_pads(v2)
    fill_inverse(core, square, inv, 0, low_m, near_t, 0, low)
    fill_inverse(core, square, inv, 1, low_m, near_t, 0, low)
    fill_inverse(core, square, inv, 4, high_m, near_t, SLAB, high)
    fill_inverse(core, square, inv, 5, high_m, near_t, SLAB, high)

    def start(off):
        def body(t, carry):
            v0[t, INNER, :] = inv[t] * b_near[t - off]
            return carry

        return body

    v0[12, INNER, :] = b_near[8]
    walk(0, 4, start(0), 0)
    walk(8, 12, start(4), 0)
    advance(v0, 0, inv, 0, v1, 1, 1, 4, False)
    m1, m2 = advance(v0, 0, inv, 0, v1, 1, 4, 5, True)
    more1, more2 = advance(v0, 0, inv, 0, v1, 1, 7, 8, True)
    advance(v0, 0, inv, 0, v1, 1, 8, 12, False)
    m1 = m1 + more1 + held[8:16, :]
    m2 = m2 + more2 + held[16:24, :]
    advance(v1, 1, inv, 0, v2, 2, 2, 4, False)
    m3, m4 = advance(v1, 1, inv, 0, v2, 2, 4, 8, True)
    advance(v1, 1, inv, 0, v2, 2, 8, 11, False)
    m5 = last_moment(v2, 2)
    msg[...] = message([held[0:8, :], m1, m2, m3, m4, m5])


def adjoint_kernel(
    t0, t1, t2, t3, inv, v0, v1, v2, ob_own, cn_own, ob_near, cn_near, wave, u0, u1, u2, msg
):
    a = coefficients((t0, t1, t2, t3))

    def start(ob, cn, off, own):
        def body(t, carry):
            w = times(a[0], v0[t, INNER, :]) + times(a[1], v1[t - 1, INNER, :])
            w = w + times(a[2], v2[t - 2, INNER, :])
            right = cn[t - off] * w - ob[t - off]
            new = inv[t] * right
            u0[t, INNER, :] = new
            if not own:
                return carry
            wave[t - 4] = w
            return carry + fold(new * right)

        return body

    zero = jnp.zeros((8, 128), jnp.float32)
    walk(2, 4, start(ob_near, cn_near, 2, False), 0)
    m0 = walk(4, 8, start(ob_own, cn_own, 4, True), zero)
    walk(8, 11, start(ob_near, cn_near, 6, False), 0)
    advance(u0, 0, inv, 0, u1, 1, 3, 4, False)
    m1, m2 = advance(u0, 0, inv, 0, u1, 1, 4, 8, True)
    advance(u0, 0, inv, 0, u1, 1, 8, 10, False)
    m3, m4 = advance(u1, 1, inv, 0, u2, 2, 4, 8, True)
    advance(u1, 1, inv, 0, u2, 2, 8, 9, False)
    m5 = last_moment(u2, 2)
    msg[...] = message([m0, m1, m2, m3, m4, m5])


def gradient_kernel(other, damp, t0, t1, t2, t3, wave, u0, u1, u2, *rest):
    held = rest[-1]
    a = coefficients((t0, t1, t2, t3))
    sub = lax.broadcasted_iota(jnp.int32, (8, 128), 0)
    square = jnp.where(sub % HALF == 0, *squares(damp))
    a = [-square * v for v in a]
    core = lax.axis_index("core")
    core = 1 - core if other else core
    bands = rest[0] if other else rest[-2]
    for p in range(2):
        t = 4 + 2 * core + p
        x = times(a[0], u0[t, INNER, :]) + times(a[1], u1[t - 1, INNER, :])
        x = x + times(a[2], u2[t - 2, INNER, :])
        held[...] = x * wave[t - 4]
        for band in range(4):
            at = band * 256
            both = held[pl.ds(at, 128, stride=HALF), :] + held[pl.ds(at + 1, 128, stride=HALF), :]
            bands[band, p] = both if other else both + rest[0][band, p]
    if not other:
        lap = lax.axis_index("lap")
        for d in range(4):
            rest[1 + d][...] = bands[lap ^ d]


def power_kernel(g0, g1, g2, g3, own, msg):
    g = (g0[...] + g1[...]) + (g2[...] + g3[...])
    own[...] = g
    msg[...] = jnp.full((128, 128), jnp.sum(g * g), jnp.float32)


def variation_kernel(slow, own_t, near_t, dual, dual_next, base, send_x, send_y):
    lap, pair, core = (lax.axis_index(name) for name in ("lap", "pair", "core"))
    start = pl.multiple_of(lap * 128, 128)
    band = pl.ds(start, 128)
    after = pl.ds(pl.multiple_of(jnp.minimum(start + 128, 504), 8), 8)
    row = lax.broadcasted_iota(jnp.int32, (128, 128), 0)
    lane = lax.broadcasted_iota(jnp.int32, (128, 128), 1)
    last_y = (row == 127) & (lap == 3)
    last_z = lane == 127
    comps = []
    for p in range(2):
        here = slow[p, band, :]
        if p == 0:
            step_x = slow[1, band, :] - here
        else:
            beyond = near_t[pl.ds(pl.multiple_of(SLAB + start, 8), 128), :]
            step_x = jnp.where(core == 0, own_t[band, :], beyond) - here
            step_x = jnp.where((core == 1) & (pair == 15), 0.0, step_x)
        rolled = pltpu.roll(here, 127, 0)
        step_y = jnp.where(row == 127, slow[p, after, :][0:1], rolled) - here
        step_y = jnp.where(last_y, 0.0, step_y)
        step_z = jnp.where(last_z, 0.0, pltpu.roll(here, 127, 1) - here)
        trial = [dual[k, p] + dual_step * step for k, step in enumerate((step_x, step_y, step_z))]
        magnitude = jnp.sqrt(trial[0] * trial[0] + trial[1] * trial[1] + trial[2] * trial[2])
        scale = jnp.maximum(1.0, magnitude / tv_weight)
        new = [x / scale for x in trial]
        for k in range(3):
            dual_next[k, p] = new[k]
        if p == 1:
            new[0] = jnp.where((core == 1) & (pair == 15), 0.0, new[0])
        new[1] = jnp.where(last_y, 0.0, new[1])
        new[2] = jnp.where(last_z, 0.0, new[2])
        comps.append(new)
    for p in range(2):
        x, y, z = comps[p]
        back = jnp.where(row == 0, 0.0, pltpu.roll(y, 1, 0)) - y
        back = back + (jnp.where(lane == 0, 0.0, pltpu.roll(z, 1, 1)) - z)
        back = back + (comps[0][0] - x if p == 1 else -x)
        base[p] = slow[p, band, :] - primal_step * back
        send_y[p] = y[120:128]
    send_x[0] = comps[1][0]


def model_kernel(cells, base, grad, power, prior_x, prior_y, model):
    total = power[0]
    for k in range(1, 16):
        total = total + power[k]
    total = jnp.sum(total, axis=0, keepdims=True)
    scale = 1.0 / jnp.sqrt(total / cells + 1e-06)
    row = lax.broadcasted_iota(jnp.int32, (128, 128), 0)
    for p in range(2):
        back = jnp.where(row == 0, prior_y[p][7:8], 0.0)
        if p == 0:
            back = back + prior_x[0]
        model[p] = base[p] - primal_step * (grad[p] * scale + back)


def cost(work):
    return pl.CostEstimate(flops=work * 10**9, bytes_accessed=10**6, transcendentals=0)


def struct(*shape):
    return jax.ShapeDtypeStruct(shape, jnp.float32)


def moved(x, axis, by):
    peers = lax.axis_size(axis)
    return lax.ppermute(x, axis, [(i, i + by) for i in range(peers) if 0 <= i + by < peers])


def swapped(x):
    return lax.ppermute(x, "core", [(0, 1), (1, 0)])


def pair_sum(x):
    def others(x, masks):
        return [lax.ppermute(x, "pair", [(i, i ^ d) for i in range(16)]) for d in masks]

    x = x + sum(others(x, (1, 2, 3)))
    return [x] + others(x, (4, 8, 12))


def scatter(kernel, name, work, inputs, shapes, into=()):
    scalars = 1 if inputs[0].ndim == 1 else 0
    first = len(inputs)
    return pl.pallas_call(
        kernel,
        out_shape=tuple(struct(*shape) for shape in shapes),
        in_specs=[SMEM] * scalars + [VMEM] * (len(inputs) - scalars + len(into)),
        out_specs=(VMEM,) * len(shapes),
        input_output_aliases={first + k: k for k in range(len(into))},
        compiler_params=params(8),
        cost_estimate=cost(work),
        name=name,
    )(*inputs, *into)


def on_device(slowness, damping, src_index, src_amp, rec_index, observed, dual):
    width_x, rows_y, depth_z = slowness.shape
    slab_cells = width_x * rows_y * depth_z
    pairs = lax.axis_size("pair")

    packed, lists = pl.pallas_call(
        pack_kernel,
        out_shape=(struct(SLAB, 128), struct(LIST, 128)),
        in_specs=[pl.BlockSpec(memory_space=pltpu.HBM)] * 5,
        out_specs=(VMEM,) * 2,
        scratch_shapes=[
            pltpu.VMEM((8, 128), jnp.int32), pltpu.VMEM((8, 128), jnp.int32),
            pltpu.VMEM(src_amp.shape, jnp.float32), pltpu.VMEM(observed.shape, jnp.float32),
            pltpu.SemaphoreType.DMA((5,)),
        ],
        compiler_params=params(8),
        name="pack",
    )(
        *(
            pltpu.with_memory_space_constraint(x, pltpu.HBM)
            for x in (
                slowness.reshape(ROWS, 128), src_index.reshape(8, 128), rec_index.reshape(8, 128),
                src_amp, observed,
            )
        )
    )
    low_m, high_m = moved(packed, "pair", 1), moved(packed, "pair", -1)
    own_t = swapped(packed)

    block, near_block = (4, ROWS, 128), (5, ROWS, 128)
    own = scatter(scatter_own_kernel, "scatter_own", 5, (lists,), [block] * 3)
    b_own, ob_own, cn_own, first = scatter(
        scatter_other_kernel, "scatter_other", 5, (packed, own_t), [block] * 3 + [(LIST, 128)], own
    )
    far_m = moved(first, "pair", -2)
    padded = ROWS + 2 * PAD
    inv, v0, v1, held = pl.pallas_call(
        forward_own_kernel,
        out_shape=(
            struct(PLANES, ROWS, 128), struct(13, padded, 128), struct(11, padded, 128),
            struct(24, 128),
        ),
        in_specs=[SMEM] + [VMEM] * 3,
        out_specs=(VMEM,) * 4,
        compiler_params=params(2),
        cost_estimate=cost(4),
        name="forward_own",
    )(damping, slowness.reshape(ROWS, 128), own_t, b_own)
    low_m, high_m, far_m, held = lax.optimization_barrier((low_m, high_m, far_m, held))
    near_t = swapped(jnp.concatenate([low_m, high_m]))
    b_near, ob_near, cn_near = scatter(
        scatter_mine_kernel, "scatter_mine", 6, (low_m, high_m),
        [(9, ROWS, 128), near_block, near_block],
    )
    near_t, b_near = lax.optimization_barrier((near_t, b_near))
    b_near, = scatter(
        scatter_theirs_kernel, "scatter_theirs", 5, (damping, far_m, near_t), [(9, ROWS, 128)],
        (b_near,),
    )

    inv, v0, v1, v2, msg = pl.pallas_call(
        forward_kernel,
        out_shape=(
            struct(PLANES, ROWS, 128), struct(13, padded, 128), struct(11, padded, 128),
            struct(9, padded, 128), struct(8, 128),
        ),
        in_specs=[SMEM] + [VMEM] * 8,
        out_specs=(VMEM,) * 5,
        input_output_aliases={6: 0, 7: 1, 8: 2},
        compiler_params=params(2),
        cost_estimate=cost(20),
        name="forward",
    )(damping, low_m, high_m, near_t, b_near, held, inv, v0, v1)

    near_t, msg = lax.optimization_barrier((near_t, msg))
    ob_near, cn_near = scatter(
        scatter_late_kernel, "scatter_late", 5, (high_m, near_t), [near_block] * 2,
        (ob_near, cn_near),
    )
    wave, u0, u1, u2, msg = pl.pallas_call(
        adjoint_kernel,
        out_shape=(
            struct(4, ROWS, 128), struct(13, padded, 128), struct(11, padded, 128),
            struct(9, padded, 128), struct(8, 128),
        ),
        in_specs=[VMEM] * 12,
        out_specs=(VMEM,) * 5,
        input_output_aliases={5: 1, 6: 2, 7: 3},
        compiler_params=params(2),
        cost_estimate=cost(14),
        name="adjoint",
    )(*pair_sum(msg), inv, v0, v1, v2, ob_own, cn_own, ob_near, cn_near)

    terms = pair_sum(msg)

    def gradient(other, *more):
        bands = (4, 2, 128, 128)
        scratch = [] if other else [pltpu.VMEM(bands, jnp.float32)]
        return pl.pallas_call(
            functools.partial(gradient_kernel, other),
            out_shape=struct(*bands) if other else (struct(*bands[1:]),) * 4,
            in_specs=[SMEM] + [VMEM] * (8 + len(more)),
            out_specs=VMEM if other else (VMEM,) * 4,
            scratch_shapes=scratch + [pltpu.VMEM((ROWS, 128), jnp.float32)],
            compiler_params=params(8),
            name="gradient",
        )(damping, *terms, wave, u0, u1, u2, *more)

    bands = gradient(False, swapped(gradient(True)))
    slowness, dual, own_t, near_t, bands = lax.optimization_barrier(
        (slowness, dual, own_t, near_t, bands)
    )
    arrived = [bands[0]] + [
        lax.ppermute(bands[d], "lap", [(i, i ^ d) for i in range(4)]) for d in (1, 2, 3)
    ]
    dual_next, base, send_x, send_y = pl.pallas_call(
        variation_kernel,
        out_shape=(
            struct(3, 2, 128, 128), struct(2, 128, 128), struct(1, 128, 128), struct(2, 8, 128),
        ),
        in_specs=[VMEM] * 4,
        out_specs=(VMEM,) * 4,
        compiler_params=params(8),
        cost_estimate=cost(1),
        name="variation",
    )(slowness, own_t, near_t, dual)
    prior_x = moved(send_x, ("pair", "core"), 1)
    prior_y = moved(send_y, "lap", 1)
    arrived, prior_x, prior_y = lax.optimization_barrier((arrived, prior_x, prior_y))
    own_grad, power = pl.pallas_call(
        power_kernel,
        out_shape=(struct(2, 128, 128), struct(128, 128)),
        in_specs=[VMEM] * 4,
        out_specs=(VMEM, VMEM),
        compiler_params=params(8),
        name="power",
    )(*arrived)
    power = lax.all_to_all(power, ("lap", "pair", "core"), 0, 0, tiled=True)
    model = pl.pallas_call(
        functools.partial(model_kernel, float(slab_cells * 2 * pairs)),
        out_shape=struct(2, 128, 128),
        in_specs=[VMEM] * 5,
        out_specs=VMEM,
        compiler_params=params(8),
        name="model",
    )(base, own_grad, power.reshape(16, 8, 128), prior_x, prior_y)
    return (model, dual_next)


def solution(mesh):
    space = mesh.devices.shape[1]
    mesh = Mesh(mesh.devices.reshape(-1, space // 2, 2), ("lap", "pair", "core"))
    both = ("pair", "core")
    in_specs = (
        P(both, None, None),
        P("lap"),
        P(both),
        P("lap", both),
        P(both),
        P("lap", both),
        P(None, both, "lap", None),
    )
    out_specs = (P(both, "lap", None), P(None, both, "lap", None))
    return jax.shard_map(
        on_device, mesh=mesh, in_specs=in_specs, out_specs=out_specs, check_vma=False
    )
```

```python
import functools

import jax
import jax.numpy as jnp
from jax import lax
from jax.experimental import pallas as pl
from jax.experimental.pallas import tpu as pltpu
from jax.sharding import Mesh
from jax.sharding import PartitionSpec as P


HALF = 2
PLANES = 13
KEPT = 9
PAD = 8
ROWS = 1024
LIST = 88
SLAB = ROWS + LIST

dual_step = 0.5
primal_step = 0.2
tv_weight = 0.5

VMEM = pl.BlockSpec(memory_space=pltpu.VMEM)
SMEM = pl.BlockSpec(memory_space=pltpu.SMEM)


def params(mib):
    return pltpu.CompilerParams(vmem_limit_bytes=mib * 2**20)


def spread_points(index, parts, right_planes, write):
    points = index.shape[1]
    column = (index >> 16) * 128 + (index & 127)
    row = (index >> 7) & 511
    rows = ROWS
    if right_planes == 1:
        rows = ROWS // 2
        column = jnp.where(index >> 16 == 0, (row >> 8) * 128 + (index & 127), -1)
        row = row & 255
    row = row - lax.broadcasted_iota(jnp.int32, (8, points), 0) // HALF
    lanes = lax.broadcasted_iota(jnp.int32, (256, points), 0)
    right = jnp.where(lanes == column, 1.0, 0.0).astype(jnp.bfloat16)
    tile = lax.broadcasted_iota(jnp.int32, (rows // 8, 8, points), 0)
    mask = row[None] == (8 // HALF) * tile
    for which, part in enumerate(parts):
        total = None
        for piece in part:
            left = jnp.where(mask, piece[None], 0.0).reshape(rows, points).astype(jnp.bfloat16)
            got = lax.dot_general(
                left, right, (((1,), (1,)), ((), ())), preferred_element_type=jnp.float32
            )
            total = got if total is None else total + got
        lower, upper = total[:, 0:128], total[:, 128:256]
        if right_planes == 1:
            write(which, 0, jnp.concatenate([lower, upper]))
        else:
            write(which, 0, lower)
            write(which, 1, upper)


def pieces_of(value, count):
    high = value.astype(jnp.bfloat16).astype(jnp.float32)
    return [high, value - high][:count]


def list_row(ref, base, i):
    block = ref[base + 8 * i : base + 8 * i + 8, :]
    return jnp.concatenate([block[j : j + 1] for j in range(8)], 1)


def either(core, zero, one):
    return lambda i: jnp.where(core == 0, list_row(*zero, i), list_row(*one, i))


def by_parity(even, odd, points):
    parity = lax.broadcasted_iota(jnp.int32, (8, points), 0) % HALF
    return jnp.where(parity == 0, even, odd)


def points_of(core, row, first):
    even = jnp.where(core == 0, row(first), row(first + 2))
    odd = jnp.where(core == 0, row(first + 1), row(first + 3))
    return by_parity(even, odd, even.shape[1])


def writer(stores):
    def write(which, p, value):
        ref, first = stores[which]
        ref[first + p] = value

    return write


def scatter_src(core, row, count, store, first, divisor=None, planes=2):
    amp = points_of(core, row, 2)
    if divisor is not None:
        amp = amp / divisor
    index = row(0).astype(jnp.int32)
    spread_points(index, [pieces_of(amp, count)], planes, writer([(store, first)]))


def scatter_rec(core, row, count, planes, ob, cn, first):
    obs = points_of(core, row, 6)
    parts = [pieces_of(obs, count), [jnp.ones_like(obs)]]
    index = row(1).astype(jnp.int32)
    spread_points(index, parts, planes, writer([(ob, first), (cn, first)]))


def squares(damp):
    core = lax.axis_index("core")
    first, second = damp[HALF * core], damp[HALF * core + 1]
    return first * first, second * second


def diagonal_at(damp, row):
    sigma = row(10)
    first, second = squares(damp)
    return by_parity(6.0 + first * sigma, 6.0 + second * sigma, sigma.shape[1])


def pack_kernel(slow_in, src_in, rec_in, amp_in, obs_in, out, far, src, rec, amp, obs, sem):
    slab = lax.axis_index("pair") * 2 + lax.axis_index("core")
    offset = slab * (2 * 512 * 128)
    pairs = ((src_in, src), (rec_in, rec), (amp_in, amp), (obs_in, obs), (slow_in, out.at[0:ROWS]))
    copies = [pltpu.make_async_copy(x, y, sem.at[k]) for k, (x, y) in enumerate(pairs)]
    for copy in copies[::-1]:
        copy.start()
    for copy in copies[:4]:
        copy.wait()
    far[80:88, :] = jnp.zeros((8, 128), jnp.float32)
    points = amp.shape[1]
    far[0:8, :] = (src[...] - offset).astype(jnp.float32)
    far[8:16, :] = (rec[...] - offset).astype(jnp.float32)
    for k, values in ((2, amp), (6, obs)):
        for i in range(4):
            for j in range(8):
                at = 8 * (k + i) + j
                far[at : at + 1, :] = values[i : i + 1, 128 * j : 128 * j + 128]
    out[ROWS : ROWS + LIST, :] = far[...]
    for copy in copies[4:]:
        copy.wait()


def gather_sigma(sigma, row, store):
    index = row(0).astype(jnp.int32)
    points = index.shape[1]
    rows = lax.broadcasted_iota(jnp.int32, (ROWS, points), 0)
    pick = jnp.where(rows == index >> 7, 1.0, 0.0).astype(jnp.bfloat16)
    high = sigma.astype(jnp.bfloat16)
    low = (sigma - high.astype(jnp.float32)).astype(jnp.bfloat16)
    dims = (((0,), (0,)), ((), ()))
    got = lax.dot_general(high, pick, dims, preferred_element_type=jnp.float32)
    got = got + lax.dot_general(low, pick, dims, preferred_element_type=jnp.float32)
    lane = lax.broadcasted_iota(jnp.int32, (128, points), 0)
    found = jnp.sum(jnp.where(lane == index & 127, got, 0.0), axis=0, keepdims=True)
    for j in range(8):
        store[80 + j : 81 + j, :] = found[:, 128 * j : 128 * j + 128]


def scatter_slab(h, row, b, ob, cn):
    core = lax.axis_index("core")
    scatter_src(core, row, 2, b, 2 * h)
    scatter_rec(core, row, 2, 2, ob, cn, 2 * h)


def scatter_own_kernel(lists, b, ob, cn):
    scatter_slab(lax.axis_index("core"), functools.partial(list_row, lists, 0), b, ob, cn)


def scatter_other_kernel(mine, other, b_in, ob_in, cn_in, b, ob, cn, first):
    core = lax.axis_index("core")
    whole = jnp.where(core == 0, mine[...], other[...])
    first[...] = whole[ROWS:SLAB]
    gather_sigma(whole[0:ROWS], functools.partial(list_row, first, 0), first)
    row = functools.partial(list_row, other, ROWS)
    scatter_slab(1 - lax.axis_index("core"), row, b, ob, cn)


def scatter_near(core, heavy, heavy_low, light, light_low, b):
    scatter_src(core, heavy, 2, b, jnp.where(heavy_low, 2, 4))
    scatter_src(core, light, 1, b, jnp.where(light_low, 0, 6))


def scatter_mine_kernel(low, high, b, ob, cn):
    core = lax.axis_index("core")
    heavy = either(core, (high, ROWS), (low, ROWS))
    light = either(core, (low, ROWS), (high, ROWS))
    scatter_near(core, heavy, core == 1, light, core == 0, b)
    scatter_rec(core, heavy, 2, 2, ob, cn, jnp.where(core == 1, 0, 2))


def scatter_theirs_kernel(damp, far, near, b_in, b):
    core = lax.axis_index("core")
    low_at, high_at = ROWS, SLAB + ROWS
    heavy = either(core, (near, low_at), (near, high_at))
    light = either(core, (near, high_at), (near, low_at))
    scatter_near(core, heavy, core == 0, light, core == 1, b)
    last = functools.partial(list_row, far, 0)
    scatter_src(core, last, 1, b, 8, diagonal_at(damp, last), 1)


def scatter_late_kernel(high, near, ob_in, cn_in, ob, cn):
    core = lax.axis_index("core")
    low_at, high_at = ROWS, SLAB + ROWS
    heavy = either(core, (near, low_at), (near, high_at))
    scatter_rec(core, heavy, 2, 2, ob, cn, jnp.where(core == 0, 0, 2))
    scatter_rec(core, either(core, (near, high_at), (high, ROWS)), 1, 1, ob, cn, 4)


def shift_matrix():
    i = lax.broadcasted_iota(jnp.int32, (128, 128), 0)
    j = lax.broadcasted_iota(jnp.int32, (128, 128), 1)
    return jnp.where(jnp.abs(i - j) == 1, 1.0, 0.0).astype(jnp.bfloat16)


def neighbours(ref, t):
    ext = ref[t]
    x = ext[PAD : PAD + ROWS]
    total = ROWS + 2 * PAD
    down = pltpu.roll(ext, HALF, 0)[PAD : PAD + ROWS]
    up = pltpu.roll(ext, total - HALF, 0)[PAD : PAD + ROWS]
    high = x.astype(jnp.bfloat16)
    low = (x - high.astype(jnp.float32)).astype(jnp.bfloat16)
    matrix = shift_matrix()
    along = jnp.dot(high, matrix, preferred_element_type=jnp.float32)
    along = along + jnp.dot(low, matrix, preferred_element_type=jnp.float32)
    return x, (down + up) + along


def fold(x):
    return jnp.sum(x.reshape(ROWS // 8, 8, 128), 0)


def walk(first, last, body, carry):
    return lax.fori_loop(first, last, body, carry)


INNER = pl.ds(PAD, 1024)


def advance(src, s_off, inv, i_off, dst, d_off, first, last, dots):
    def body(t, carry):
        x, q = neighbours(src, t - s_off)
        q = q + (src[t - s_off - 1, INNER, :] + src[t - s_off + 1, INNER, :])
        new = inv[t - i_off] * q
        dst[t - d_off, INNER, :] = new
        if not dots:
            return carry
        return carry[0] + fold(x * q), carry[1] + fold(new * q)

    zero = jnp.zeros((8, 128), jnp.float32)
    return walk(first, last, body, (zero, zero) if dots else 0)


def last_moment(src, off):
    def body(t, carry):
        x, q = neighbours(src, t - off)
        q = q + 2.0 * src[t - off + 1, INNER, :]
        return carry + fold(x * q)

    return walk(4, 8, body, jnp.zeros((8, 128), jnp.float32))


def clear_pads(*refs):
    for ref in refs:
        zero = jnp.zeros((8, 128), jnp.float32)
        for t in range(ref.shape[0]):
            ref[t, 0:PAD, :] = zero
            ref[t, ref.shape[1] - PAD :, :] = zero


def message(moments):
    sub = lax.broadcasted_iota(jnp.int32, (8, 128), 0)
    lane = lax.broadcasted_iota(jnp.int32, (8, 128), 1)
    out = jnp.zeros((8, 128), jnp.float32)
    for k, moment in enumerate(moments):
        for c in range(HALF):
            total = jnp.sum(jnp.where(sub % HALF == c, moment, 0.0))
            out = out + jnp.where((sub == k) & (lane == c), total, 0.0)
    return out


def coefficients(terms):
    moments = (terms[0][...] + terms[1][...]) + (terms[2][...] + terms[3][...])
    m = [moments[k : k + 1, :] for k in range(6)]

    def product(p, shift):
        total = 0.0
        for i, a in enumerate(p):
            for j, b in enumerate(p):
                total = total + a * b * (m[i + j] - m[i + j + 1] if shift else m[i + j])
        return total

    one = jnp.ones_like(m[0])
    z, p, energy = [one], [one], m[0]
    x = [0.0 * one] * 3
    for it in range(3):
        stride = energy / product(p, True)
        x = [x[i] + (stride * p[i] if i < len(p) else 0.0) for i in range(3)]
        if it < 2:
            applied = [a - b for a, b in zip(p + [0.0 * one], [0.0 * one] + p)]
            z = [a - stride * b for a, b in zip(z + [0.0 * one], applied)]
            new = product(z, False)
            p = [a + new / energy * b for a, b in zip(z, p + [0.0 * one])]
            energy = new
    lane = lax.broadcasted_iota(jnp.int32, (1, 128), 1)
    sub = lax.broadcasted_iota(jnp.int32, (8, 128), 0)
    out = []
    for v in x:
        value = [jnp.sum(jnp.where(lane == c, v, 0.0)) for c in range(HALF)]
        out.append(jnp.where(sub % HALF == 0, value[0], value[1]))
    return out


def times(pattern, x):
    return (pattern[None] * x.reshape(ROWS // 8, 8, 128)).reshape(ROWS, 128)


def fill_inverse(core, square, inv, slab, mine, theirs, base, valid):
    def fill(p, _):
        at = pl.multiple_of(p * 512, 512)
        here = mine[pl.ds(at, 512), :]
        there = theirs[pl.ds(pl.multiple_of(base + at, 8), 512), :]
        sigma = jnp.where(core == slab % 2, here, there)
        for c in range(HALF):
            inv[2 * slab + p, pl.ds(c, 512, stride=HALF), :] = valid / (6.0 + square[c] * sigma)
        return 0

    lax.fori_loop(0, 2, fill, 0)


def forward_own_kernel(damp, own_m, own_t, b_own, inv, v0, v1, held):
    core = lax.axis_index("core")
    square = squares(damp)
    clear_pads(v0, v1)
    for slab in (2, 3):
        fill_inverse(core, square, inv, slab, own_m, own_t, 0, 1.0)

    def start(t, carry):
        right = b_own[t - 4]
        new = inv[t] * right
        v0[t, INNER, :] = new
        return carry + fold(new * right)

    held[0:8, :] = walk(4, 8, start, jnp.zeros((8, 128), jnp.float32))
    held[8:16, :], held[16:24, :] = advance(v0, 0, inv, 0, v1, 1, 5, 7, True)


def forward_kernel(
    damp, low_m, high_m, near_t, b_near, held, inv_in, v0_in, v1_in, inv, v0, v1, v2, msg
):
    pair, core = lax.axis_index("pair"), lax.axis_index("core")
    low = jnp.where(pair >= 1, 1.0, 0.0)
    high = jnp.where(pair + 1 < lax.axis_size("pair"), 1.0, 0.0)
    square = squares(damp)
    clear_pads(v2)
    fill_inverse(core, square, inv, 0, low_m, near_t, 0, low)
    fill_inverse(core, square, inv, 1, low_m, near_t, 0, low)
    fill_inverse(core, square, inv, 4, high_m, near_t, SLAB, high)
    fill_inverse(core, square, inv, 5, high_m, near_t, SLAB, high)

    def start(off):
        def body(t, carry):
            v0[t, INNER, :] = inv[t] * b_near[t - off]
            return carry

        return body

    v0[12, INNER, :] = b_near[8]
    walk(0, 4, start(0), 0)
    walk(8, 12, start(4), 0)
    advance(v0, 0, inv, 0, v1, 1, 1, 4, False)
    m1, m2 = advance(v0, 0, inv, 0, v1, 1, 4, 5, True)
    more1, more2 = advance(v0, 0, inv, 0, v1, 1, 7, 8, True)
    advance(v0, 0, inv, 0, v1, 1, 8, 12, False)
    m1 = m1 + more1 + held[8:16, :]
    m2 = m2 + more2 + held[16:24, :]
    advance(v1, 1, inv, 0, v2, 2, 2, 4, False)
    m3, m4 = advance(v1, 1, inv, 0, v2, 2, 4, 8, True)
    advance(v1, 1, inv, 0, v2, 2, 8, 11, False)
    m5 = last_moment(v2, 2)
    msg[...] = message([held[0:8, :], m1, m2, m3, m4, m5])


def adjoint_kernel(
    t0, t1, t2, t3, inv, v0, v1, v2, ob_own, cn_own, ob_near, cn_near, wave, u0, u1, u2, msg
):
    a = coefficients((t0, t1, t2, t3))

    def start(ob, cn, off, own):
        def body(t, carry):
            w = times(a[0], v0[t, INNER, :]) + times(a[1], v1[t - 1, INNER, :])
            w = w + times(a[2], v2[t - 2, INNER, :])
            right = cn[t - off] * w - ob[t - off]
            new = inv[t] * right
            u0[t, INNER, :] = new
            if not own:
                return carry
            wave[t - 4] = w
            return carry + fold(new * right)

        return body

    zero = jnp.zeros((8, 128), jnp.float32)
    walk(2, 4, start(ob_near, cn_near, 2, False), 0)
    m0 = walk(4, 8, start(ob_own, cn_own, 4, True), zero)
    walk(8, 11, start(ob_near, cn_near, 6, False), 0)
    advance(u0, 0, inv, 0, u1, 1, 3, 4, False)
    m1, m2 = advance(u0, 0, inv, 0, u1, 1, 4, 8, True)
    advance(u0, 0, inv, 0, u1, 1, 8, 10, False)
    m3, m4 = advance(u1, 1, inv, 0, u2, 2, 4, 8, True)
    advance(u1, 1, inv, 0, u2, 2, 8, 9, False)
    m5 = last_moment(u2, 2)
    msg[...] = message([m0, m1, m2, m3, m4, m5])


def gradient_kernel(other, damp, t0, t1, t2, t3, wave, u0, u1, u2, *rest):
    held = rest[-1]
    a = coefficients((t0, t1, t2, t3))
    sub = lax.broadcasted_iota(jnp.int32, (8, 128), 0)
    square = jnp.where(sub % HALF == 0, *squares(damp))
    a = [-square * v for v in a]
    core = lax.axis_index("core")
    core = 1 - core if other else core
    bands = rest[0] if other else rest[-2]
    for p in range(2):
        t = 4 + 2 * core + p
        x = times(a[0], u0[t, INNER, :]) + times(a[1], u1[t - 1, INNER, :])
        x = x + times(a[2], u2[t - 2, INNER, :])
        held[...] = x * wave[t - 4]
        for band in range(4):
            at = band * 256
            both = held[pl.ds(at, 128, stride=HALF), :] + held[pl.ds(at + 1, 128, stride=HALF), :]
            bands[band, p] = both if other else both + rest[0][band, p]
    if not other:
        lap = lax.axis_index("lap")
        for d in range(4):
            rest[2 + d][:, 0:128, :] = bands[lap ^ d]
            rest[2 + d][:, 128:136, :] = rest[1][...]


def power_kernel(g0, g1, g2, g3, own, msg, prior_y):
    lap = lax.axis_index("lap")
    g = (g0[:, 0:128] + g1[:, 0:128]) + (g2[:, 0:128] + g3[:, 0:128])
    own[...] = g
    msg[...] = jnp.full((128, 128), jnp.sum(g * g), jnp.float32)
    before = jnp.where(lap == 2, g3[:, 128:136], g1[:, 128:136])
    prior_y[...] = jnp.where(lap == 0, 0.0, before)


def variation_kernel(slow, own_t, near_t, dual, dual_next, base, send_x, send_y):
    lap, pair, core = (lax.axis_index(name) for name in ("lap", "pair", "core"))
    start = pl.multiple_of(lap * 128, 128)
    band = pl.ds(start, 128)
    after = pl.ds(pl.multiple_of(jnp.minimum(start + 128, 504), 8), 8)
    row = lax.broadcasted_iota(jnp.int32, (128, 128), 0)
    lane = lax.broadcasted_iota(jnp.int32, (128, 128), 1)
    last_y = (row == 127) & (lap == 3)
    last_z = lane == 127
    comps = []
    for p in range(2):
        here = slow[p, band, :]
        if p == 0:
            step_x = slow[1, band, :] - here
        else:
            beyond = near_t[pl.ds(pl.multiple_of(SLAB + start, 8), 128), :]
            step_x = jnp.where(core == 0, own_t[band, :], beyond) - here
            step_x = jnp.where((core == 1) & (pair == 15), 0.0, step_x)
        rolled = pltpu.roll(here, 127, 0)
        step_y = jnp.where(row == 127, slow[p, after, :][0:1], rolled) - here
        step_y = jnp.where(last_y, 0.0, step_y)
        step_z = jnp.where(last_z, 0.0, pltpu.roll(here, 127, 1) - here)
        trial = [dual[k, p] + dual_step * step for k, step in enumerate((step_x, step_y, step_z))]
        magnitude = jnp.sqrt(trial[0] * trial[0] + trial[1] * trial[1] + trial[2] * trial[2])
        scale = jnp.maximum(1.0, magnitude / tv_weight)
        new = [x / scale for x in trial]
        for k in range(3):
            dual_next[k, p] = new[k]
        if p == 1:
            new[0] = jnp.where((core == 1) & (pair == 15), 0.0, new[0])
        new[1] = jnp.where(last_y, 0.0, new[1])
        new[2] = jnp.where(last_z, 0.0, new[2])
        comps.append(new)
    for p in range(2):
        x, y, z = comps[p]
        back = jnp.where(row == 0, 0.0, pltpu.roll(y, 1, 0)) - y
        back = back + (jnp.where(lane == 0, 0.0, pltpu.roll(z, 1, 1)) - z)
        back = back + (comps[0][0] - x if p == 1 else -x)
        base[p] = slow[p, band, :] - primal_step * back
        send_y[p] = y[120:128]
    send_x[0] = comps[1][0]


def model_kernel(cells, base, grad, power, prior_x, prior_y, model):
    total = power[0]
    for k in range(1, 16):
        total = total + power[k]
    total = jnp.sum(total, axis=0, keepdims=True)
    scale = 1.0 / jnp.sqrt(total / cells + 1e-06)
    row = lax.broadcasted_iota(jnp.int32, (128, 128), 0)
    for p in range(2):
        back = jnp.where(row == 0, prior_y[p][7:8], 0.0)
        if p == 0:
            back = back + prior_x[0]
        model[p] = base[p] - primal_step * (grad[p] * scale + back)


def cost(work):
    return pl.CostEstimate(flops=work * 10**9, bytes_accessed=10**6, transcendentals=0)


def struct(*shape):
    return jax.ShapeDtypeStruct(shape, jnp.float32)


def moved(x, axis, by):
    peers = lax.axis_size(axis)
    return lax.ppermute(x, axis, [(i, i + by) for i in range(peers) if 0 <= i + by < peers])


def swapped(x):
    return lax.ppermute(x, "core", [(0, 1), (1, 0)])


def pair_sum(x):
    def others(x, masks):
        return [lax.ppermute(x, "pair", [(i, i ^ d) for i in range(16)]) for d in masks]

    x = x + sum(others(x, (1, 2, 3)))
    return [x] + others(x, (4, 8, 12))


def scatter(kernel, name, work, inputs, shapes, into=()):
    scalars = 1 if inputs[0].ndim == 1 else 0
    first = len(inputs)
    return pl.pallas_call(
        kernel,
        out_shape=tuple(struct(*shape) for shape in shapes),
        in_specs=[SMEM] * scalars + [VMEM] * (len(inputs) - scalars + len(into)),
        out_specs=(VMEM,) * len(shapes),
        input_output_aliases={first + k: k for k in range(len(into))},
        compiler_params=params(8),
        cost_estimate=cost(work),
        name=name,
    )(*inputs, *into)


def on_device(slowness, damping, src_index, src_amp, rec_index, observed, dual):
    width_x, rows_y, depth_z = slowness.shape
    slab_cells = width_x * rows_y * depth_z
    pairs = lax.axis_size("pair")

    packed, lists = pl.pallas_call(
        pack_kernel,
        out_shape=(struct(SLAB, 128), struct(LIST, 128)),
        in_specs=[pl.BlockSpec(memory_space=pltpu.HBM)] * 5,
        out_specs=(VMEM,) * 2,
        scratch_shapes=[
            pltpu.VMEM((8, 128), jnp.int32), pltpu.VMEM((8, 128), jnp.int32),
            pltpu.VMEM(src_amp.shape, jnp.float32), pltpu.VMEM(observed.shape, jnp.float32),
            pltpu.SemaphoreType.DMA((5,)),
        ],
        compiler_params=params(8),
        name="pack",
    )(
        *(
            pltpu.with_memory_space_constraint(x, pltpu.HBM)
            for x in (
                slowness.reshape(ROWS, 128), src_index.reshape(8, 128), rec_index.reshape(8, 128),
                src_amp, observed,
            )
        )
    )
    low_m, high_m = moved(packed, "pair", 1), moved(packed, "pair", -1)
    own_t = swapped(packed)

    block, near_block = (4, ROWS, 128), (5, ROWS, 128)
    own = scatter(scatter_own_kernel, "scatter_own", 5, (lists,), [block] * 3)
    b_own, ob_own, cn_own, first = scatter(
        scatter_other_kernel, "scatter_other", 5, (packed, own_t), [block] * 3 + [(LIST, 128)], own
    )
    far_m = moved(first, "pair", -2)
    padded = ROWS + 2 * PAD
    inv, v0, v1, held = pl.pallas_call(
        forward_own_kernel,
        out_shape=(
            struct(PLANES, ROWS, 128), struct(13, padded, 128), struct(11, padded, 128),
            struct(24, 128),
        ),
        in_specs=[SMEM] + [VMEM] * 3,
        out_specs=(VMEM,) * 4,
        compiler_params=params(2),
        cost_estimate=cost(4),
        name="forward_own",
    )(damping, slowness.reshape(ROWS, 128), own_t, b_own)
    low_m, high_m, far_m, held = lax.optimization_barrier((low_m, high_m, far_m, held))
    near_t = swapped(jnp.concatenate([low_m, high_m]))
    b_near, ob_near, cn_near = scatter(
        scatter_mine_kernel, "scatter_mine", 6, (low_m, high_m),
        [(9, ROWS, 128), near_block, near_block],
    )
    near_t, b_near = lax.optimization_barrier((near_t, b_near))
    b_near, = scatter(
        scatter_theirs_kernel, "scatter_theirs", 5, (damping, far_m, near_t), [(9, ROWS, 128)],
        (b_near,),
    )

    inv, v0, v1, v2, msg = pl.pallas_call(
        forward_kernel,
        out_shape=(
            struct(PLANES, ROWS, 128), struct(13, padded, 128), struct(11, padded, 128),
            struct(9, padded, 128), struct(8, 128),
        ),
        in_specs=[SMEM] + [VMEM] * 8,
        out_specs=(VMEM,) * 5,
        input_output_aliases={6: 0, 7: 1, 8: 2},
        compiler_params=params(2),
        cost_estimate=cost(20),
        name="forward",
    )(damping, low_m, high_m, near_t, b_near, held, inv, v0, v1)

    near_t, msg = lax.optimization_barrier((near_t, msg))
    ob_near, cn_near = scatter(
        scatter_late_kernel, "scatter_late", 5, (high_m, near_t), [near_block] * 2,
        (ob_near, cn_near),
    )
    wave, u0, u1, u2, msg = pl.pallas_call(
        adjoint_kernel,
        out_shape=(
            struct(4, ROWS, 128), struct(13, padded, 128), struct(11, padded, 128),
            struct(9, padded, 128), struct(8, 128),
        ),
        in_specs=[VMEM] * 12,
        out_specs=(VMEM,) * 5,
        input_output_aliases={5: 1, 6: 2, 7: 3},
        compiler_params=params(2),
        cost_estimate=cost(14),
        name="adjoint",
    )(*pair_sum(msg), inv, v0, v1, v2, ob_own, cn_own, ob_near, cn_near)

    terms = pair_sum(msg)

    def gradient(other, *more):
        scratch = [] if other else [pltpu.VMEM((4, 2, 128, 128), jnp.float32)]
        return pl.pallas_call(
            functools.partial(gradient_kernel, other),
            out_shape=struct(4, 2, 128, 128) if other else (struct(2, 136, 128),) * 4,
            in_specs=[SMEM] + [VMEM] * (8 + len(more)),
            out_specs=VMEM if other else (VMEM,) * 4,
            scratch_shapes=scratch + [pltpu.VMEM((ROWS, 128), jnp.float32)],
            compiler_params=params(8),
            name="gradient",
        )(damping, *terms, wave, u0, u1, u2, *more)

    given = gradient(True)
    slowness, dual, own_t, near_t, given = lax.optimization_barrier(
        (slowness, dual, own_t, near_t, given)
    )
    dual_next, base, send_x, send_y = pl.pallas_call(
        variation_kernel,
        out_shape=(
            struct(3, 2, 128, 128), struct(2, 128, 128), struct(1, 128, 128), struct(2, 8, 128),
        ),
        in_specs=[VMEM] * 4,
        out_specs=(VMEM,) * 4,
        compiler_params=params(8),
        cost_estimate=cost(1),
        name="variation",
    )(slowness, own_t, near_t, dual)
    bands = gradient(False, swapped(given), send_y)
    send_x, bands = lax.optimization_barrier((send_x, bands))
    arrived = [bands[0]] + [
        lax.ppermute(bands[d], "lap", [(i, i ^ d) for i in range(4)]) for d in (1, 2, 3)
    ]
    prior_x = moved(send_x, ("pair", "core"), 1)
    arrived, prior_x = lax.optimization_barrier((arrived, prior_x))
    own_grad, power, prior_y = pl.pallas_call(
        power_kernel,
        out_shape=(struct(2, 128, 128), struct(128, 128), struct(2, 8, 128)),
        in_specs=[VMEM] * 4,
        out_specs=(VMEM,) * 3,
        compiler_params=params(8),
        name="power",
    )(*arrived)
    power = lax.all_to_all(power, ("lap", "pair", "core"), 0, 0, tiled=True)
    model = pl.pallas_call(
        functools.partial(model_kernel, float(slab_cells * 2 * pairs)),
        out_shape=struct(2, 128, 128),
        in_specs=[VMEM] * 5,
        out_specs=VMEM,
        compiler_params=params(8),
        name="model",
    )(base, own_grad, power.reshape(16, 8, 128), prior_x, prior_y)
    return (model, dual_next)


def solution(mesh):
    space = mesh.devices.shape[1]
    mesh = Mesh(mesh.devices.reshape(-1, space // 2, 2), ("lap", "pair", "core"))
    both = ("pair", "core")
    in_specs = (
        P(both, None, None),
        P("lap"),
        P(both),
        P("lap", both),
        P(both),
        P("lap", both),
        P(None, both, "lap", None),
    )
    out_specs = (P(both, "lap", None), P(None, both, "lap", None))
    return jax.shard_map(
        on_device, mesh=mesh, in_specs=in_specs, out_specs=out_specs, check_vma=False
    )
```

```python
import functools

import jax
import jax.numpy as jnp
from jax import lax
from jax.experimental import pallas as pl
from jax.experimental.pallas import tpu as pltpu
from jax.sharding import Mesh
from jax.sharding import PartitionSpec as P


HALF = 2
PLANES = 13
LINES = 512
ROWS = HALF * LINES
TURNED = 192
LIST = 88
SLAB = ROWS + LIST

dual_step = 0.5
primal_step = 0.2
tv_weight = 0.5

VMEM = pl.BlockSpec(memory_space=pltpu.VMEM)
SMEM = pl.BlockSpec(memory_space=pltpu.SMEM)


def params(mib):
    return pltpu.CompilerParams(vmem_limit_bytes=mib * 2**20)


def line_of(row):
    return (row & 63) * 8 + (row >> 6)


def spread_points(index, parts, right_planes, write):
    points = index.shape[1]
    column = (index >> 16) * 128 + (index & 127)
    line = line_of((index >> 7) & 511)
    lines = LINES
    if right_planes == 1:
        lines = LINES // 2
        column = jnp.where(index >> 16 == 0, (line >> 8) * 128 + (index & 127), -1)
        line = line & 255
    lanes = lax.broadcasted_iota(jnp.int32, (256, points), 0)
    right = jnp.where(lanes == column, 1.0, 0.0).astype(jnp.bfloat16)
    mask = lax.broadcasted_iota(jnp.int32, (lines, points), 0) == line
    for which, part in enumerate(parts):
        total = None
        for piece in zip(*part):
            left = [jnp.where(mask, value, 0.0).astype(jnp.bfloat16) for value in piece]
            got = lax.dot_general(
                jnp.concatenate(left), right, (((1,), (1,)), ((), ())),
                preferred_element_type=jnp.float32,
            )
            total = got if total is None else total + got
        for c in range(len(part)):
            rows = total[lines * c : lines * c + lines]
            lower, upper = rows[:, 0:128], rows[:, 128:256]
            if right_planes == 1:
                write(which, 0, c, jnp.concatenate([lower, upper]))
            else:
                write(which, 0, c, lower)
                write(which, 1, c, upper)


def pieces_of(value, count):
    high = value.astype(jnp.bfloat16).astype(jnp.float32)
    return [high, value - high][:count]


def list_row(ref, base, i):
    block = ref[base + 8 * i : base + 8 * i + 8, :]
    return jnp.concatenate([block[j : j + 1] for j in range(8)], 1)


def either(core, zero, one):
    return lambda i: jnp.where(core == 0, list_row(*zero, i), list_row(*one, i))


def points_of(core, row, first):
    return [jnp.where(core == 0, row(first + c), row(first + HALF + c)) for c in range(HALF)]


def writer(stores):
    def write(which, p, c, value):
        ref, first = stores[which]
        ref[first + p, LINES * c : LINES * c + LINES, :] = value

    return write


def scatter_src(core, row, count, store, first, divisor=None, planes=2):
    amp = points_of(core, row, 2)
    if divisor is not None:
        amp = [a / d for a, d in zip(amp, divisor)]
    index = row(0).astype(jnp.int32)
    spread_points(index, [[pieces_of(a, count) for a in amp]], planes, writer([(store, first)]))


def scatter_rec(core, row, count, planes, ob, cn, first):
    obs = points_of(core, row, 6)
    parts = [[pieces_of(o, count) for o in obs], [[jnp.ones_like(obs[0])]]]
    index = row(1).astype(jnp.int32)
    spread_points(index, parts, planes, writer([(ob, first), (cn, first)]))


def squares(damp):
    core = lax.axis_index("core")
    first, second = damp[HALF * core], damp[HALF * core + 1]
    return first * first, second * second


def diagonal_at(damp, row):
    sigma = row(10)
    return [6.0 + square * sigma for square in squares(damp)]


def pack_kernel(slow_in, src_in, rec_in, amp_in, obs_in, out, far, slow, src, rec, amp, obs, sem):
    slab = lax.axis_index("pair") * 2 + lax.axis_index("core")
    offset = slab * (2 * 512 * 128)
    pairs = ((src_in, src), (rec_in, rec), (amp_in, amp), (obs_in, obs), (slow_in, slow))
    copies = [pltpu.make_async_copy(x, y, sem.at[k]) for k, (x, y) in enumerate(pairs)]
    for copy in copies[::-1]:
        copy.start()
    for copy in copies[:4]:
        copy.wait()
    far[80:88, :] = jnp.zeros((8, 128), jnp.float32)
    points = amp.shape[1]
    far[0:8, :] = (src[...] - offset).astype(jnp.float32)
    far[8:16, :] = (rec[...] - offset).astype(jnp.float32)
    for k, values in ((2, amp), (6, obs)):
        for i in range(4):
            for j in range(8):
                at = 8 * (k + i) + j
                far[at : at + 1, :] = values[i : i + 1, 128 * j : 128 * j + 128]
    out[ROWS : ROWS + LIST, :] = far[...]
    for copy in copies[4:]:
        copy.wait()
    for p in range(2):
        for j in range(64):
            at = LINES * p + 8 * j
            out[at : at + 8, :] = slow[pl.ds(LINES * p + j, 8, stride=64), :]


def gather_sigma(sigma, row, store):
    index = row(0).astype(jnp.int32)
    points = index.shape[1]
    rows = lax.broadcasted_iota(jnp.int32, (ROWS, points), 0)
    line = (index >> 16) * LINES + line_of((index >> 7) & 511)
    pick = jnp.where(rows == line, 1.0, 0.0).astype(jnp.bfloat16)
    high = sigma.astype(jnp.bfloat16)
    low = (sigma - high.astype(jnp.float32)).astype(jnp.bfloat16)
    dims = (((0,), (0,)), ((), ()))
    got = lax.dot_general(high, pick, dims, preferred_element_type=jnp.float32)
    got = got + lax.dot_general(low, pick, dims, preferred_element_type=jnp.float32)
    lane = lax.broadcasted_iota(jnp.int32, (128, points), 0)
    found = jnp.sum(jnp.where(lane == index & 127, got, 0.0), axis=0, keepdims=True)
    for j in range(8):
        store[80 + j : 81 + j, :] = found[:, 128 * j : 128 * j + 128]


def scatter_slab(h, row, b, ob, cn):
    core = lax.axis_index("core")
    scatter_src(core, row, 2, b, 2 * h)
    scatter_rec(core, row, 2, 2, ob, cn, 2 * h)


def scatter_own_kernel(lists, b, ob, cn):
    scatter_slab(lax.axis_index("core"), functools.partial(list_row, lists, 0), b, ob, cn)


def scatter_other_kernel(mine, other, b_in, ob_in, cn_in, b, ob, cn, first):
    core = lax.axis_index("core")
    whole = jnp.where(core == 0, mine[...], other[...])
    first[...] = whole[ROWS:SLAB]
    gather_sigma(whole[0:ROWS], functools.partial(list_row, first, 0), first)
    row = functools.partial(list_row, other, ROWS)
    scatter_slab(1 - lax.axis_index("core"), row, b, ob, cn)


def scatter_near(core, heavy, heavy_low, light, light_low, b):
    scatter_src(core, heavy, 2, b, jnp.where(heavy_low, 2, 4))
    scatter_src(core, light, 1, b, jnp.where(light_low, 0, 6))


def scatter_mine_kernel(low, high, b, ob, cn):
    core = lax.axis_index("core")
    heavy = either(core, (high, ROWS), (low, ROWS))
    light = either(core, (low, ROWS), (high, ROWS))
    scatter_near(core, heavy, core == 1, light, core == 0, b)
    scatter_rec(core, heavy, 2, 2, ob, cn, jnp.where(core == 1, 0, 2))


def scatter_theirs_kernel(damp, far, near, b_in, b):
    core = lax.axis_index("core")
    low_at, high_at = ROWS, SLAB + ROWS
    heavy = either(core, (near, low_at), (near, high_at))
    light = either(core, (near, high_at), (near, low_at))
    scatter_near(core, heavy, core == 0, light, core == 1, b)
    last = functools.partial(list_row, far, 0)
    scatter_src(core, last, 1, b, 8, diagonal_at(damp, last), 1)


def scatter_late_kernel(high, near, ob_in, cn_in, ob, cn):
    core = lax.axis_index("core")
    low_at, high_at = ROWS, SLAB + ROWS
    heavy = either(core, (near, low_at), (near, high_at))
    scatter_rec(core, heavy, 2, 2, ob, cn, jnp.where(core == 0, 0, 2))
    scatter_rec(core, either(core, (near, high_at), (high, ROWS)), 1, 1, ob, cn, 4)


def shift_matrix():
    i = lax.broadcasted_iota(jnp.int32, (128, 128), 0)
    j = lax.broadcasted_iota(jnp.int32, (128, 128), 1)
    return jnp.where(jnp.abs(i - j) == 1, 1.0, 0.0).astype(jnp.bfloat16)


def half(ref, t, c):
    return ref[t, LINES * c : LINES * c + LINES, :]


def beside(x):
    sub = lax.broadcasted_iota(jnp.int32, (8, 128), 0)
    before = jnp.where(sub == 0, 0.0, pltpu.roll(x[LINES - 8 :], 1, 0))
    after = jnp.where(sub == 7, 0.0, pltpu.roll(x[:8], 7, 0))
    across = jnp.concatenate([before, x[: LINES - 8]]) + jnp.concatenate([x[8:], after])
    turned, rest = x[:TURNED], x[TURNED:]
    lane = lax.broadcasted_iota(jnp.int32, turned.shape, 1)
    low = jnp.where(lane == 0, 0.0, pltpu.roll(turned, 1, 1))
    high = jnp.where(lane == 127, 0.0, pltpu.roll(turned, 127, 1))
    matrix = shift_matrix()
    coarse = rest.astype(jnp.bfloat16)
    fine = (rest - coarse.astype(jnp.float32)).astype(jnp.bfloat16)
    along = jnp.dot(coarse, matrix, preferred_element_type=jnp.float32)
    along = along + jnp.dot(fine, matrix, preferred_element_type=jnp.float32)
    return across + jnp.concatenate([low + high, along])


def fold(x):
    return jnp.sum(x.reshape(LINES // 8, 8, 128), 0)


def walk(first, last, body, carry):
    return lax.fori_loop(first, last, body, carry)


def nothing():
    return [jnp.zeros((8, 128), jnp.float32) for _ in range(HALF)]


def advance(src, s_off, inv, dst, d_off, first, last, dots):
    def body(t, carry):
        one, two = [], []
        for c in range(HALF):
            x = half(src, t - s_off, c)
            q = beside(x) + (half(src, t - s_off - 1, c) + half(src, t - s_off + 1, c))
            new = half(inv, t, c) * q
            dst[t - d_off, LINES * c : LINES * c + LINES, :] = new
            if dots:
                one.append(carry[0][c] + fold(x * q))
                two.append(carry[1][c] + fold(new * q))
        return (one, two) if dots else carry

    return walk(first, last, body, (nothing(), nothing()) if dots else 0)


def last_moment(src, off):
    def body(t, carry):
        out = []
        for c in range(HALF):
            x = half(src, t - off, c)
            out.append(carry[c] + fold(x * (beside(x) + 2.0 * half(src, t - off + 1, c))))
        return out

    return walk(4, 8, body, nothing())


def message(moments):
    sub = lax.broadcasted_iota(jnp.int32, (8, 128), 0)
    lane = lax.broadcasted_iota(jnp.int32, (8, 128), 1)
    out = jnp.zeros((8, 128), jnp.float32)
    for k, moment in enumerate(moments):
        for c in range(HALF):
            total = jnp.sum(moment[c])
            out = out + jnp.where((sub == k) & (lane == c), total, 0.0)
    return out


def coefficients(terms):
    moments = (terms[0][...] + terms[1][...]) + (terms[2][...] + terms[3][...])
    m = [moments[k : k + 1, :] for k in range(6)]

    def product(p, shift):
        total = 0.0
        for i, a in enumerate(p):
            for j, b in enumerate(p):
                total = total + a * b * (m[i + j] - m[i + j + 1] if shift else m[i + j])
        return total

    one = jnp.ones_like(m[0])
    z, p, energy = [one], [one], m[0]
    x = [0.0 * one] * 3
    for it in range(3):
        stride = energy / product(p, True)
        x = [x[i] + (stride * p[i] if i < len(p) else 0.0) for i in range(3)]
        if it < 2:
            applied = [a - b for a, b in zip(p + [0.0 * one], [0.0 * one] + p)]
            z = [a - stride * b for a, b in zip(z + [0.0 * one], applied)]
            new = product(z, False)
            p = [a + new / energy * b for a, b in zip(z, p + [0.0 * one])]
            energy = new
    lane = lax.broadcasted_iota(jnp.int32, (1, 128), 1)
    return [[jnp.sum(jnp.where(lane == c, v, 0.0)) for c in range(HALF)] for v in x]


def fill_inverse(core, square, inv, slab, mine, theirs, base, valid):
    def fill(p, _):
        at = pl.multiple_of(p * 512, 512)
        here = mine[pl.ds(at, 512), :]
        there = theirs[pl.ds(pl.multiple_of(base + at, 8), 512), :]
        sigma = jnp.where(core == slab % 2, here, there)
        for c in range(HALF):
            inv[2 * slab + p, LINES * c : LINES * c + LINES, :] = valid / (6.0 + square[c] * sigma)
        return 0

    lax.fori_loop(0, 2, fill, 0)


def forward_own_kernel(damp, own_m, own_t, b_own, inv, v0, v1, held):
    core = lax.axis_index("core")
    square = squares(damp)
    for slab in (2, 3):
        fill_inverse(core, square, inv, slab, own_m, own_t, 0, 1.0)

    def start(t, carry):
        out = []
        for c in range(HALF):
            right = half(b_own, t - 4, c)
            new = half(inv, t, c) * right
            v0[t, LINES * c : LINES * c + LINES, :] = new
            out.append(carry[c] + fold(new * right))
        return out

    m0 = walk(4, 8, start, nothing())
    m1, m2 = advance(v0, 0, inv, v1, 1, 5, 7, True)
    for k, part in enumerate(m0 + m1 + m2):
        held[8 * k : 8 * k + 8, :] = part


def forward_kernel(
    damp, low_m, high_m, near_t, b_near, held, inv_in, v0_in, v1_in, inv, v0, v1, v2, msg
):
    pair, core = lax.axis_index("pair"), lax.axis_index("core")
    low = jnp.where(pair >= 1, 1.0, 0.0)
    high = jnp.where(pair + 1 < lax.axis_size("pair"), 1.0, 0.0)
    square = squares(damp)
    fill_inverse(core, square, inv, 0, low_m, near_t, 0, low)
    fill_inverse(core, square, inv, 1, low_m, near_t, 0, low)
    fill_inverse(core, square, inv, 4, high_m, near_t, SLAB, high)
    fill_inverse(core, square, inv, 5, high_m, near_t, SLAB, high)

    def start(off):
        def body(t, carry):
            v0[t] = inv[t] * b_near[t - off]
            return carry

        return body

    v0[12] = b_near[8]
    walk(0, 4, start(0), 0)
    walk(8, 12, start(4), 0)
    kept = [held[8 * k : 8 * k + 8, :] for k in range(3 * HALF)]
    advance(v0, 0, inv, v1, 1, 1, 4, False)
    lower = advance(v0, 0, inv, v1, 1, 4, 5, True)
    upper = advance(v0, 0, inv, v1, 1, 7, 8, True)
    advance(v0, 0, inv, v1, 1, 8, 12, False)
    m1 = [a + b + c for a, b, c in zip(lower[0], upper[0], kept[HALF : 2 * HALF])]
    m2 = [a + b + c for a, b, c in zip(lower[1], upper[1], kept[2 * HALF :])]
    advance(v1, 1, inv, v2, 2, 2, 4, False)
    m3, m4 = advance(v1, 1, inv, v2, 2, 4, 8, True)
    advance(v1, 1, inv, v2, 2, 8, 11, False)
    m5 = last_moment(v2, 2)
    msg[...] = message([kept[:HALF], m1, m2, m3, m4, m5])


def adjoint_kernel(
    t0, t1, t2, t3, inv, v0, v1, v2, ob_own, cn_own, ob_near, cn_near, wave, u0, u1, u2, msg
):
    a = coefficients((t0, t1, t2, t3))

    def start(ob, cn, off, own):
        def body(t, carry):
            out = []
            count = cn[t - off]
            for c in range(HALF):
                lines = slice(LINES * c, LINES * c + LINES)
                w = a[0][c] * half(v0, t, c) + a[1][c] * half(v1, t - 1, c)
                w = w + a[2][c] * half(v2, t - 2, c)
                right = count * w - half(ob, t - off, c)
                new = half(inv, t, c) * right
                u0[t, lines, :] = new
                if own:
                    wave[t - 4, lines, :] = w
                    out.append(carry[c] + fold(new * right))
            return out if own else carry

        return body

    walk(2, 4, start(ob_near, cn_near, 2, False), 0)
    m0 = walk(4, 8, start(ob_own, cn_own, 4, True), nothing())
    walk(8, 11, start(ob_near, cn_near, 6, False), 0)
    advance(u0, 0, inv, u1, 1, 3, 4, False)
    m1, m2 = advance(u0, 0, inv, u1, 1, 4, 8, True)
    advance(u0, 0, inv, u1, 1, 8, 10, False)
    m3, m4 = advance(u1, 1, inv, u2, 2, 4, 8, True)
    advance(u1, 1, inv, u2, 2, 8, 9, False)
    m5 = last_moment(u2, 2)
    msg[...] = message([m0, m1, m2, m3, m4, m5])


def gradient_kernel(other, damp, t0, t1, t2, t3, wave, u0, u1, u2, *rest):
    held = rest[-1]
    a = coefficients((t0, t1, t2, t3))
    a = [[-square * v for square, v in zip(squares(damp), one)] for one in a]
    core = lax.axis_index("core")
    core = 1 - core if other else core
    bands = rest[0] if other else rest[-2]
    for p in range(2):
        t = 4 + 2 * core + p
        total = 0.0
        for c in range(HALF):
            x = a[0][c] * half(u0, t, c) + a[1][c] * half(u1, t - 1, c) + a[2][c] * half(u2, t - 2, c)
            total = total + x * half(wave, t - 4, c)
        held[...] = total
        for s in range(8):
            band, rows = s // 2, slice(64 * (s % 2), 64 * (s % 2) + 64)
            part = held[pl.ds(s, 64, stride=8), :]
            bands[band, p, rows, :] = part if other else part + rest[0][band, p, rows, :]
    if not other:
        lap = lax.axis_index("lap")
        for d in range(4):
            rest[2 + d][:, 0:128, :] = bands[lap ^ d]
            rest[2 + d][:, 128:136, :] = rest[1][...]


def power_kernel(g0, g1, g2, g3, own, msg, prior_y):
    lap = lax.axis_index("lap")
    g = (g0[:, 0:128] + g1[:, 0:128]) + (g2[:, 0:128] + g3[:, 0:128])
    own[...] = g
    msg[...] = jnp.full((128, 128), jnp.sum(g * g), jnp.float32)
    before = jnp.where(lap == 2, g3[:, 128:136], g1[:, 128:136])
    prior_y[...] = jnp.where(lap == 0, 0.0, before)


def band_of(ref, base, lap):
    out = None
    for k in range(4):
        parts = [ref[pl.ds(base + 2 * k + i, 64, stride=8), :] for i in range(2)]
        band = jnp.concatenate(parts)
        out = band if out is None else jnp.where(lap == k, band, out)
    return out


def variation_kernel(slow, own_t, near_t, dual, dual_next, base, send_x, send_y):
    lap, pair, core = (lax.axis_index(name) for name in ("lap", "pair", "core"))
    start = pl.multiple_of(lap * 128, 128)
    band = pl.ds(start, 128)
    after = pl.ds(pl.multiple_of(jnp.minimum(start + 128, 504), 8), 8)
    row = lax.broadcasted_iota(jnp.int32, (128, 128), 0)
    lane = lax.broadcasted_iota(jnp.int32, (128, 128), 1)
    last_y = (row == 127) & (lap == 3)
    last_z = lane == 127
    comps = []
    for p in range(2):
        here = slow[p, band, :]
        if p == 0:
            step_x = slow[1, band, :] - here
        else:
            beyond = jnp.where(core == 0, band_of(own_t, 0, lap), band_of(near_t, SLAB, lap))
            step_x = beyond - here
            step_x = jnp.where((core == 1) & (pair == 15), 0.0, step_x)
        rolled = pltpu.roll(here, 127, 0)
        step_y = jnp.where(row == 127, slow[p, after, :][0:1], rolled) - here
        step_y = jnp.where(last_y, 0.0, step_y)
        step_z = jnp.where(last_z, 0.0, pltpu.roll(here, 127, 1) - here)
        trial = [dual[k, p] + dual_step * step for k, step in enumerate((step_x, step_y, step_z))]
        magnitude = jnp.sqrt(trial[0] * trial[0] + trial[1] * trial[1] + trial[2] * trial[2])
        scale = jnp.maximum(1.0, magnitude / tv_weight)
        new = [x / scale for x in trial]
        for k in range(3):
            dual_next[k, p] = new[k]
        if p == 1:
            new[0] = jnp.where((core == 1) & (pair == 15), 0.0, new[0])
        new[1] = jnp.where(last_y, 0.0, new[1])
        new[2] = jnp.where(last_z, 0.0, new[2])
        comps.append(new)
    for p in range(2):
        x, y, z = comps[p]
        back = jnp.where(row == 0, 0.0, pltpu.roll(y, 1, 0)) - y
        back = back + (jnp.where(lane == 0, 0.0, pltpu.roll(z, 1, 1)) - z)
        back = back + (comps[0][0] - x if p == 1 else -x)
        base[p] = slow[p, band, :] - primal_step * back
        send_y[p] = y[120:128]
    send_x[0] = comps[1][0]


def model_kernel(cells, base, grad, power, prior_x, prior_y, model):
    total = power[0]
    for k in range(1, 16):
        total = total + power[k]
    total = jnp.sum(total, axis=0, keepdims=True)
    scale = 1.0 / jnp.sqrt(total / cells + 1e-06)
    row = lax.broadcasted_iota(jnp.int32, (128, 128), 0)
    for p in range(2):
        back = jnp.where(row == 0, prior_y[p][7:8], 0.0)
        if p == 0:
            back = back + prior_x[0]
        model[p] = base[p] - primal_step * (grad[p] * scale + back)


def cost(work):
    return pl.CostEstimate(flops=work * 10**9, bytes_accessed=10**6, transcendentals=0)


def struct(*shape):
    return jax.ShapeDtypeStruct(shape, jnp.float32)


def moved(x, axis, by):
    peers = lax.axis_size(axis)
    return lax.ppermute(x, axis, [(i, i + by) for i in range(peers) if 0 <= i + by < peers])


def swapped(x):
    return lax.ppermute(x, "core", [(0, 1), (1, 0)])


def pair_sum(x):
    def others(x, masks):
        return [lax.ppermute(x, "pair", [(i, i ^ d) for i in range(16)]) for d in masks]

    x = x + sum(others(x, (1, 2, 3)))
    return [x] + others(x, (4, 8, 12))


def scatter(kernel, name, work, inputs, shapes, into=()):
    scalars = 1 if inputs[0].ndim == 1 else 0
    first = len(inputs)
    return pl.pallas_call(
        kernel,
        out_shape=tuple(struct(*shape) for shape in shapes),
        in_specs=[SMEM] * scalars + [VMEM] * (len(inputs) - scalars + len(into)),
        out_specs=(VMEM,) * len(shapes),
        input_output_aliases={first + k: k for k in range(len(into))},
        compiler_params=params(8),
        cost_estimate=cost(work),
        name=name,
    )(*inputs, *into)


def on_device(slowness, damping, src_index, src_amp, rec_index, observed, dual):
    width_x, rows_y, depth_z = slowness.shape
    slab_cells = width_x * rows_y * depth_z
    pairs = lax.axis_size("pair")

    packed, lists = pl.pallas_call(
        pack_kernel,
        out_shape=(struct(SLAB, 128), struct(LIST, 128)),
        in_specs=[pl.BlockSpec(memory_space=pltpu.HBM)] * 5,
        out_specs=(VMEM,) * 2,
        scratch_shapes=[
            pltpu.VMEM((ROWS, 128), jnp.float32), pltpu.VMEM((8, 128), jnp.int32), pltpu.VMEM((8, 128), jnp.int32),
            pltpu.VMEM(src_amp.shape, jnp.float32), pltpu.VMEM(observed.shape, jnp.float32),
            pltpu.SemaphoreType.DMA((5,)),
        ],
        compiler_params=params(8),
        name="pack",
    )(
        *(
            pltpu.with_memory_space_constraint(x, pltpu.HBM)
            for x in (
                slowness.reshape(ROWS, 128), src_index.reshape(8, 128), rec_index.reshape(8, 128),
                src_amp, observed,
            )
        )
    )
    low_m, high_m = moved(packed, "pair", 1), moved(packed, "pair", -1)
    own_t = swapped(packed)

    block, near_block = (4, ROWS, 128), (5, ROWS, 128)
    count, near_count = (4, LINES, 128), (5, LINES, 128)
    own = scatter(scatter_own_kernel, "scatter_own", 5, (lists,), [block, block, count])
    b_own, ob_own, cn_own, first = scatter(
        scatter_other_kernel, "scatter_other", 5, (packed, own_t), [block, block, count, (LIST, 128)], own
    )
    far_m = moved(first, "pair", -2)
    inv, v0, v1, held = pl.pallas_call(
        forward_own_kernel,
        out_shape=(
            struct(PLANES, ROWS, 128), struct(13, ROWS, 128), struct(11, ROWS, 128),
            struct(48, 128),
        ),
        in_specs=[SMEM] + [VMEM] * 3,
        out_specs=(VMEM,) * 4,
        compiler_params=params(2),
        cost_estimate=cost(4),
        name="forward_own",
    )(damping, packed, own_t, b_own)
    low_m, high_m, far_m, held = lax.optimization_barrier((low_m, high_m, far_m, held))
    near_t = swapped(jnp.concatenate([low_m, high_m]))
    b_near, ob_near, cn_near = scatter(
        scatter_mine_kernel, "scatter_mine", 6, (low_m, high_m),
        [(9, ROWS, 128), near_block, near_count],
    )
    near_t, b_near = lax.optimization_barrier((near_t, b_near))
    b_near, = scatter(
        scatter_theirs_kernel, "scatter_theirs", 5, (damping, far_m, near_t), [(9, ROWS, 128)],
        (b_near,),
    )

    inv, v0, v1, v2, msg = pl.pallas_call(
        forward_kernel,
        out_shape=(
            struct(PLANES, ROWS, 128), struct(13, ROWS, 128), struct(11, ROWS, 128),
            struct(9, ROWS, 128), struct(8, 128),
        ),
        in_specs=[SMEM] + [VMEM] * 8,
        out_specs=(VMEM,) * 5,
        input_output_aliases={6: 0, 7: 1, 8: 2},
        compiler_params=params(2),
        cost_estimate=cost(20),
        name="forward",
    )(damping, low_m, high_m, near_t, b_near, held, inv, v0, v1)

    near_t, msg = lax.optimization_barrier((near_t, msg))
    ob_near, cn_near = scatter(
        scatter_late_kernel, "scatter_late", 5, (high_m, near_t), [near_block, near_count],
        (ob_near, cn_near),
    )
    wave, u0, u1, u2, msg = pl.pallas_call(
        adjoint_kernel,
        out_shape=(
            struct(4, ROWS, 128), struct(13, ROWS, 128), struct(11, ROWS, 128),
            struct(9, ROWS, 128), struct(8, 128),
        ),
        in_specs=[VMEM] * 12,
        out_specs=(VMEM,) * 5,
        input_output_aliases={5: 1, 6: 2, 7: 3},
        compiler_params=params(2),
        cost_estimate=cost(14),
        name="adjoint",
    )(*pair_sum(msg), inv, v0, v1, v2, ob_own, cn_own, ob_near, cn_near)

    terms = pair_sum(msg)

    def gradient(other, *more):
        scratch = [] if other else [pltpu.VMEM((4, 2, 128, 128), jnp.float32)]
        return pl.pallas_call(
            functools.partial(gradient_kernel, other),
            out_shape=struct(4, 2, 128, 128) if other else (struct(2, 136, 128),) * 4,
            in_specs=[SMEM] + [VMEM] * (8 + len(more)),
            out_specs=VMEM if other else (VMEM,) * 4,
            scratch_shapes=scratch + [pltpu.VMEM((LINES, 128), jnp.float32)],
            compiler_params=params(8),
            name="gradient",
        )(damping, *terms, wave, u0, u1, u2, *more)

    given = gradient(True)
    slowness, dual, own_t, near_t, given = lax.optimization_barrier(
        (slowness, dual, own_t, near_t, given)
    )
    dual_next, base, send_x, send_y = pl.pallas_call(
        variation_kernel,
        out_shape=(
            struct(3, 2, 128, 128), struct(2, 128, 128), struct(1, 128, 128), struct(2, 8, 128),
        ),
        in_specs=[VMEM] * 4,
        out_specs=(VMEM,) * 4,
        compiler_params=params(8),
        cost_estimate=cost(1),
        name="variation",
    )(slowness, own_t, near_t, dual)
    bands = gradient(False, swapped(given), send_y)
    send_x, bands = lax.optimization_barrier((send_x, bands))
    arrived = [bands[0]] + [
        lax.ppermute(bands[d], "lap", [(i, i ^ d) for i in range(4)]) for d in (1, 2, 3)
    ]
    prior_x = moved(send_x, ("pair", "core"), 1)
    arrived, prior_x = lax.optimization_barrier((arrived, prior_x))
    own_grad, power, prior_y = pl.pallas_call(
        power_kernel,
        out_shape=(struct(2, 128, 128), struct(128, 128), struct(2, 8, 128)),
        in_specs=[VMEM] * 4,
        out_specs=(VMEM,) * 3,
        compiler_params=params(8),
        name="power",
    )(*arrived)
    power = lax.all_to_all(power, ("lap", "pair", "core"), 0, 0, tiled=True)
    model = pl.pallas_call(
        functools.partial(model_kernel, float(slab_cells * 2 * pairs)),
        out_shape=struct(2, 128, 128),
        in_specs=[VMEM] * 5,
        out_specs=VMEM,
        compiler_params=params(8),
        name="model",
    )(base, own_grad, power.reshape(16, 8, 128), prior_x, prior_y)
    return (model, dual_next)


def solution(mesh):
    space = mesh.devices.shape[1]
    mesh = Mesh(mesh.devices.reshape(-1, space // 2, 2), ("lap", "pair", "core"))
    both = ("pair", "core")
    in_specs = (
        P(both, None, None),
        P("lap"),
        P(both),
        P("lap", both),
        P(both),
        P("lap", both),
        P(None, both, "lap", None),
    )
    out_specs = (P(both, "lap", None), P(None, both, "lap", None))
    return jax.shard_map(
        on_device, mesh=mesh, in_specs=in_specs, out_specs=out_specs, check_vma=False
    )
```

```python
import functools

import jax
import jax.numpy as jnp
from jax import lax
from jax.experimental import pallas as pl
from jax.experimental.pallas import tpu as pltpu
from jax.sharding import Mesh
from jax.sharding import PartitionSpec as P


HALF = 2
PLANES = 13
LINES = 512
ROWS = HALF * LINES
TURNED = 192
LIST = 88
SLAB = ROWS + LIST

dual_step = 0.5
primal_step = 0.2
tv_weight = 0.5

VMEM = pl.BlockSpec(memory_space=pltpu.VMEM)
SMEM = pl.BlockSpec(memory_space=pltpu.SMEM)


def params(mib):
    return pltpu.CompilerParams(vmem_limit_bytes=mib * 2**20)


def line_of(row):
    return (row & 63) * 8 + (row >> 6)


def spread_points(index, parts, right_planes, write):
    points = index.shape[1]
    column = (index >> 16) * 128 + (index & 127)
    line = line_of((index >> 7) & 511)
    lines = LINES
    if right_planes == 1:
        lines = LINES // 2
        column = jnp.where(index >> 16 == 0, (line >> 8) * 128 + (index & 127), -1)
        line = line & 255
    lanes = lax.broadcasted_iota(jnp.int32, (256, points), 0)
    right = jnp.where(lanes == column, 1.0, 0.0).astype(jnp.bfloat16)
    mask = lax.broadcasted_iota(jnp.int32, (lines, points), 0) == line
    for which, part in enumerate(parts):
        total = None
        for piece in zip(*part):
            left = [jnp.where(mask, value, 0.0).astype(jnp.bfloat16) for value in piece]
            got = lax.dot_general(
                jnp.concatenate(left), right, (((1,), (1,)), ((), ())),
                preferred_element_type=jnp.float32,
            )
            total = got if total is None else total + got
        for c in range(len(part)):
            rows = total[lines * c : lines * c + lines]
            lower, upper = rows[:, 0:128], rows[:, 128:256]
            if right_planes == 1:
                write(which, 0, c, jnp.concatenate([lower, upper]))
            else:
                write(which, 0, c, lower)
                write(which, 1, c, upper)


def pieces_of(value, count):
    high = value.astype(jnp.bfloat16).astype(jnp.float32)
    return [high, value - high][:count]


def list_row(ref, base, i):
    block = ref[base + 8 * i : base + 8 * i + 8, :]
    return jnp.concatenate([block[j : j + 1] for j in range(8)], 1)


def either(core, zero, one):
    return lambda i: jnp.where(core == 0, list_row(*zero, i), list_row(*one, i))


def points_of(core, row, first):
    return [jnp.where(core == 0, row(first + c), row(first + HALF + c)) for c in range(HALF)]


def writer(stores):
    def write(which, p, c, value):
        ref, first = stores[which]
        ref[first + p, LINES * c : LINES * c + LINES, :] = value

    return write


def scatter_src(core, row, count, store, first, divisor=None, planes=2):
    amp = points_of(core, row, 2)
    if divisor is not None:
        amp = [a / d for a, d in zip(amp, divisor)]
    index = row(0).astype(jnp.int32)
    spread_points(index, [[pieces_of(a, count) for a in amp]], planes, writer([(store, first)]))


def scatter_rec(core, row, count, planes, ob, cn, first):
    obs = points_of(core, row, 6)
    parts = [[pieces_of(o, count) for o in obs], [[jnp.ones_like(obs[0])]]]
    index = row(1).astype(jnp.int32)
    spread_points(index, parts, planes, writer([(ob, first), (cn, first)]))


def squares(damp):
    core = lax.axis_index("core")
    first, second = damp[HALF * core], damp[HALF * core + 1]
    return first * first, second * second


def diagonal_at(damp, row):
    sigma = row(10)
    return [6.0 + square * sigma for square in squares(damp)]


def pack_kernel(slow_in, src_in, rec_in, amp_in, obs_in, out, far, slow, src, rec, amp, obs, sem):
    slab = lax.axis_index("pair") * 2 + lax.axis_index("core")
    offset = slab * (2 * 512 * 128)
    pairs = ((src_in, src), (rec_in, rec), (amp_in, amp), (obs_in, obs), (slow_in, slow))
    copies = [pltpu.make_async_copy(x, y, sem.at[k]) for k, (x, y) in enumerate(pairs)]
    for copy in copies[::-1]:
        copy.start()
    for copy in copies[:4]:
        copy.wait()
    far[80:88, :] = jnp.zeros((8, 128), jnp.float32)
    points = amp.shape[1]
    far[0:8, :] = (src[...] - offset).astype(jnp.float32)
    far[8:16, :] = (rec[...] - offset).astype(jnp.float32)
    for k, values in ((2, amp), (6, obs)):
        for i in range(4):
            for j in range(8):
                at = 8 * (k + i) + j
                far[at : at + 1, :] = values[i : i + 1, 128 * j : 128 * j + 128]
    out[ROWS : ROWS + LIST, :] = far[...]
    for copy in copies[4:]:
        copy.wait()
    for p in range(2):
        for j in range(64):
            at = LINES * p + 8 * j
            out[at : at + 8, :] = slow[pl.ds(LINES * p + j, 8, stride=64), :]


def gather_sigma(sigma, row, store):
    index = row(0).astype(jnp.int32)
    points = index.shape[1]
    rows = lax.broadcasted_iota(jnp.int32, (ROWS, points), 0)
    line = (index >> 16) * LINES + line_of((index >> 7) & 511)
    pick = jnp.where(rows == line, 1.0, 0.0).astype(jnp.bfloat16)
    high = sigma.astype(jnp.bfloat16)
    low = (sigma - high.astype(jnp.float32)).astype(jnp.bfloat16)
    dims = (((0,), (0,)), ((), ()))
    got = lax.dot_general(high, pick, dims, preferred_element_type=jnp.float32)
    got = got + lax.dot_general(low, pick, dims, preferred_element_type=jnp.float32)
    lane = lax.broadcasted_iota(jnp.int32, (128, points), 0)
    found = jnp.sum(jnp.where(lane == index & 127, got, 0.0), axis=0, keepdims=True)
    for j in range(8):
        store[80 + j : 81 + j, :] = found[:, 128 * j : 128 * j + 128]


def scatter_slab(h, row, b, ob, cn):
    core = lax.axis_index("core")
    scatter_src(core, row, 2, b, 2 * h)
    scatter_rec(core, row, 2, 2, ob, cn, 2 * h)


def scatter_other_kernel(mine, other, b, ob, cn, first):
    core = lax.axis_index("core")
    whole = jnp.where(core == 0, mine[...], other[...])
    first[...] = whole[ROWS:SLAB]
    gather_sigma(whole[0:ROWS], functools.partial(list_row, first, 0), first)
    row = functools.partial(list_row, other, ROWS)
    scatter_slab(1 - lax.axis_index("core"), row, b, ob, cn)


def scatter_own_kernel(lists, first_in, b_in, ob_in, cn_in, b, ob, cn):
    scatter_slab(lax.axis_index("core"), functools.partial(list_row, lists, 0), b, ob, cn)


def lists_of(ref):
    return functools.partial(list_row, ref, ROWS)


def scatter_mine_kernel(damp, touch, beyond, far, b):
    core = lax.axis_index("core")
    scatter_src(core, lists_of(touch), 2, b, jnp.where(core == 0, 4, 2))
    scatter_src(core, lists_of(beyond), 1, b, jnp.where(core == 0, 0, 6))
    last = functools.partial(list_row, far, 0)
    scatter_src(core, last, 1, b, 8, diagonal_at(damp, last), 1)


def scatter_theirs_kernel(touch, beyond, b_in, b):
    core = lax.axis_index("core")
    scatter_src(core, lists_of(touch), 2, b, jnp.where(core == 0, 2, 4))
    scatter_src(core, lists_of(beyond), 1, b, jnp.where(core == 0, 6, 0))


def scatter_later_kernel(mine, ob, cn):
    core = lax.axis_index("core")
    scatter_rec(core, lists_of(mine), 2, 2, ob, cn, jnp.where(core == 0, 2, 0))


def scatter_late_kernel(theirs, beyond_m, beyond_t, ob_in, cn_in, ob, cn):
    core = lax.axis_index("core")
    scatter_rec(core, lists_of(theirs), 2, 2, ob, cn, jnp.where(core == 0, 0, 2))
    upper = either(core, (beyond_t, ROWS), (beyond_m, ROWS))
    scatter_rec(core, upper, 1, 1, ob, cn, 4)


def shift_matrix():
    i = lax.broadcasted_iota(jnp.int32, (128, 128), 0)
    j = lax.broadcasted_iota(jnp.int32, (128, 128), 1)
    return jnp.where(jnp.abs(i - j) == 1, 1.0, 0.0).astype(jnp.bfloat16)


def half(ref, t, c):
    return ref[t, LINES * c : LINES * c + LINES, :]


def next_line(x):
    sub = lax.broadcasted_iota(jnp.int32, (8, 128), 0)
    after = jnp.where(sub == 7, 0.0, pltpu.roll(x[:8], 7, 0))
    return jnp.concatenate([x[8:], after])


def beside(x):
    sub = lax.broadcasted_iota(jnp.int32, (8, 128), 0)
    before = jnp.where(sub == 0, 0.0, pltpu.roll(x[LINES - 8 :], 1, 0))
    across = jnp.concatenate([before, x[: LINES - 8]]) + next_line(x)
    turned, rest = x[:TURNED], x[TURNED:]
    lane = lax.broadcasted_iota(jnp.int32, turned.shape, 1)
    low = jnp.where(lane == 0, 0.0, pltpu.roll(turned, 1, 1))
    high = jnp.where(lane == 127, 0.0, pltpu.roll(turned, 127, 1))
    matrix = shift_matrix()
    coarse = rest.astype(jnp.bfloat16)
    fine = (rest - coarse.astype(jnp.float32)).astype(jnp.bfloat16)
    along = jnp.dot(coarse, matrix, preferred_element_type=jnp.float32)
    along = along + jnp.dot(fine, matrix, preferred_element_type=jnp.float32)
    return across + jnp.concatenate([low + high, along])


def fold(x):
    return jnp.sum(x.reshape(LINES // 8, 8, 128), 0)


def walk(first, last, body, carry):
    return lax.fori_loop(first, last, body, carry)


def nothing():
    return [jnp.zeros((8, 128), jnp.float32) for _ in range(HALF)]


def advance(src, s_off, inv, dst, d_off, first, last, dots):
    def body(t, carry):
        one, two = [], []
        for c in range(HALF):
            x = half(src, t - s_off, c)
            q = beside(x) + (half(src, t - s_off - 1, c) + half(src, t - s_off + 1, c))
            new = half(inv, t, c) * q
            dst[t - d_off, LINES * c : LINES * c + LINES, :] = new
            if dots:
                one.append(carry[0][c] + fold(x * q))
                two.append(carry[1][c] + fold(new * q))
        return (one, two) if dots else carry

    return walk(first, last, body, (nothing(), nothing()) if dots else 0)


def last_moment(src, off):
    def body(t, carry):
        out = []
        for c in range(HALF):
            x = half(src, t - off, c)
            lane = lax.broadcasted_iota(jnp.int32, x.shape, 1)
            along = jnp.where(lane == 127, 0.0, pltpu.roll(x, 127, 1))
            q = (next_line(x) + along) + half(src, t - off + 1, c)
            out.append(carry[c] + fold(x * q))
        return out

    return [2.0 * m for m in walk(4, 8, body, nothing())]


def message(moments):
    sub = lax.broadcasted_iota(jnp.int32, (8, 128), 0)
    lane = lax.broadcasted_iota(jnp.int32, (8, 128), 1)
    out = jnp.zeros((8, 128), jnp.float32)
    for k, moment in enumerate(moments):
        for c in range(HALF):
            total = jnp.sum(moment[c])
            out = out + jnp.where((sub == k) & (lane == c), total, 0.0)
    return out


def coefficients(terms):
    moments = (terms[0][...] + terms[1][...]) + (terms[2][...] + terms[3][...])
    m = [moments[k : k + 1, :] for k in range(6)]

    def product(p, shift):
        total = 0.0
        for i, a in enumerate(p):
            for j, b in enumerate(p):
                total = total + a * b * (m[i + j] - m[i + j + 1] if shift else m[i + j])
        return total

    one = jnp.ones_like(m[0])
    z, p, energy = [one], [one], m[0]
    x = [0.0 * one] * 3
    for it in range(3):
        stride = energy / product(p, True)
        x = [x[i] + (stride * p[i] if i < len(p) else 0.0) for i in range(3)]
        if it < 2:
            applied = [a - b for a, b in zip(p + [0.0 * one], [0.0 * one] + p)]
            z = [a - stride * b for a, b in zip(z + [0.0 * one], applied)]
            new = product(z, False)
            p = [a + new / energy * b for a, b in zip(z, p + [0.0 * one])]
            energy = new
    lane = lax.broadcasted_iota(jnp.int32, (1, 128), 1)
    return [[jnp.sum(jnp.where(lane == c, v, 0.0)) for c in range(HALF)] for v in x]


def fill_inverse(core, square, inv, slab, mine, theirs, valid):
    def fill(p, _):
        at = pl.multiple_of(p * 512, 512)
        here = mine[pl.ds(at, 512), :]
        there = theirs[pl.ds(at, 512), :]
        sigma = jnp.where(core == slab % 2, here, there)
        for c in range(HALF):
            inv[2 * slab + p, LINES * c : LINES * c + LINES, :] = valid / (6.0 + square[c] * sigma)
        return 0

    lax.fori_loop(0, 2, fill, 0)


def forward_own_kernel(damp, own_m, own_t, b_own, inv, v0, v1, held):
    core = lax.axis_index("core")
    square = squares(damp)
    for slab in (2, 3):
        fill_inverse(core, square, inv, slab, own_m, own_t, 1.0)

    def start(t, carry):
        out = []
        for c in range(HALF):
            right = half(b_own, t - 4, c)
            new = half(inv, t, c) * right
            v0[t, LINES * c : LINES * c + LINES, :] = new
            out.append(carry[c] + fold(new * right))
        return out

    m0 = walk(4, 8, start, nothing())
    m1, m2 = advance(v0, 0, inv, v1, 1, 5, 7, True)
    for k, part in enumerate(m0 + m1 + m2):
        held[8 * k : 8 * k + 8, :] = part


def forward_kernel(
    damp, touch_m, touch_t, beyond_m, beyond_t, b_near, held, inv_in, v0_in, v1_in,
    inv, v0, v1, v2, msg,
):
    pair, core = lax.axis_index("pair"), lax.axis_index("core")
    low = jnp.where(pair >= 1, 1.0, 0.0)
    high = jnp.where(pair + 1 < lax.axis_size("pair"), 1.0, 0.0)
    square = squares(damp)
    fill_inverse(core, square, inv, 0, beyond_m, beyond_t, low)
    fill_inverse(core, square, inv, 1, touch_m, touch_t, low)
    fill_inverse(core, square, inv, 4, touch_m, touch_t, high)
    fill_inverse(core, square, inv, 5, beyond_m, beyond_t, high)

    def start(off):
        def body(t, carry):
            v0[t] = inv[t] * b_near[t - off]
            return carry

        return body

    v0[12] = b_near[8]
    walk(0, 4, start(0), 0)
    walk(8, 12, start(4), 0)
    kept = [held[8 * k : 8 * k + 8, :] for k in range(3 * HALF)]
    advance(v0, 0, inv, v1, 1, 1, 4, False)
    lower = advance(v0, 0, inv, v1, 1, 4, 5, True)
    upper = advance(v0, 0, inv, v1, 1, 7, 8, True)
    advance(v0, 0, inv, v1, 1, 8, 12, False)
    m1 = [a + b + c for a, b, c in zip(lower[0], upper[0], kept[HALF : 2 * HALF])]
    m2 = [a + b + c for a, b, c in zip(lower[1], upper[1], kept[2 * HALF :])]
    advance(v1, 1, inv, v2, 2, 2, 4, False)
    m3, m4 = advance(v1, 1, inv, v2, 2, 4, 8, True)
    advance(v1, 1, inv, v2, 2, 8, 11, False)
    m5 = last_moment(v2, 2)
    msg[...] = message([kept[:HALF], m1, m2, m3, m4, m5])


def adjoint_kernel(
    t0, t1, t2, t3, inv, v0, v1, v2, ob_own, cn_own, ob_near, cn_near, wave, u0, u1, u2, msg
):
    a = coefficients((t0, t1, t2, t3))

    def start(ob, cn, off, own):
        def body(t, carry):
            out = []
            count = cn[t - off]
            for c in range(HALF):
                lines = slice(LINES * c, LINES * c + LINES)
                w = a[0][c] * half(v0, t, c) + a[1][c] * half(v1, t - 1, c)
                w = w + a[2][c] * half(v2, t - 2, c)
                right = count * w - half(ob, t - off, c)
                new = half(inv, t, c) * right
                u0[t, lines, :] = new
                if own:
                    wave[t - 4, lines, :] = w
                    out.append(carry[c] + fold(new * right))
            return out if own else carry

        return body

    walk(2, 4, start(ob_near, cn_near, 2, False), 0)
    m0 = walk(4, 8, start(ob_own, cn_own, 4, True), nothing())
    walk(8, 11, start(ob_near, cn_near, 6, False), 0)
    advance(u0, 0, inv, u1, 1, 3, 4, False)
    m1, m2 = advance(u0, 0, inv, u1, 1, 4, 8, True)
    advance(u0, 0, inv, u1, 1, 8, 10, False)
    m3, m4 = advance(u1, 1, inv, u2, 2, 4, 8, True)
    advance(u1, 1, inv, u2, 2, 8, 9, False)
    m5 = last_moment(u2, 2)
    msg[...] = message([m0, m1, m2, m3, m4, m5])


def gradient_kernel(other, damp, t0, t1, t2, t3, wave, u0, u1, u2, *rest):
    held = rest[-1]
    a = coefficients((t0, t1, t2, t3))
    a = [[-square * v for square, v in zip(squares(damp), one)] for one in a]
    core = lax.axis_index("core")
    core = 1 - core if other else core
    bands = rest[0] if other else rest[-2]
    for p in range(2):
        t = 4 + 2 * core + p
        total = 0.0
        for c in range(HALF):
            x = a[0][c] * half(u0, t, c) + a[1][c] * half(u1, t - 1, c) + a[2][c] * half(u2, t - 2, c)
            total = total + x * half(wave, t - 4, c)
        held[...] = total
        for s in range(8):
            band, rows = s // 2, slice(64 * (s % 2), 64 * (s % 2) + 64)
            part = held[pl.ds(s, 64, stride=8), :]
            bands[band, p, rows, :] = part if other else part + rest[0][band, p, rows, :]
    if not other:
        lap = lax.axis_index("lap")
        for d in range(4):
            rest[2 + d][:, 0:128, :] = bands[lap ^ d]
            rest[2 + d][:, 128:136, :] = rest[1][...]


def power_kernel(g0, g1, g2, g3, own, msg, prior_y):
    lap = lax.axis_index("lap")
    g = (g0[:, 0:128] + g1[:, 0:128]) + (g2[:, 0:128] + g3[:, 0:128])
    own[...] = g
    msg[...] = jnp.full((128, 128), jnp.sum(g * g), jnp.float32)
    before = jnp.where(lap == 2, g3[:, 128:136], g1[:, 128:136])
    prior_y[...] = jnp.where(lap == 0, 0.0, before)


def band_of(ref, lap):
    out = None
    for k in range(4):
        parts = [ref[pl.ds(2 * k + i, 64, stride=8), :] for i in range(2)]
        band = jnp.concatenate(parts)
        out = band if out is None else jnp.where(lap == k, band, out)
    return out


def variation_kernel(slow, own_t, touch_t, dual, dual_next, base, send_x, send_y):
    lap, pair, core = (lax.axis_index(name) for name in ("lap", "pair", "core"))
    start = pl.multiple_of(lap * 128, 128)
    band = pl.ds(start, 128)
    after = pl.ds(pl.multiple_of(jnp.minimum(start + 128, 504), 8), 8)
    row = lax.broadcasted_iota(jnp.int32, (128, 128), 0)
    lane = lax.broadcasted_iota(jnp.int32, (128, 128), 1)
    last_y = (row == 127) & (lap == 3)
    last_z = lane == 127
    comps = []
    for p in range(2):
        here = slow[p, band, :]
        if p == 0:
            step_x = slow[1, band, :] - here
        else:
            beyond = jnp.where(core == 0, band_of(own_t, lap), band_of(touch_t, lap))
            step_x = beyond - here
            step_x = jnp.where((core == 1) & (pair == 15), 0.0, step_x)
        rolled = pltpu.roll(here, 127, 0)
        step_y = jnp.where(row == 127, slow[p, after, :][0:1], rolled) - here
        step_y = jnp.where(last_y, 0.0, step_y)
        step_z = jnp.where(last_z, 0.0, pltpu.roll(here, 127, 1) - here)
        trial = [dual[k, p] + dual_step * step for k, step in enumerate((step_x, step_y, step_z))]
        magnitude = jnp.sqrt(trial[0] * trial[0] + trial[1] * trial[1] + trial[2] * trial[2])
        scale = jnp.maximum(1.0, magnitude / tv_weight)
        new = [x / scale for x in trial]
        for k in range(3):
            dual_next[k, p] = new[k]
        if p == 1:
            new[0] = jnp.where((core == 1) & (pair == 15), 0.0, new[0])
        new[1] = jnp.where(last_y, 0.0, new[1])
        new[2] = jnp.where(last_z, 0.0, new[2])
        comps.append(new)
    for p in range(2):
        x, y, z = comps[p]
        back = jnp.where(row == 0, 0.0, pltpu.roll(y, 1, 0)) - y
        back = back + (jnp.where(lane == 0, 0.0, pltpu.roll(z, 1, 1)) - z)
        back = back + (comps[0][0] - x if p == 1 else -x)
        base[p] = slow[p, band, :] - primal_step * back
        send_y[p] = y[120:128]
    send_x[0] = comps[1][0]


def model_kernel(cells, base, grad, power, prior_x, prior_y, model):
    total = power[0]
    for k in range(1, 16):
        total = total + power[k]
    total = jnp.sum(total, axis=0, keepdims=True)
    scale = 1.0 / jnp.sqrt(total / cells + 1e-06)
    row = lax.broadcasted_iota(jnp.int32, (128, 128), 0)
    for p in range(2):
        back = jnp.where(row == 0, prior_y[p][7:8], 0.0)
        if p == 0:
            back = back + prior_x[0]
        model[p] = base[p] - primal_step * (grad[p] * scale + back)


def cost(work):
    return pl.CostEstimate(flops=work * 10**7, bytes_accessed=10**4, transcendentals=0)


def struct(*shape):
    return jax.ShapeDtypeStruct(shape, jnp.float32)


def moved(x, axis, by):
    peers = lax.axis_size(axis)
    return lax.ppermute(x, axis, [(i, i + by) for i in range(peers) if 0 <= i + by < peers])


def swapped(x):
    return lax.ppermute(x, "core", [(0, 1), (1, 0)])


def others(x, masks):
    return [lax.ppermute(x, "pair", [(i, i ^ d) for i in range(16)]) for d in masks]


def stage_sum(x):
    return x + sum(others(x, (1, 2, 3)))


def stage_terms(x):
    return [x] + others(x, (4, 8, 12))


def scatter(kernel, name, work, inputs, shapes, into=()):
    scalars = 1 if inputs[0].ndim == 1 else 0
    first = len(inputs)
    return pl.pallas_call(
        kernel,
        out_shape=tuple(struct(*shape) for shape in shapes),
        in_specs=[SMEM] * scalars + [VMEM] * (len(inputs) - scalars + len(into)),
        out_specs=(VMEM,) * len(shapes),
        input_output_aliases={first + k: k for k in range(len(into))},
        compiler_params=params(8),
        cost_estimate=cost(work),
        name=name,
    )(*inputs, *into)


def on_device(slowness, damping, src_index, src_amp, rec_index, observed, dual):
    width_x, rows_y, depth_z = slowness.shape
    slab_cells = width_x * rows_y * depth_z
    pairs = lax.axis_size("pair")

    packed, lists = pl.pallas_call(
        pack_kernel,
        out_shape=(struct(SLAB, 128), struct(LIST, 128)),
        in_specs=[pl.BlockSpec(memory_space=pltpu.HBM)] * 5,
        out_specs=(VMEM,) * 2,
        scratch_shapes=[
            pltpu.VMEM((ROWS, 128), jnp.float32), pltpu.VMEM((8, 128), jnp.int32), pltpu.VMEM((8, 128), jnp.int32),
            pltpu.VMEM(src_amp.shape, jnp.float32), pltpu.VMEM(observed.shape, jnp.float32),
            pltpu.SemaphoreType.DMA((5,)),
        ],
        compiler_params=params(8),
        name="pack",
    )(
        *(
            pltpu.with_memory_space_constraint(x, pltpu.HBM)
            for x in (
                slowness.reshape(ROWS, 128), src_index.reshape(8, 128), rec_index.reshape(8, 128),
                src_amp, observed,
            )
        )
    )
    space, last = ("pair", "core"), 2 * pairs
    inward = [(i, i - 2) for i in range(2, last, 2)] + [(i, i + 2) for i in range(1, last - 2, 2)]
    outward = [(i, i + 2) for i in range(0, last - 2, 2)] + [(i, i - 2) for i in range(3, last, 2)]
    touch_m = lax.ppermute(packed, space, inward)
    beyond_m = lax.ppermute(packed, space, outward)
    own_t = swapped(packed)

    block, near_block = (4, ROWS, 128), (5, ROWS, 128)
    count, near_count = (4, LINES, 128), (5, LINES, 128)
    *own, first = scatter(
        scatter_other_kernel, "scatter_other", 5, (packed, own_t), [block, block, count, (LIST, 128)]
    )
    far_m = moved(first, "pair", -2)
    b_own, ob_own, cn_own = scatter(
        scatter_own_kernel, "scatter_own", 5, (lists, first), [block, block, count], own
    )
    inv, v0, v1, held = pl.pallas_call(
        forward_own_kernel,
        out_shape=(
            struct(PLANES, ROWS, 128), struct(13, ROWS, 128), struct(11, ROWS, 128),
            struct(48, 128),
        ),
        in_specs=[SMEM] + [VMEM] * 3,
        out_specs=(VMEM,) * 4,
        compiler_params=params(2),
        cost_estimate=cost(4),
        name="forward_own",
    )(damping, packed, own_t, b_own)
    touch_m, beyond_m, far_m, held = lax.optimization_barrier((touch_m, beyond_m, far_m, held))
    touch_t, beyond_t = swapped(touch_m), swapped(beyond_m)
    near_shape = [(9, ROWS, 128)]
    b_near, = scatter(
        scatter_mine_kernel, "scatter_mine", 4, (damping, touch_m, beyond_m, far_m), near_shape
    )
    touch_t, beyond_t, b_near = lax.optimization_barrier((touch_t, beyond_t, b_near))
    b_near, = scatter(
        scatter_theirs_kernel, "scatter_theirs", 3, (touch_t, beyond_t), near_shape, (b_near,)
    )

    inv, v0, v1, v2, msg = pl.pallas_call(
        forward_kernel,
        out_shape=(
            struct(PLANES, ROWS, 128), struct(13, ROWS, 128), struct(11, ROWS, 128),
            struct(9, ROWS, 128), struct(8, 128),
        ),
        in_specs=[SMEM] + [VMEM] * 9,
        out_specs=(VMEM,) * 5,
        input_output_aliases={7: 0, 8: 1, 9: 2},
        compiler_params=params(2),
        cost_estimate=cost(20),
        name="forward",
    )(damping, touch_m, touch_t, beyond_m, beyond_t, b_near, held, inv, v0, v1)

    touch_m, msg = lax.optimization_barrier((touch_m, msg))
    near = scatter(scatter_later_kernel, "scatter_later", 3, (touch_m,), [near_block, near_count])
    half_sum = stage_sum(msg)
    half_sum, near, touch_t = lax.optimization_barrier((half_sum, near, touch_t))
    ob_near, cn_near = scatter(
        scatter_late_kernel, "scatter_late", 4, (touch_t, beyond_m, beyond_t),
        [near_block, near_count], near,
    )
    wave, u0, u1, u2, msg = pl.pallas_call(
        adjoint_kernel,
        out_shape=(
            struct(4, ROWS, 128), struct(13, ROWS, 128), struct(11, ROWS, 128),
            struct(9, ROWS, 128), struct(8, 128),
        ),
        in_specs=[VMEM] * 12,
        out_specs=(VMEM,) * 5,
        input_output_aliases={5: 1, 6: 2, 7: 3},
        compiler_params=params(2),
        cost_estimate=cost(14),
        name="adjoint",
    )(*stage_terms(half_sum), inv, v0, v1, v2, ob_own, cn_own, ob_near, cn_near)

    terms = stage_terms(stage_sum(msg))

    def gradient(other, *more):
        scratch = [] if other else [pltpu.VMEM((4, 2, 128, 128), jnp.float32)]
        return pl.pallas_call(
            functools.partial(gradient_kernel, other),
            out_shape=struct(4, 2, 128, 128) if other else (struct(2, 136, 128),) * 4,
            in_specs=[SMEM] + [VMEM] * (8 + len(more)),
            out_specs=VMEM if other else (VMEM,) * 4,
            scratch_shapes=scratch + [pltpu.VMEM((LINES, 128), jnp.float32)],
            compiler_params=params(8),
            name="gradient",
        )(damping, *terms, wave, u0, u1, u2, *more)

    given = gradient(True)
    slowness, dual, own_t, touch_t, given = lax.optimization_barrier(
        (slowness, dual, own_t, touch_t, given)
    )
    dual_next, base, send_x, send_y = pl.pallas_call(
        variation_kernel,
        out_shape=(
            struct(3, 2, 128, 128), struct(2, 128, 128), struct(1, 128, 128), struct(2, 8, 128),
        ),
        in_specs=[VMEM] * 4,
        out_specs=(VMEM,) * 4,
        compiler_params=params(8),
        cost_estimate=cost(1),
        name="variation",
    )(slowness, own_t, touch_t, dual)
    bands = gradient(False, swapped(given), send_y)
    send_x, bands = lax.optimization_barrier((send_x, bands))
    arrived = [bands[0]] + [
        lax.ppermute(bands[d], "lap", [(i, i ^ d) for i in range(4)]) for d in (1, 2, 3)
    ]
    prior_x = moved(send_x, ("pair", "core"), 1)
    arrived, prior_x = lax.optimization_barrier((arrived, prior_x))
    own_grad, power, prior_y = pl.pallas_call(
        power_kernel,
        out_shape=(struct(2, 128, 128), struct(128, 128), struct(2, 8, 128)),
        in_specs=[VMEM] * 4,
        out_specs=(VMEM,) * 3,
        compiler_params=params(8),
        name="power",
    )(*arrived)
    power = lax.all_to_all(power, ("lap", "pair", "core"), 0, 0, tiled=True)
    model = pl.pallas_call(
        functools.partial(model_kernel, float(slab_cells * 2 * pairs)),
        out_shape=struct(2, 128, 128),
        in_specs=[VMEM] * 5,
        out_specs=VMEM,
        compiler_params=params(8),
        name="model",
    )(base, own_grad, power.reshape(16, 8, 128), prior_x, prior_y)
    return (model, dual_next)


def solution(mesh):
    space = mesh.devices.shape[1]
    mesh = Mesh(mesh.devices.reshape(-1, space // 2, 2), ("lap", "pair", "core"))
    both = ("pair", "core")
    in_specs = (
        P(both, None, None),
        P("lap"),
        P(both),
        P("lap", both),
        P(both),
        P("lap", both),
        P(None, both, "lap", None),
    )
    out_specs = (P(both, "lap", None), P(None, both, "lap", None))
    return jax.shard_map(
        on_device, mesh=mesh, in_specs=in_specs, out_specs=out_specs, check_vma=False
    )
```

```python
import functools

import jax
import jax.numpy as jnp
from jax import lax
from jax.experimental import pallas as pl
from jax.experimental.pallas import tpu as pltpu
from jax.sharding import Mesh
from jax.sharding import PartitionSpec as P


HALF = 2
PLANES = 13
LINES = 512
ROWS = HALF * LINES
TURNED = 192
LIST = 88
SLAB = ROWS + LIST

dual_step = 0.5
primal_step = 0.2
tv_weight = 0.5

VMEM = pl.BlockSpec(memory_space=pltpu.VMEM)
SMEM = pl.BlockSpec(memory_space=pltpu.SMEM)


def params(mib):
    return pltpu.CompilerParams(vmem_limit_bytes=mib * 2**20)


def line_of(row):
    return (row & 63) * 8 + (row >> 6)


def spread_points(index, parts, right_planes, write):
    points = index.shape[1]
    column = (index >> 16) * 128 + (index & 127)
    line = line_of((index >> 7) & 511)
    lines = LINES
    if right_planes == 1:
        lines = LINES // 2
        column = jnp.where(index >> 16 == 0, (line >> 8) * 128 + (index & 127), -1)
        line = line & 255
    lanes = lax.broadcasted_iota(jnp.int32, (256, points), 0)
    right = jnp.where(lanes == column, 1.0, 0.0).astype(jnp.bfloat16)
    mask = lax.broadcasted_iota(jnp.int32, (lines, points), 0) == line
    for which, part in enumerate(parts):
        total = None
        for piece in zip(*part):
            left = [jnp.where(mask, value, 0.0).astype(jnp.bfloat16) for value in piece]
            got = lax.dot_general(
                jnp.concatenate(left), right, (((1,), (1,)), ((), ())),
                preferred_element_type=jnp.float32,
            )
            total = got if total is None else total + got
        for c in range(len(part)):
            rows = total[lines * c : lines * c + lines]
            lower, upper = rows[:, 0:128], rows[:, 128:256]
            if right_planes == 1:
                write(which, 0, c, jnp.concatenate([lower, upper]))
            else:
                write(which, 0, c, lower)
                write(which, 1, c, upper)


def pieces_of(value, count):
    high = value.astype(jnp.bfloat16).astype(jnp.float32)
    return [high, value - high][:count]


def list_row(ref, base, i):
    block = ref[base + 8 * i : base + 8 * i + 8, :]
    return jnp.concatenate([block[j : j + 1] for j in range(8)], 1)


def either(core, zero, one):
    return lambda i: jnp.where(core == 0, list_row(*zero, i), list_row(*one, i))


def points_of(core, row, first):
    return [jnp.where(core == 0, row(first + c), row(first + HALF + c)) for c in range(HALF)]


def writer(stores):
    def write(which, p, c, value):
        ref, first = stores[which]
        ref[first + p, LINES * c : LINES * c + LINES, :] = value

    return write


def scatter_src(core, row, count, store, first, divisor=None, planes=2):
    amp = points_of(core, row, 2)
    if divisor is not None:
        amp = [a / d for a, d in zip(amp, divisor)]
    index = row(0).astype(jnp.int32)
    spread_points(index, [[pieces_of(a, count) for a in amp]], planes, writer([(store, first)]))


def scatter_rec(core, row, count, planes, ob, cn, first):
    obs = points_of(core, row, 6)
    parts = [[pieces_of(o, count) for o in obs], [[jnp.ones_like(obs[0])]]]
    index = row(1).astype(jnp.int32)
    spread_points(index, parts, planes, writer([(ob, first), (cn, first)]))


def squares(damp):
    core = lax.axis_index("core")
    first, second = damp[HALF * core], damp[HALF * core + 1]
    return first * first, second * second


def diagonal_at(damp, row):
    sigma = row(10)
    return [6.0 + square * sigma for square in squares(damp)]


def pack_kernel(slow_in, src_in, rec_in, amp_in, obs_in, out, far, slow, src, rec, amp, obs, sem):
    slab = lax.axis_index("pair") * 2 + lax.axis_index("core")
    offset = slab * (2 * 512 * 128)
    pairs = ((src_in, src), (rec_in, rec), (amp_in, amp), (obs_in, obs), (slow_in, slow))
    copies = [pltpu.make_async_copy(x, y, sem.at[k]) for k, (x, y) in enumerate(pairs)]
    for copy in copies[::-1]:
        copy.start()
    for copy in copies[:4]:
        copy.wait()
    far[80:88, :] = jnp.zeros((8, 128), jnp.float32)
    points = amp.shape[1]
    far[0:8, :] = (src[...] - offset).astype(jnp.float32)
    far[8:16, :] = (rec[...] - offset).astype(jnp.float32)
    for k, values in ((2, amp), (6, obs)):
        for i in range(4):
            for j in range(8):
                at = 8 * (k + i) + j
                far[at : at + 1, :] = values[i : i + 1, 128 * j : 128 * j + 128]
    out[ROWS : ROWS + LIST, :] = far[...]
    for copy in copies[4:]:
        copy.wait()
    for p in range(2):
        for j in range(64):
            at = LINES * p + 8 * j
            out[at : at + 8, :] = slow[pl.ds(LINES * p + j, 8, stride=64), :]


def gather_sigma(sigma, row, store):
    index = row(0).astype(jnp.int32)
    points = index.shape[1]
    rows = lax.broadcasted_iota(jnp.int32, (ROWS, points), 0)
    line = (index >> 16) * LINES + line_of((index >> 7) & 511)
    pick = jnp.where(rows == line, 1.0, 0.0).astype(jnp.bfloat16)
    high = sigma.astype(jnp.bfloat16)
    low = (sigma - high.astype(jnp.float32)).astype(jnp.bfloat16)
    dims = (((0,), (0,)), ((), ()))
    got = lax.dot_general(high, pick, dims, preferred_element_type=jnp.float32)
    got = got + lax.dot_general(low, pick, dims, preferred_element_type=jnp.float32)
    lane = lax.broadcasted_iota(jnp.int32, (128, points), 0)
    found = jnp.sum(jnp.where(lane == index & 127, got, 0.0), axis=0, keepdims=True)
    for j in range(8):
        store[80 + j : 81 + j, :] = found[:, 128 * j : 128 * j + 128]


def scatter_slab(h, row, b, ob, cn):
    core = lax.axis_index("core")
    scatter_src(core, row, 2, b, 2 * h)
    scatter_rec(core, row, 2, 2, ob, cn, 2 * h)


def scatter_other_kernel(mine, other, b, ob, cn, first):
    core = lax.axis_index("core")
    whole = jnp.where(core == 0, mine[...], other[...])
    first[...] = whole[ROWS:SLAB]
    gather_sigma(whole[0:ROWS], functools.partial(list_row, first, 0), first)
    row = functools.partial(list_row, other, ROWS)
    scatter_slab(1 - lax.axis_index("core"), row, b, ob, cn)


def scatter_own_kernel(lists, first_in, b_in, ob_in, cn_in, b, ob, cn):
    scatter_slab(lax.axis_index("core"), functools.partial(list_row, lists, 0), b, ob, cn)


def lists_of(ref):
    return functools.partial(list_row, ref, ROWS)


def scatter_mine_kernel(damp, touch, beyond, far, b):
    core = lax.axis_index("core")
    scatter_src(core, lists_of(touch), 2, b, jnp.where(core == 0, 4, 2))
    scatter_src(core, lists_of(beyond), 1, b, jnp.where(core == 0, 0, 6))
    last = functools.partial(list_row, far, 0)
    scatter_src(core, last, 1, b, 8, diagonal_at(damp, last), 1)


def scatter_theirs_kernel(touch, beyond, b_in, b):
    core = lax.axis_index("core")
    scatter_src(core, lists_of(touch), 2, b, jnp.where(core == 0, 2, 4))
    scatter_src(core, lists_of(beyond), 1, b, jnp.where(core == 0, 6, 0))


def scatter_later_kernel(mine, ob, cn):
    core = lax.axis_index("core")
    scatter_rec(core, lists_of(mine), 2, 2, ob, cn, jnp.where(core == 0, 2, 0))


def scatter_late_kernel(theirs, beyond_m, beyond_t, ob_in, cn_in, ob, cn):
    core = lax.axis_index("core")
    scatter_rec(core, lists_of(theirs), 2, 2, ob, cn, jnp.where(core == 0, 0, 2))
    upper = either(core, (beyond_t, ROWS), (beyond_m, ROWS))
    scatter_rec(core, upper, 1, 1, ob, cn, 4)


def shift_matrix():
    i = lax.broadcasted_iota(jnp.int32, (128, 128), 0)
    j = lax.broadcasted_iota(jnp.int32, (128, 128), 1)
    return jnp.where(jnp.abs(i - j) == 1, 1.0, 0.0).astype(jnp.bfloat16)


def half(ref, t, c):
    return ref[t, LINES * c : LINES * c + LINES, :]


def next_line(x):
    sub = lax.broadcasted_iota(jnp.int32, (8, 128), 0)
    after = jnp.where(sub == 7, 0.0, pltpu.roll(x[:8], 7, 0))
    return jnp.concatenate([x[8:], after])


def beside(x):
    sub = lax.broadcasted_iota(jnp.int32, (8, 128), 0)
    before = jnp.where(sub == 0, 0.0, pltpu.roll(x[LINES - 8 :], 1, 0))
    across = jnp.concatenate([before, x[: LINES - 8]]) + next_line(x)
    turned, rest = x[:TURNED], x[TURNED:]
    lane = lax.broadcasted_iota(jnp.int32, turned.shape, 1)
    low = jnp.where(lane == 0, 0.0, pltpu.roll(turned, 1, 1))
    high = jnp.where(lane == 127, 0.0, pltpu.roll(turned, 127, 1))
    matrix = shift_matrix()
    coarse = rest.astype(jnp.bfloat16)
    fine = (rest - coarse.astype(jnp.float32)).astype(jnp.bfloat16)
    along = jnp.dot(coarse, matrix, preferred_element_type=jnp.float32)
    along = along + jnp.dot(fine, matrix, preferred_element_type=jnp.float32)
    return across + jnp.concatenate([low + high, along])


def fold(x):
    return jnp.sum(x.reshape(LINES // 8, 8, 128), 0)


def walk(first, last, body, carry, unroll=False):
    return lax.fori_loop(first, last, body, carry, unroll=unroll)


def nothing():
    return [jnp.zeros((8, 128), jnp.float32) for _ in range(HALF)]


def advance(src, s_off, inv, dst, d_off, first, last, dots, unroll=False):
    def body(t, carry):
        one, two = [], []
        for c in range(HALF):
            x = half(src, t - s_off, c)
            q = beside(x) + (half(src, t - s_off - 1, c) + half(src, t - s_off + 1, c))
            new = half(inv, t, c) * q
            dst[t - d_off, LINES * c : LINES * c + LINES, :] = new
            if dots:
                one.append(carry[0][c] + fold(x * q))
                two.append(carry[1][c] + fold(new * q))
        return (one, two) if dots else carry

    return walk(first, last, body, (nothing(), nothing()) if dots else 0, unroll)


def last_moment(src, off):
    def body(t, carry):
        out = []
        for c in range(HALF):
            x = half(src, t - off, c)
            lane = lax.broadcasted_iota(jnp.int32, x.shape, 1)
            along = jnp.where(lane == 127, 0.0, pltpu.roll(x, 127, 1))
            q = (next_line(x) + along) + half(src, t - off + 1, c)
            out.append(carry[c] + fold(x * q))
        return out

    return [2.0 * m for m in walk(4, 8, body, nothing())]


def message(moments):
    sub = lax.broadcasted_iota(jnp.int32, (8, 128), 0)
    lane = lax.broadcasted_iota(jnp.int32, (8, 128), 1)
    out = jnp.zeros((8, 128), jnp.float32)
    for k, moment in enumerate(moments):
        for c in range(HALF):
            total = jnp.sum(moment[c])
            out = out + jnp.where((sub == k) & (lane == c), total, 0.0)
    return out


def coefficients(terms):
    moments = (terms[0][...] + terms[1][...]) + (terms[2][...] + terms[3][...])
    m = [moments[k : k + 1, :] for k in range(6)]

    def product(p, shift):
        total = 0.0
        for i, a in enumerate(p):
            for j, b in enumerate(p):
                total = total + a * b * (m[i + j] - m[i + j + 1] if shift else m[i + j])
        return total

    one = jnp.ones_like(m[0])
    z, p, energy = [one], [one], m[0]
    x = [0.0 * one] * 3
    for it in range(3):
        stride = energy / product(p, True)
        x = [x[i] + (stride * p[i] if i < len(p) else 0.0) for i in range(3)]
        if it < 2:
            applied = [a - b for a, b in zip(p + [0.0 * one], [0.0 * one] + p)]
            z = [a - stride * b for a, b in zip(z + [0.0 * one], applied)]
            new = product(z, False)
            p = [a + new / energy * b for a, b in zip(z, p + [0.0 * one])]
            energy = new
    lane = lax.broadcasted_iota(jnp.int32, (1, 128), 1)
    return [[jnp.sum(jnp.where(lane == c, v, 0.0)) for c in range(HALF)] for v in x]


def fill_inverse(core, square, inv, slab, mine, theirs, valid):
    def fill(p, _):
        at = pl.multiple_of(p * 512, 512)
        here = mine[pl.ds(at, 512), :]
        there = theirs[pl.ds(at, 512), :]
        sigma = jnp.where(core == slab % 2, here, there)
        for c in range(HALF):
            inv[2 * slab + p, LINES * c : LINES * c + LINES, :] = valid / (6.0 + square[c] * sigma)
        return 0

    lax.fori_loop(0, 2, fill, 0)


def forward_own_kernel(damp, own_m, own_t, b_own, inv, v0, v1, held):
    core = lax.axis_index("core")
    square = squares(damp)
    for slab in (2, 3):
        fill_inverse(core, square, inv, slab, own_m, own_t, 1.0)

    def start(t, carry):
        out = []
        for c in range(HALF):
            right = half(b_own, t - 4, c)
            new = half(inv, t, c) * right
            v0[t, LINES * c : LINES * c + LINES, :] = new
            out.append(carry[c] + fold(new * right))
        return out

    m0 = walk(4, 8, start, nothing())
    m1, m2 = advance(v0, 0, inv, v1, 1, 5, 7, True)
    for k, part in enumerate(m0 + m1 + m2):
        held[8 * k : 8 * k + 8, :] = part


def forward_kernel(
    damp, touch_m, touch_t, beyond_m, beyond_t, b_near, held, inv_in, v0_in, v1_in,
    inv, v0, v1, v2, msg,
):
    pair, core = lax.axis_index("pair"), lax.axis_index("core")
    low = jnp.where(pair >= 1, 1.0, 0.0)
    high = jnp.where(pair + 1 < lax.axis_size("pair"), 1.0, 0.0)
    square = squares(damp)
    fill_inverse(core, square, inv, 0, beyond_m, beyond_t, low)
    fill_inverse(core, square, inv, 1, touch_m, touch_t, low)
    fill_inverse(core, square, inv, 4, touch_m, touch_t, high)
    fill_inverse(core, square, inv, 5, beyond_m, beyond_t, high)

    def start(off):
        def body(t, carry):
            v0[t] = inv[t] * b_near[t - off]
            return carry

        return body

    v0[12] = b_near[8] * jnp.where(pair + 2 < lax.axis_size("pair"), 1.0, 0.0)
    walk(0, 4, start(0), 0)
    walk(8, 12, start(4), 0)
    kept = [held[8 * k : 8 * k + 8, :] for k in range(3 * HALF)]
    advance(v0, 0, inv, v1, 1, 1, 4, False, True)
    lower = advance(v0, 0, inv, v1, 1, 4, 5, True, True)
    upper = advance(v0, 0, inv, v1, 1, 7, 8, True, True)
    advance(v0, 0, inv, v1, 1, 8, 12, False, True)
    m1 = [a + b + c for a, b, c in zip(lower[0], upper[0], kept[HALF : 2 * HALF])]
    m2 = [a + b + c for a, b, c in zip(lower[1], upper[1], kept[2 * HALF :])]
    advance(v1, 1, inv, v2, 2, 2, 4, False, True)
    m3, m4 = advance(v1, 1, inv, v2, 2, 4, 8, True, True)
    advance(v1, 1, inv, v2, 2, 8, 11, False, True)
    m5 = last_moment(v2, 2)
    msg[...] = message([kept[:HALF], m1, m2, m3, m4, m5])


def adjoint_kernel(
    t0, t1, t2, t3, inv, v0, v1, v2, ob_own, cn_own, ob_near, cn_near, wave, u0, u1, u2, msg
):
    a = coefficients((t0, t1, t2, t3))

    def start(ob, cn, off, own):
        def body(t, carry):
            out = []
            count = cn[t - off]
            for c in range(HALF):
                lines = slice(LINES * c, LINES * c + LINES)
                w = a[0][c] * half(v0, t, c) + a[1][c] * half(v1, t - 1, c)
                w = w + a[2][c] * half(v2, t - 2, c)
                right = count * w - half(ob, t - off, c)
                new = half(inv, t, c) * right
                u0[t, lines, :] = new
                if own:
                    wave[t - 4, lines, :] = w
                    out.append(carry[c] + fold(new * right))
            return out if own else carry

        return body

    walk(2, 4, start(ob_near, cn_near, 2, False), 0)
    m0 = walk(4, 8, start(ob_own, cn_own, 4, True), nothing())
    walk(8, 11, start(ob_near, cn_near, 6, False), 0)
    advance(u0, 0, inv, u1, 1, 3, 4, False, True)
    m1, m2 = advance(u0, 0, inv, u1, 1, 4, 8, True, True)
    advance(u0, 0, inv, u1, 1, 8, 10, False, True)
    m3, m4 = advance(u1, 1, inv, u2, 2, 4, 8, True, True)
    advance(u1, 1, inv, u2, 2, 8, 9, False, True)
    m5 = last_moment(u2, 2)
    msg[...] = message([m0, m1, m2, m3, m4, m5])


def gradient_kernel(other, damp, t0, t1, t2, t3, wave, u0, u1, u2, *rest):
    held = rest[-1]
    a = coefficients((t0, t1, t2, t3))
    a = [[-square * v for square, v in zip(squares(damp), one)] for one in a]
    core = lax.axis_index("core")
    core = 1 - core if other else core
    bands = rest[0] if other else rest[-2]
    for p in range(2):
        t = 4 + 2 * core + p
        total = 0.0
        for c in range(HALF):
            x = a[0][c] * half(u0, t, c) + a[1][c] * half(u1, t - 1, c) + a[2][c] * half(u2, t - 2, c)
            total = total + x * half(wave, t - 4, c)
        held[...] = total
        for s in range(8):
            band, rows = s // 2, slice(64 * (s % 2), 64 * (s % 2) + 64)
            part = held[pl.ds(s, 64, stride=8), :]
            bands[band, p, rows, :] = part if other else part + rest[0][band, p, rows, :]
    if not other:
        lap = lax.axis_index("lap")
        for d in range(4):
            rest[2 + d][:, 0:128, :] = bands[lap ^ d]
            rest[2 + d][:, 128:136, :] = rest[1][...]


def power_kernel(g0, g1, g2, g3, own, msg, prior_y):
    lap = lax.axis_index("lap")
    g = (g0[:, 0:128] + g1[:, 0:128]) + (g2[:, 0:128] + g3[:, 0:128])
    own[...] = g
    msg[...] = jnp.full((128, 128), jnp.sum(g * g), jnp.float32)
    before = jnp.where(lap == 2, g3[:, 128:136], g1[:, 128:136])
    prior_y[...] = jnp.where(lap == 0, 0.0, before)


def band_of(ref, lap):
    out = None
    for k in range(4):
        parts = [ref[pl.ds(2 * k + i, 64, stride=8), :] for i in range(2)]
        band = jnp.concatenate(parts)
        out = band if out is None else jnp.where(lap == k, band, out)
    return out


def variation_kernel(slow, own_t, touch_t, dual, dual_next, base, send_x, send_y):
    lap, pair, core = (lax.axis_index(name) for name in ("lap", "pair", "core"))
    start = pl.multiple_of(lap * 128, 128)
    band = pl.ds(start, 128)
    after = pl.ds(pl.multiple_of(jnp.minimum(start + 128, 504), 8), 8)
    row = lax.broadcasted_iota(jnp.int32, (128, 128), 0)
    lane = lax.broadcasted_iota(jnp.int32, (128, 128), 1)
    last_y = (row == 127) & (lap == 3)
    last_z = lane == 127
    comps = []
    for p in range(2):
        here = slow[p, band, :]
        if p == 0:
            step_x = slow[1, band, :] - here
        else:
            beyond = jnp.where(core == 0, band_of(own_t, lap), band_of(touch_t, lap))
            step_x = beyond - here
            step_x = jnp.where((core == 1) & (pair == 15), 0.0, step_x)
        rolled = pltpu.roll(here, 127, 0)
        step_y = jnp.where(row == 127, slow[p, after, :][0:1], rolled) - here
        step_y = jnp.where(last_y, 0.0, step_y)
        step_z = jnp.where(last_z, 0.0, pltpu.roll(here, 127, 1) - here)
        trial = [dual[k, p] + dual_step * step for k, step in enumerate((step_x, step_y, step_z))]
        magnitude = jnp.sqrt(trial[0] * trial[0] + trial[1] * trial[1] + trial[2] * trial[2])
        scale = jnp.maximum(1.0, magnitude / tv_weight)
        new = [x / scale for x in trial]
        for k in range(3):
            dual_next[k, p] = new[k]
        if p == 1:
            new[0] = jnp.where((core == 1) & (pair == 15), 0.0, new[0])
        new[1] = jnp.where(last_y, 0.0, new[1])
        new[2] = jnp.where(last_z, 0.0, new[2])
        comps.append(new)
    for p in range(2):
        x, y, z = comps[p]
        back = jnp.where(row == 0, 0.0, pltpu.roll(y, 1, 0)) - y
        back = back + (jnp.where(lane == 0, 0.0, pltpu.roll(z, 1, 1)) - z)
        back = back + (comps[0][0] - x if p == 1 else -x)
        base[p] = slow[p, band, :] - primal_step * back
        send_y[p] = y[120:128]
    send_x[0] = comps[1][0]


def model_kernel(cells, base, grad, power, prior_x, prior_y, model):
    total = power[0]
    for k in range(1, 16):
        total = total + power[k]
    total = jnp.sum(total, axis=0, keepdims=True)
    scale = 1.0 / jnp.sqrt(total / cells + 1e-06)
    row = lax.broadcasted_iota(jnp.int32, (128, 128), 0)
    for p in range(2):
        back = jnp.where(row == 0, prior_y[p][7:8], 0.0)
        if p == 0:
            first = (lax.axis_index("pair") == 0) & (lax.axis_index("core") == 0)
            back = back + jnp.where(first, 0.0, prior_x[0])
        model[p] = base[p] - primal_step * (grad[p] * scale + back)


def cost(work):
    return pl.CostEstimate(flops=work * 10**7, bytes_accessed=10**4, transcendentals=0)


def struct(*shape):
    return jax.ShapeDtypeStruct(shape, jnp.float32)


def moved(x, axis, by):
    peers = lax.axis_size(axis)
    return lax.ppermute(x, axis, [(i, (i + by) % peers) for i in range(peers)])


def swapped(x):
    return lax.ppermute(x, "core", [(0, 1), (1, 0)])


def others(x, masks):
    return [lax.ppermute(x, "pair", [(i, i ^ d) for i in range(16)]) for d in masks]


def stage_sum(x):
    return x + sum(others(x, (1, 2, 3)))


def stage_terms(x):
    return [x] + others(x, (4, 8, 12))


def scatter(kernel, name, work, inputs, shapes, into=()):
    scalars = 1 if inputs[0].ndim == 1 else 0
    first = len(inputs)
    return pl.pallas_call(
        kernel,
        out_shape=tuple(struct(*shape) for shape in shapes),
        in_specs=[SMEM] * scalars + [VMEM] * (len(inputs) - scalars + len(into)),
        out_specs=(VMEM,) * len(shapes),
        input_output_aliases={first + k: k for k in range(len(into))},
        compiler_params=params(8),
        cost_estimate=cost(work),
        name=name,
    )(*inputs, *into)


def on_device(slowness, damping, src_index, src_amp, rec_index, observed, dual):
    width_x, rows_y, depth_z = slowness.shape
    slab_cells = width_x * rows_y * depth_z
    pairs = lax.axis_size("pair")

    packed, lists = pl.pallas_call(
        pack_kernel,
        out_shape=(struct(SLAB, 128), struct(LIST, 128)),
        in_specs=[pl.BlockSpec(memory_space=pltpu.HBM)] * 5,
        out_specs=(VMEM,) * 2,
        scratch_shapes=[
            pltpu.VMEM((ROWS, 128), jnp.float32), pltpu.VMEM((8, 128), jnp.int32), pltpu.VMEM((8, 128), jnp.int32),
            pltpu.VMEM(src_amp.shape, jnp.float32), pltpu.VMEM(observed.shape, jnp.float32),
            pltpu.SemaphoreType.DMA((5,)),
        ],
        compiler_params=params(8),
        name="pack",
    )(
        *(
            pltpu.with_memory_space_constraint(x, pltpu.HBM)
            for x in (
                slowness.reshape(ROWS, 128), src_index.reshape(8, 128), rec_index.reshape(8, 128),
                src_amp, observed,
            )
        )
    )
    space, last = ("pair", "core"), 2 * pairs
    inward = [(i, (i + 2 * (-1, 1)[i % 2]) % last) for i in range(last)]
    outward = [(i, (i + 2 * (1, -1)[i % 2]) % last) for i in range(last)]
    touch_m = lax.ppermute(packed, space, inward)
    beyond_m = lax.ppermute(packed, space, outward)
    own_t = swapped(packed)

    block, near_block = (4, ROWS, 128), (5, ROWS, 128)
    count, near_count = (4, LINES, 128), (5, LINES, 128)
    *own, first = scatter(
        scatter_other_kernel, "scatter_other", 5, (packed, own_t), [block, block, count, (LIST, 128)]
    )
    far_m = moved(first, "pair", -2)
    b_own, ob_own, cn_own = scatter(
        scatter_own_kernel, "scatter_own", 5, (lists, first), [block, block, count], own
    )
    inv, v0, v1, held = pl.pallas_call(
        forward_own_kernel,
        out_shape=(
            struct(PLANES, ROWS, 128), struct(13, ROWS, 128), struct(11, ROWS, 128),
            struct(48, 128),
        ),
        in_specs=[SMEM] + [VMEM] * 3,
        out_specs=(VMEM,) * 4,
        compiler_params=params(2),
        cost_estimate=cost(4),
        name="forward_own",
    )(damping, packed, own_t, b_own)
    touch_m, beyond_m, far_m, held = lax.optimization_barrier((touch_m, beyond_m, far_m, held))
    touch_t, beyond_t = swapped(touch_m), swapped(beyond_m)
    near_shape = [(9, ROWS, 128)]
    b_near, = scatter(
        scatter_mine_kernel, "scatter_mine", 4, (damping, touch_m, beyond_m, far_m), near_shape
    )
    touch_t, beyond_t, b_near = lax.optimization_barrier((touch_t, beyond_t, b_near))
    b_near, = scatter(
        scatter_theirs_kernel, "scatter_theirs", 3, (touch_t, beyond_t), near_shape, (b_near,)
    )

    inv, v0, v1, v2, msg = pl.pallas_call(
        forward_kernel,
        out_shape=(
            struct(PLANES, ROWS, 128), struct(13, ROWS, 128), struct(11, ROWS, 128),
            struct(9, ROWS, 128), struct(8, 128),
        ),
        in_specs=[SMEM] + [VMEM] * 9,
        out_specs=(VMEM,) * 5,
        input_output_aliases={7: 0, 8: 1, 9: 2},
        compiler_params=params(2),
        cost_estimate=cost(20),
        name="forward",
    )(damping, touch_m, touch_t, beyond_m, beyond_t, b_near, held, inv, v0, v1)

    touch_m, msg = lax.optimization_barrier((touch_m, msg))
    near = scatter(scatter_later_kernel, "scatter_later", 3, (touch_m,), [near_block, near_count])
    half_sum = stage_sum(msg)
    half_sum, near, touch_t = lax.optimization_barrier((half_sum, near, touch_t))
    ob_near, cn_near = scatter(
        scatter_late_kernel, "scatter_late", 4, (touch_t, beyond_m, beyond_t),
        [near_block, near_count], near,
    )
    wave, u0, u1, u2, msg = pl.pallas_call(
        adjoint_kernel,
        out_shape=(
            struct(4, ROWS, 128), struct(13, ROWS, 128), struct(11, ROWS, 128),
            struct(9, ROWS, 128), struct(8, 128),
        ),
        in_specs=[VMEM] * 12,
        out_specs=(VMEM,) * 5,
        input_output_aliases={5: 1, 6: 2, 7: 3},
        compiler_params=params(2),
        cost_estimate=cost(14),
        name="adjoint",
    )(*stage_terms(half_sum), inv, v0, v1, v2, ob_own, cn_own, ob_near, cn_near)

    terms = stage_terms(stage_sum(msg))

    def gradient(other, *more):
        scratch = [] if other else [pltpu.VMEM((4, 2, 128, 128), jnp.float32)]
        return pl.pallas_call(
            functools.partial(gradient_kernel, other),
            out_shape=struct(4, 2, 128, 128) if other else (struct(2, 136, 128),) * 4,
            in_specs=[SMEM] + [VMEM] * (8 + len(more)),
            out_specs=VMEM if other else (VMEM,) * 4,
            scratch_shapes=scratch + [pltpu.VMEM((LINES, 128), jnp.float32)],
            compiler_params=params(8),
            name="gradient",
        )(damping, *terms, wave, u0, u1, u2, *more)

    given = gradient(True)
    slowness, dual, own_t, touch_t, given = lax.optimization_barrier(
        (slowness, dual, own_t, touch_t, given)
    )
    dual_next, base, send_x, send_y = pl.pallas_call(
        variation_kernel,
        out_shape=(
            struct(3, 2, 128, 128), struct(2, 128, 128), struct(1, 128, 128), struct(2, 8, 128),
        ),
        in_specs=[VMEM] * 4,
        out_specs=(VMEM,) * 4,
        compiler_params=params(8),
        cost_estimate=cost(1),
        name="variation",
    )(slowness, own_t, touch_t, dual)
    bands = gradient(False, swapped(given), send_y)
    send_x, bands = lax.optimization_barrier((send_x, bands))
    arrived = [bands[0]] + [
        lax.ppermute(bands[d], "lap", [(i, i ^ d) for i in range(4)]) for d in (1, 2, 3)
    ]
    prior_x = moved(send_x, ("pair", "core"), 1)
    arrived, prior_x = lax.optimization_barrier((arrived, prior_x))
    own_grad, power, prior_y = pl.pallas_call(
        power_kernel,
        out_shape=(struct(2, 128, 128), struct(128, 128), struct(2, 8, 128)),
        in_specs=[VMEM] * 4,
        out_specs=(VMEM,) * 3,
        compiler_params=params(8),
        name="power",
    )(*arrived)
    power = lax.all_to_all(power, ("lap", "pair", "core"), 0, 0, tiled=True)
    model = pl.pallas_call(
        functools.partial(model_kernel, float(slab_cells * 2 * pairs)),
        out_shape=struct(2, 128, 128),
        in_specs=[VMEM] * 5,
        out_specs=VMEM,
        compiler_params=params(8),
        name="model",
    )(base, own_grad, power.reshape(16, 8, 128), prior_x, prior_y)
    return (model, dual_next)


def solution(mesh):
    space = mesh.devices.shape[1]
    mesh = Mesh(mesh.devices.reshape(-1, space // 2, 2), ("lap", "pair", "core"))
    both = ("pair", "core")
    in_specs = (
        P(both, None, None),
        P("lap"),
        P(both),
        P("lap", both),
        P(both),
        P("lap", both),
        P(None, both, "lap", None),
    )
    out_specs = (P(both, "lap", None), P(None, both, "lap", None))
    return jax.shard_map(
        on_device, mesh=mesh, in_specs=in_specs, out_specs=out_specs, check_vma=False
    )
```

```python
import functools

import jax
import jax.numpy as jnp
from jax import lax
from jax.experimental import pallas as pl
from jax.experimental.pallas import tpu as pltpu
from jax.sharding import Mesh
from jax.sharding import PartitionSpec as P


HALF = 2
PLANES = 13
LINES = 512
ROWS = HALF * LINES
TURNED = 192
LIST = 88
SLAB = ROWS + LIST

dual_step = 0.5
primal_step = 0.2
tv_weight = 0.5

VMEM = pl.BlockSpec(memory_space=pltpu.VMEM)
SMEM = pl.BlockSpec(memory_space=pltpu.SMEM)


def params(mib):
    return pltpu.CompilerParams(vmem_limit_bytes=mib * 2**20)


def line_of(row):
    return (row & 63) * 8 + (row >> 6)


def spread_points(index, parts, right_planes, write):
    points = index.shape[1]
    column = (index >> 16) * 128 + (index & 127)
    line = line_of((index >> 7) & 511)
    lines = LINES
    if right_planes == 1:
        lines = LINES // 2
        column = jnp.where(index >> 16 == 0, (line >> 8) * 128 + (index & 127), -1)
        line = line & 255
    lanes = lax.broadcasted_iota(jnp.int32, (256, points), 0)
    right = jnp.where(lanes == column, 1.0, 0.0).astype(jnp.bfloat16)
    mask = lax.broadcasted_iota(jnp.int32, (lines, points), 0) == line
    for which, part in enumerate(parts):
        total = None
        for piece in zip(*part):
            left = [jnp.where(mask, value, 0.0).astype(jnp.bfloat16) for value in piece]
            got = lax.dot_general(
                jnp.concatenate(left), right, (((1,), (1,)), ((), ())),
                preferred_element_type=jnp.float32,
            )
            total = got if total is None else total + got
        for c in range(len(part)):
            rows = total[lines * c : lines * c + lines]
            lower, upper = rows[:, 0:128], rows[:, 128:256]
            if right_planes == 1:
                write(which, 0, c, jnp.concatenate([lower, upper]))
            else:
                write(which, 0, c, lower)
                write(which, 1, c, upper)


def pieces_of(value, count):
    high = value.astype(jnp.bfloat16).astype(jnp.float32)
    return [high, value - high][:count]


def list_row(ref, base, i):
    block = ref[base + 8 * i : base + 8 * i + 8, :]
    return jnp.concatenate([block[j : j + 1] for j in range(8)], 1)


def either(core, zero, one):
    return lambda i: jnp.where(core == 0, list_row(*zero, i), list_row(*one, i))


def points_of(core, row, first):
    return [jnp.where(core == 0, row(first + c), row(first + HALF + c)) for c in range(HALF)]


def writer(stores):
    def write(which, p, c, value):
        ref, first = stores[which]
        ref[first + p, LINES * c : LINES * c + LINES, :] = value

    return write


def scatter_src(core, row, count, store, first, divisor=None, planes=2):
    amp = points_of(core, row, 2)
    if divisor is not None:
        amp = [a / d for a, d in zip(amp, divisor)]
    index = row(0).astype(jnp.int32)
    spread_points(index, [[pieces_of(a, count) for a in amp]], planes, writer([(store, first)]))


def scatter_rec(core, row, count, planes, ob, cn, first):
    obs = points_of(core, row, 6)
    parts = [[pieces_of(o, count) for o in obs], [[jnp.ones_like(obs[0])]]]
    index = row(1).astype(jnp.int32)
    spread_points(index, parts, planes, writer([(ob, first), (cn, first)]))


def squares(damp):
    core = lax.axis_index("core")
    first, second = damp[HALF * core], damp[HALF * core + 1]
    return first * first, second * second


def diagonal_at(damp, row):
    sigma = row(10)
    return [6.0 + square * sigma for square in squares(damp)]


def pack_kernel(slow_in, src_in, rec_in, amp_in, obs_in, out, far, slow, src, rec, amp, obs, sem):
    slab = lax.axis_index("pair") * 2 + lax.axis_index("core")
    offset = slab * (2 * 512 * 128)
    pairs = ((src_in, src), (rec_in, rec), (amp_in, amp), (obs_in, obs), (slow_in, slow))
    copies = [pltpu.make_async_copy(x, y, sem.at[k]) for k, (x, y) in enumerate(pairs)]
    for copy in copies[::-1]:
        copy.start()
    for copy in copies[:4]:
        copy.wait()
    far[80:88, :] = jnp.zeros((8, 128), jnp.float32)
    points = amp.shape[1]
    far[0:8, :] = (src[...] - offset).astype(jnp.float32)
    far[8:16, :] = (rec[...] - offset).astype(jnp.float32)
    for k, values in ((2, amp), (6, obs)):
        for i in range(4):
            for j in range(8):
                at = 8 * (k + i) + j
                far[at : at + 1, :] = values[i : i + 1, 128 * j : 128 * j + 128]
    out[ROWS : ROWS + LIST, :] = far[...]
    for copy in copies[4:]:
        copy.wait()
    for p in range(2):
        for j in range(64):
            at = LINES * p + 8 * j
            out[at : at + 8, :] = slow[pl.ds(LINES * p + j, 8, stride=64), :]


def gather_sigma(sigma, row, store):
    index = row(0).astype(jnp.int32)
    points = index.shape[1]
    rows = lax.broadcasted_iota(jnp.int32, (ROWS, points), 0)
    line = (index >> 16) * LINES + line_of((index >> 7) & 511)
    pick = jnp.where(rows == line, 1.0, 0.0).astype(jnp.bfloat16)
    high = sigma.astype(jnp.bfloat16)
    low = (sigma - high.astype(jnp.float32)).astype(jnp.bfloat16)
    dims = (((0,), (0,)), ((), ()))
    got = lax.dot_general(high, pick, dims, preferred_element_type=jnp.float32)
    got = got + lax.dot_general(low, pick, dims, preferred_element_type=jnp.float32)
    lane = lax.broadcasted_iota(jnp.int32, (128, points), 0)
    found = jnp.sum(jnp.where(lane == index & 127, got, 0.0), axis=0, keepdims=True)
    for j in range(8):
        store[80 + j : 81 + j, :] = found[:, 128 * j : 128 * j + 128]


def scatter_slab(h, row, b, ob, cn):
    core = lax.axis_index("core")
    scatter_src(core, row, 2, b, 2 * h)
    scatter_rec(core, row, 2, 2, ob, cn, 2 * h)


def scatter_other_kernel(mine, other, b, ob, cn, first):
    core = lax.axis_index("core")
    whole = jnp.where(core == 0, mine[...], other[...])
    first[...] = whole[ROWS:SLAB]
    gather_sigma(whole[0:ROWS], functools.partial(list_row, first, 0), first)
    row = functools.partial(list_row, other, ROWS)
    scatter_slab(1 - lax.axis_index("core"), row, b, ob, cn)


def scatter_own_kernel(lists, first_in, b_in, ob_in, cn_in, b, ob, cn):
    scatter_slab(lax.axis_index("core"), functools.partial(list_row, lists, 0), b, ob, cn)


def lists_of(ref):
    return functools.partial(list_row, ref, ROWS)


def scatter_mine_kernel(damp, touch, beyond, far, b):
    core = lax.axis_index("core")
    scatter_src(core, lists_of(touch), 2, b, jnp.where(core == 0, 4, 2))
    scatter_src(core, lists_of(beyond), 1, b, jnp.where(core == 0, 0, 6))
    last = functools.partial(list_row, far, 0)
    scatter_src(core, last, 1, b, 8, diagonal_at(damp, last), 1)


def scatter_theirs_kernel(touch, beyond, b_in, b):
    core = lax.axis_index("core")
    scatter_src(core, lists_of(touch), 2, b, jnp.where(core == 0, 2, 4))
    scatter_src(core, lists_of(beyond), 1, b, jnp.where(core == 0, 6, 0))


def scatter_later_kernel(mine, ob, cn):
    core = lax.axis_index("core")
    scatter_rec(core, lists_of(mine), 2, 2, ob, cn, jnp.where(core == 0, 2, 0))


def scatter_late_kernel(theirs, beyond_m, beyond_t, ob_in, cn_in, ob, cn):
    core = lax.axis_index("core")
    scatter_rec(core, lists_of(theirs), 2, 2, ob, cn, jnp.where(core == 0, 0, 2))
    upper = either(core, (beyond_t, ROWS), (beyond_m, ROWS))
    scatter_rec(core, upper, 1, 1, ob, cn, 4)


def shift_matrix():
    i = lax.broadcasted_iota(jnp.int32, (128, 128), 0)
    j = lax.broadcasted_iota(jnp.int32, (128, 128), 1)
    return jnp.where(jnp.abs(i - j) == 1, 1.0, 0.0).astype(jnp.bfloat16)


def half(ref, t, c):
    return ref[t, LINES * c : LINES * c + LINES, :]


def next_line(x):
    sub = lax.broadcasted_iota(jnp.int32, (8, 128), 0)
    after = jnp.where(sub == 7, 0.0, pltpu.roll(x[:8], 7, 0))
    return jnp.concatenate([x[8:], after])


def beside(x):
    sub = lax.broadcasted_iota(jnp.int32, (8, 128), 0)
    before = jnp.where(sub == 0, 0.0, pltpu.roll(x[LINES - 8 :], 1, 0))
    across = jnp.concatenate([before, x[: LINES - 8]]) + next_line(x)
    turned, rest = x[:TURNED], x[TURNED:]
    lane = lax.broadcasted_iota(jnp.int32, turned.shape, 1)
    low = jnp.where(lane == 0, 0.0, pltpu.roll(turned, 1, 1))
    high = jnp.where(lane == 127, 0.0, pltpu.roll(turned, 127, 1))
    matrix = shift_matrix()
    coarse = rest.astype(jnp.bfloat16)
    fine = (rest - coarse.astype(jnp.float32)).astype(jnp.bfloat16)
    along = jnp.dot(coarse, matrix, preferred_element_type=jnp.float32)
    along = along + jnp.dot(fine, matrix, preferred_element_type=jnp.float32)
    return across + jnp.concatenate([low + high, along])


def fold(x):
    return jnp.sum(x.reshape(LINES // 8, 8, 128), 0)


def walk(first, last, body, carry, unroll=False):
    return lax.fori_loop(first, last, body, carry, unroll=unroll)


def nothing():
    return [jnp.zeros((8, 128), jnp.float32) for _ in range(HALF)]


def advance(src, s_off, inv, dst, d_off, first, last, dots, unroll=False):
    def body(t, carry):
        one, two = [], []
        for c in range(HALF):
            x = half(src, t - s_off, c)
            q = beside(x) + (half(src, t - s_off - 1, c) + half(src, t - s_off + 1, c))
            new = half(inv, t, c) * q
            dst[t - d_off, LINES * c : LINES * c + LINES, :] = new
            if dots:
                one.append(carry[0][c] + fold(x * q))
                two.append(carry[1][c] + fold(new * q))
        return (one, two) if dots else carry

    return walk(first, last, body, (nothing(), nothing()) if dots else 0, unroll)


def last_moment(src, off):
    def body(t, carry):
        out = []
        for c in range(HALF):
            x = half(src, t - off, c)
            lane = lax.broadcasted_iota(jnp.int32, x.shape, 1)
            along = jnp.where(lane == 127, 0.0, pltpu.roll(x, 127, 1))
            q = (next_line(x) + along) + half(src, t - off + 1, c)
            out.append(carry[c] + fold(x * q))
        return out

    return [2.0 * m for m in walk(4, 8, body, nothing(), True)]


def message(moments):
    sub = lax.broadcasted_iota(jnp.int32, (8, 128), 0)
    lane = lax.broadcasted_iota(jnp.int32, (8, 128), 1)
    out = jnp.zeros((8, 128), jnp.float32)
    for k, moment in enumerate(moments):
        for c in range(HALF):
            total = jnp.sum(moment[c])
            out = out + jnp.where((sub == k) & (lane == c), total, 0.0)
    return out


def coefficients(terms):
    moments = (terms[0][...] + terms[1][...]) + (terms[2][...] + terms[3][...])
    m = [moments[k : k + 1, :] for k in range(6)]

    def product(p, shift):
        total = 0.0
        for i, a in enumerate(p):
            for j, b in enumerate(p):
                total = total + a * b * (m[i + j] - m[i + j + 1] if shift else m[i + j])
        return total

    one = jnp.ones_like(m[0])
    z, p, energy = [one], [one], m[0]
    x = [0.0 * one] * 3
    for it in range(3):
        stride = energy / product(p, True)
        x = [x[i] + (stride * p[i] if i < len(p) else 0.0) for i in range(3)]
        if it < 2:
            applied = [a - b for a, b in zip(p + [0.0 * one], [0.0 * one] + p)]
            z = [a - stride * b for a, b in zip(z + [0.0 * one], applied)]
            new = product(z, False)
            p = [a + new / energy * b for a, b in zip(z, p + [0.0 * one])]
            energy = new
    lane = lax.broadcasted_iota(jnp.int32, (1, 128), 1)
    return [[jnp.sum(jnp.where(lane == c, v, 0.0)) for c in range(HALF)] for v in x]


def fill_inverse(core, square, inv, slab, mine, theirs, valid):
    def fill(p, _):
        at = pl.multiple_of(p * 512, 512)
        here = mine[pl.ds(at, 512), :]
        there = theirs[pl.ds(at, 512), :]
        sigma = jnp.where(core == slab % 2, here, there)
        for c in range(HALF):
            inv[2 * slab + p, LINES * c : LINES * c + LINES, :] = valid / (6.0 + square[c] * sigma)
        return 0

    lax.fori_loop(0, 2, fill, 0)


def forward_own_kernel(damp, own_m, own_t, b_own, inv, v0, v1, held):
    core = lax.axis_index("core")
    square = squares(damp)
    for slab in (2, 3):
        fill_inverse(core, square, inv, slab, own_m, own_t, 1.0)

    def start(t, carry):
        out = []
        for c in range(HALF):
            right = half(b_own, t - 4, c)
            new = half(inv, t, c) * right
            v0[t, LINES * c : LINES * c + LINES, :] = new
            out.append(carry[c] + fold(new * right))
        return out

    m0 = walk(4, 8, start, nothing())
    m1, m2 = advance(v0, 0, inv, v1, 1, 5, 7, True)
    for k, part in enumerate(m0 + m1 + m2):
        held[8 * k : 8 * k + 8, :] = part


def forward_kernel(
    damp, touch_m, touch_t, beyond_m, beyond_t, b_near, held, inv_in, v0_in, v1_in,
    inv, v0, v1, v2, msg,
):
    pair, core = lax.axis_index("pair"), lax.axis_index("core")
    low = jnp.where(pair >= 1, 1.0, 0.0)
    high = jnp.where(pair + 1 < lax.axis_size("pair"), 1.0, 0.0)
    square = squares(damp)
    fill_inverse(core, square, inv, 0, beyond_m, beyond_t, low)
    fill_inverse(core, square, inv, 1, touch_m, touch_t, low)
    fill_inverse(core, square, inv, 4, touch_m, touch_t, high)
    fill_inverse(core, square, inv, 5, beyond_m, beyond_t, high)

    def start(off):
        def body(t, carry):
            v0[t] = inv[t] * b_near[t - off]
            return carry

        return body

    v0[12] = b_near[8] * jnp.where(pair + 2 < lax.axis_size("pair"), 1.0, 0.0)
    walk(0, 4, start(0), 0)
    walk(8, 12, start(4), 0)
    kept = [held[8 * k : 8 * k + 8, :] for k in range(3 * HALF)]
    advance(v0, 0, inv, v1, 1, 1, 4, False, True)
    lower = advance(v0, 0, inv, v1, 1, 4, 5, True, True)
    upper = advance(v0, 0, inv, v1, 1, 7, 8, True, True)
    advance(v0, 0, inv, v1, 1, 8, 12, False, True)
    m1 = [a + b + c for a, b, c in zip(lower[0], upper[0], kept[HALF : 2 * HALF])]
    m2 = [a + b + c for a, b, c in zip(lower[1], upper[1], kept[2 * HALF :])]
    advance(v1, 1, inv, v2, 2, 2, 4, False, True)
    m3, m4 = advance(v1, 1, inv, v2, 2, 4, 8, True, True)
    advance(v1, 1, inv, v2, 2, 8, 11, False, True)
    m5 = last_moment(v2, 2)
    msg[...] = message([kept[:HALF], m1, m2, m3, m4, m5])


def adjoint_kernel(
    t0, t1, t2, t3, inv, v0, v1, v2, ob_own, cn_own, ob_near, cn_near, wave, u0, u1, u2, msg
):
    a = coefficients((t0, t1, t2, t3))

    def start(ob, cn, off, own):
        def body(t, carry):
            out = []
            count = cn[t - off]
            for c in range(HALF):
                lines = slice(LINES * c, LINES * c + LINES)
                w = a[0][c] * half(v0, t, c) + a[1][c] * half(v1, t - 1, c)
                w = w + a[2][c] * half(v2, t - 2, c)
                right = count * w - half(ob, t - off, c)
                new = half(inv, t, c) * right
                u0[t, lines, :] = new
                if own:
                    wave[t - 4, lines, :] = w
                    out.append(carry[c] + fold(new * right))
            return out if own else carry

        return body

    walk(2, 4, start(ob_near, cn_near, 2, False), 0)
    m0 = walk(4, 8, start(ob_own, cn_own, 4, True), nothing())
    walk(8, 11, start(ob_near, cn_near, 6, False), 0)
    advance(u0, 0, inv, u1, 1, 3, 4, False, True)
    m1, m2 = advance(u0, 0, inv, u1, 1, 4, 8, True, True)
    advance(u0, 0, inv, u1, 1, 8, 10, False, True)
    m3, m4 = advance(u1, 1, inv, u2, 2, 4, 8, True, True)
    advance(u1, 1, inv, u2, 2, 8, 9, False, True)
    m5 = last_moment(u2, 2)
    msg[...] = message([m0, m1, m2, m3, m4, m5])


def gradient_kernel(other, damp, t0, t1, t2, t3, wave, u0, u1, u2, *rest):
    held = rest[-1]
    a = coefficients((t0, t1, t2, t3))
    a = [[-square * v for square, v in zip(squares(damp), one)] for one in a]
    core = lax.axis_index("core")
    core = 1 - core if other else core
    bands = rest[0] if other else rest[-2]
    for p in range(2):
        t = 4 + 2 * core + p
        total = 0.0
        for c in range(HALF):
            x = a[0][c] * half(u0, t, c) + a[1][c] * half(u1, t - 1, c) + a[2][c] * half(u2, t - 2, c)
            total = total + x * half(wave, t - 4, c)
        held[...] = total
        for s in range(8):
            band, rows = s // 2, slice(64 * (s % 2), 64 * (s % 2) + 64)
            part = held[pl.ds(s, 64, stride=8), :]
            bands[band, p, rows, :] = part if other else part + rest[0][band, p, rows, :]
    if not other:
        lap = lax.axis_index("lap")
        for d in range(4):
            rest[2 + d][:, 0:128, :] = bands[lap ^ d]
            rest[2 + d][:, 128:136, :] = rest[1][...]


def power_kernel(g0, g1, g2, g3, own, msg, prior_y):
    lap = lax.axis_index("lap")
    g = (g0[:, 0:128] + g1[:, 0:128]) + (g2[:, 0:128] + g3[:, 0:128])
    own[...] = g
    msg[...] = jnp.full((128, 128), jnp.sum(g * g), jnp.float32)
    before = jnp.where(lap == 2, g3[:, 128:136], g1[:, 128:136])
    prior_y[...] = jnp.where(lap == 0, 0.0, before)


def band_of(ref, lap):
    out = None
    for k in range(4):
        parts = [ref[pl.ds(2 * k + i, 64, stride=8), :] for i in range(2)]
        band = jnp.concatenate(parts)
        out = band if out is None else jnp.where(lap == k, band, out)
    return out


def variation_kernel(slow, own_t, touch_t, dual, dual_next, base, send_x, send_y):
    lap, pair, core = (lax.axis_index(name) for name in ("lap", "pair", "core"))
    start = pl.multiple_of(lap * 128, 128)
    band = pl.ds(start, 128)
    after = pl.ds(pl.multiple_of(jnp.minimum(start + 128, 504), 8), 8)
    row = lax.broadcasted_iota(jnp.int32, (128, 128), 0)
    lane = lax.broadcasted_iota(jnp.int32, (128, 128), 1)
    last_y = (row == 127) & (lap == 3)
    last_z = lane == 127
    comps = []
    for p in range(2):
        here = slow[p, band, :]
        if p == 0:
            step_x = slow[1, band, :] - here
        else:
            beyond = jnp.where(core == 0, band_of(own_t, lap), band_of(touch_t, lap))
            step_x = beyond - here
            step_x = jnp.where((core == 1) & (pair == 15), 0.0, step_x)
        rolled = pltpu.roll(here, 127, 0)
        step_y = jnp.where(row == 127, slow[p, after, :][0:1], rolled) - here
        step_y = jnp.where(last_y, 0.0, step_y)
        step_z = jnp.where(last_z, 0.0, pltpu.roll(here, 127, 1) - here)
        trial = [dual[k, p] + dual_step * step for k, step in enumerate((step_x, step_y, step_z))]
        magnitude = jnp.sqrt(trial[0] * trial[0] + trial[1] * trial[1] + trial[2] * trial[2])
        scale = jnp.maximum(1.0, magnitude / tv_weight)
        new = [x / scale for x in trial]
        for k in range(3):
            dual_next[k, p] = new[k]
        if p == 1:
            new[0] = jnp.where((core == 1) & (pair == 15), 0.0, new[0])
        new[1] = jnp.where(last_y, 0.0, new[1])
        new[2] = jnp.where(last_z, 0.0, new[2])
        comps.append(new)
    for p in range(2):
        x, y, z = comps[p]
        back = jnp.where(row == 0, 0.0, pltpu.roll(y, 1, 0)) - y
        back = back + (jnp.where(lane == 0, 0.0, pltpu.roll(z, 1, 1)) - z)
        back = back + (comps[0][0] - x if p == 1 else -x)
        base[p] = slow[p, band, :] - primal_step * back
        send_y[p] = y[120:128]
    send_x[0] = comps[1][0]


def model_kernel(cells, base, grad, power, prior_x, prior_y, model):
    total = power[0]
    for k in range(1, 16):
        total = total + power[k]
    total = jnp.sum(total, axis=0, keepdims=True)
    scale = 1.0 / jnp.sqrt(total / cells + 1e-06)
    row = lax.broadcasted_iota(jnp.int32, (128, 128), 0)
    for p in range(2):
        back = jnp.where(row == 0, prior_y[p][7:8], 0.0)
        if p == 0:
            first = (lax.axis_index("pair") == 0) & (lax.axis_index("core") == 0)
            back = back + jnp.where(first, 0.0, prior_x[0])
        model[p] = base[p] - primal_step * (grad[p] * scale + back)


def cost(work):
    return pl.CostEstimate(flops=work * 10**7, bytes_accessed=10**4, transcendentals=0)


def struct(*shape):
    return jax.ShapeDtypeStruct(shape, jnp.float32)


def moved(x, axis, by):
    peers = lax.axis_size(axis)
    return lax.ppermute(x, axis, [(i, (i + by) % peers) for i in range(peers)])


def swapped(x):
    return lax.ppermute(x, "core", [(0, 1), (1, 0)])


def others(x, masks):
    return [lax.ppermute(x, "pair", [(i, i ^ d) for i in range(16)]) for d in masks]


def stage_sum(x):
    return x + sum(others(x, (1, 2, 3)))


def stage_terms(x):
    return [x] + others(x, (4, 8, 12))


def scatter(kernel, name, work, inputs, shapes, into=()):
    scalars = 1 if inputs[0].ndim == 1 else 0
    first = len(inputs)
    return pl.pallas_call(
        kernel,
        out_shape=tuple(struct(*shape) for shape in shapes),
        in_specs=[SMEM] * scalars + [VMEM] * (len(inputs) - scalars + len(into)),
        out_specs=(VMEM,) * len(shapes),
        input_output_aliases={first + k: k for k in range(len(into))},
        compiler_params=params(8),
        cost_estimate=cost(work),
        name=name,
    )(*inputs, *into)


def on_device(slowness, damping, src_index, src_amp, rec_index, observed, dual):
    width_x, rows_y, depth_z = slowness.shape
    slab_cells = width_x * rows_y * depth_z
    pairs = lax.axis_size("pair")

    packed, lists = pl.pallas_call(
        pack_kernel,
        out_shape=(struct(SLAB, 128), struct(LIST, 128)),
        in_specs=[pl.BlockSpec(memory_space=pltpu.HBM)] * 5,
        out_specs=(VMEM,) * 2,
        scratch_shapes=[
            pltpu.VMEM((ROWS, 128), jnp.float32), pltpu.VMEM((8, 128), jnp.int32), pltpu.VMEM((8, 128), jnp.int32),
            pltpu.VMEM(src_amp.shape, jnp.float32), pltpu.VMEM(observed.shape, jnp.float32),
            pltpu.SemaphoreType.DMA((5,)),
        ],
        compiler_params=params(8),
        name="pack",
    )(
        *(
            pltpu.with_memory_space_constraint(x, pltpu.HBM)
            for x in (
                slowness.reshape(ROWS, 128), src_index.reshape(8, 128), rec_index.reshape(8, 128),
                src_amp, observed,
            )
        )
    )
    space, last = ("pair", "core"), 2 * pairs
    inward = [(i, (i + 2 * (-1, 1)[i % 2]) % last) for i in range(last)]
    outward = [(i, (i + 2 * (1, -1)[i % 2]) % last) for i in range(last)]
    touch_m = lax.ppermute(packed, space, inward)
    beyond_m = lax.ppermute(packed, space, outward)
    own_t = swapped(packed)

    block, near_block = (4, ROWS, 128), (5, ROWS, 128)
    count, near_count = (4, LINES, 128), (5, LINES, 128)
    *own, first = scatter(
        scatter_other_kernel, "scatter_other", 5, (packed, own_t), [block, block, count, (LIST, 128)]
    )
    far_m = moved(first, "pair", -2)
    b_own, ob_own, cn_own = scatter(
        scatter_own_kernel, "scatter_own", 5, (lists, first), [block, block, count], own
    )
    inv, v0, v1, held = pl.pallas_call(
        forward_own_kernel,
        out_shape=(
            struct(PLANES, ROWS, 128), struct(13, ROWS, 128), struct(11, ROWS, 128),
            struct(48, 128),
        ),
        in_specs=[SMEM] + [VMEM] * 3,
        out_specs=(VMEM,) * 4,
        compiler_params=params(2),
        cost_estimate=cost(4),
        name="forward_own",
    )(damping, packed, own_t, b_own)
    touch_m, beyond_m, far_m, held = lax.optimization_barrier((touch_m, beyond_m, far_m, held))
    touch_t, beyond_t = swapped(touch_m), swapped(beyond_m)
    near_shape = [(9, ROWS, 128)]
    b_near, = scatter(
        scatter_mine_kernel, "scatter_mine", 4, (damping, touch_m, beyond_m, far_m), near_shape
    )
    touch_t, beyond_t, b_near = lax.optimization_barrier((touch_t, beyond_t, b_near))
    b_near, = scatter(
        scatter_theirs_kernel, "scatter_theirs", 3, (touch_t, beyond_t), near_shape, (b_near,)
    )

    inv, v0, v1, v2, msg = pl.pallas_call(
        forward_kernel,
        out_shape=(
            struct(PLANES, ROWS, 128), struct(13, ROWS, 128), struct(11, ROWS, 128),
            struct(9, ROWS, 128), struct(8, 128),
        ),
        in_specs=[SMEM] + [VMEM] * 9,
        out_specs=(VMEM,) * 5,
        input_output_aliases={7: 0, 8: 1, 9: 2},
        compiler_params=params(4),
        cost_estimate=cost(20),
        name="forward",
    )(damping, touch_m, touch_t, beyond_m, beyond_t, b_near, held, inv, v0, v1)

    touch_m, msg = lax.optimization_barrier((touch_m, msg))
    near = scatter(scatter_later_kernel, "scatter_later", 3, (touch_m,), [near_block, near_count])
    half_sum = stage_sum(msg)
    half_sum, near, touch_t = lax.optimization_barrier((half_sum, near, touch_t))
    ob_near, cn_near = scatter(
        scatter_late_kernel, "scatter_late", 4, (touch_t, beyond_m, beyond_t),
        [near_block, near_count], near,
    )
    wave, u0, u1, u2, msg = pl.pallas_call(
        adjoint_kernel,
        out_shape=(
            struct(4, ROWS, 128), struct(13, ROWS, 128), struct(11, ROWS, 128),
            struct(9, ROWS, 128), struct(8, 128),
        ),
        in_specs=[VMEM] * 12,
        out_specs=(VMEM,) * 5,
        input_output_aliases={5: 1, 6: 2, 7: 3},
        compiler_params=params(4),
        cost_estimate=cost(14),
        name="adjoint",
    )(*stage_terms(half_sum), inv, v0, v1, v2, ob_own, cn_own, ob_near, cn_near)

    terms = stage_terms(stage_sum(msg))

    def gradient(other, *more):
        scratch = [] if other else [pltpu.VMEM((4, 2, 128, 128), jnp.float32)]
        return pl.pallas_call(
            functools.partial(gradient_kernel, other),
            out_shape=struct(4, 2, 128, 128) if other else (struct(2, 136, 128),) * 4,
            in_specs=[SMEM] + [VMEM] * (8 + len(more)),
            out_specs=VMEM if other else (VMEM,) * 4,
            scratch_shapes=scratch + [pltpu.VMEM((LINES, 128), jnp.float32)],
            compiler_params=params(8),
            name="gradient",
        )(damping, *terms, wave, u0, u1, u2, *more)

    given = gradient(True)
    slowness, dual, own_t, touch_t, given = lax.optimization_barrier(
        (slowness, dual, own_t, touch_t, given)
    )
    dual_next, base, send_x, send_y = pl.pallas_call(
        variation_kernel,
        out_shape=(
            struct(3, 2, 128, 128), struct(2, 128, 128), struct(1, 128, 128), struct(2, 8, 128),
        ),
        in_specs=[VMEM] * 4,
        out_specs=(VMEM,) * 4,
        compiler_params=params(8),
        cost_estimate=cost(1),
        name="variation",
    )(slowness, own_t, touch_t, dual)
    bands = gradient(False, swapped(given), send_y)
    send_x, bands = lax.optimization_barrier((send_x, bands))
    arrived = [bands[0]] + [
        lax.ppermute(bands[d], "lap", [(i, i ^ d) for i in range(4)]) for d in (1, 2, 3)
    ]
    prior_x = moved(send_x, ("pair", "core"), 1)
    arrived, prior_x = lax.optimization_barrier((arrived, prior_x))
    own_grad, power, prior_y = pl.pallas_call(
        power_kernel,
        out_shape=(struct(2, 128, 128), struct(128, 128), struct(2, 8, 128)),
        in_specs=[VMEM] * 4,
        out_specs=(VMEM,) * 3,
        compiler_params=params(8),
        name="power",
    )(*arrived)
    power = lax.all_to_all(power, ("lap", "pair", "core"), 0, 0, tiled=True)
    model = pl.pallas_call(
        functools.partial(model_kernel, float(slab_cells * 2 * pairs)),
        out_shape=struct(2, 128, 128),
        in_specs=[VMEM] * 5,
        out_specs=VMEM,
        compiler_params=params(8),
        name="model",
    )(base, own_grad, power.reshape(16, 8, 128), prior_x, prior_y)
    return (model, dual_next)


def solution(mesh):
    space = mesh.devices.shape[1]
    mesh = Mesh(mesh.devices.reshape(-1, space // 2, 2), ("lap", "pair", "core"))
    both = ("pair", "core")
    in_specs = (
        P(both, None, None),
        P("lap"),
        P(both),
        P("lap", both),
        P(both),
        P("lap", both),
        P(None, both, "lap", None),
    )
    out_specs = (P(both, "lap", None), P(None, both, "lap", None))
    return jax.shard_map(
        on_device, mesh=mesh, in_specs=in_specs, out_specs=out_specs, check_vma=False
    )
```
